32 devices in a mesh: groups: 2 (over x), leaf: 16 (over z, y, core).
Axes of the slice: x: 2, y: 2, z: 4, core: 2. Of those that a mesh axis runs over, the one named last changes fastest.
Arguments:
- coords: bfloat16 [64, 32768], P(None, ('groups', 'leaf')), parts along dimension 1, may hold values from -1.1953125 to 1.1953125
- charges: bfloat16 [64, 32768], P(None, ('groups', 'leaf')), parts along dimension 1, may hold values from -6 to 6
- near_lists: int32 [64, 16], P(('groups', 'leaf')), parts along dimension 0, may hold values from -1 to 31, as said below
- far_lists: int32 [64, 32], P(('groups', 'leaf')), parts along dimension 0, may hold values from -1 to 16, as said below
- leaf_interp: bfloat16 [32768, 128], P(('groups', 'leaf')), parts along dimension 0, may hold values from -0.25 to 0.25
- node_interp: bfloat16 [8192, 128], P(('groups', 'leaf')), parts along dimension 0, may hold values from -0.375 to 0.375
- upper_interp: bfloat16 [4096, 128], P(('groups', 'leaf')), parts along dimension 0, may hold values from -0.125 to 0.125
- node_points: bfloat16 [64, 4096], P(None, ('groups', 'leaf')), parts along dimension 1, may hold values from -1.1953125 to 1.1953125
- upper_points: bfloat16 [64, 256], P(None, 'groups'), parts along dimension 1, may hold values from -1.1953125 to 1.1953125
Outputs:
- first: bfloat16 [64, 32768], P(None, ('groups', 'leaf')), parts along dimension 1
- second: bfloat16 [64, 32768], P(None, ('groups', 'leaf')), parts along dimension 1
The draws below stay inside these ranges and needn't reach their ends.
There are 2 independent parts, one for each index of `groups`. The reference program is written for one: setup_inputs(seed, part) draws one part's arguments, and reference() takes and returns one part's arrays. A program takes and returns all parts, laid end to end along the dimension named above; each array names one. Nothing has to cross between parts.
Inputs may be any that keep to these rules, and one draw needn't show every extreme that they name: `near_lists`: used slots come first, then -1 for each unused slot. Slot 0 of leaf b names b itself and slot 1 names another leaf of b's device. Over the near lists of the leaves of one device, at most one distinct leaf of any other device is named, though it may be named several times. `far_lists`: used slots come first, then -1 for each unused slot. An entry under 16 names a device node, the others name upper nodes. No entry names the device node that holds the leaf itself.
All inputs are finite; a program needn't handle non-finite values.
Results may differ from the reference program's by a relative error of at most 0.008.
Values may be sent and summed in bfloat16 or wider, within the bound.
No kernel may reach another device: no remote copies, remote signals or barrier semaphores. Data moves between devices by JAX's collectives and lax.ppermute only.
A program may use at most 64 MiB of HBM per device.

```python
import jax
import jax.numpy as jnp
from jax import lax

DIM = 64
RHS = 64
LEAF = 512
SKEL = 128
BRANCH = 16
NEAR = 16
FAR = 32
LEAVES_DEV = 2
LEAVES = 32
POINTS = 16384
N_SUB = 1
N_LEAF = 16


def draw_near_lists(key, part):
    key = jax.random.fold_in(key, 17)
    key_leaf, key_order, key_count = jax.random.split(key, 3)
    chosen = jax.random.randint(key_leaf, (N_LEAF, N_LEAF), 0, LEAVES_DEV)
    orders = jax.vmap(lambda single: jax.random.permutation(single, N_LEAF - 1))(jax.random.split(key_order, N_LEAF)) + 1
    leaf_ids = jnp.arange(LEAVES)
    device = leaf_ids // LEAVES_DEV
    within = leaf_ids % LEAVES_DEV
    slots = jnp.arange(NEAR)
    entry = within[:, None] * (NEAR - 2) + slots[None, :] - 2
    offset = jnp.take_along_axis(orders[device], jnp.maximum(entry, 0) % (N_LEAF - 1), axis=1)
    partner = (device[:, None] + offset) % N_LEAF
    remote = partner * LEAVES_DEV + chosen[device[:, None], partner]
    sibling = device * LEAVES_DEV + (within + 1) % LEAVES_DEV
    listed = jnp.where(slots[None, :] == 0, leaf_ids[:, None], jnp.where(slots[None, :] == 1, sibling[:, None], remote))
    counts = jax.random.randint(key_count, (LEAVES, 1), NEAR - NEAR // 4, NEAR + 1)
    return jnp.where(slots[None, :] < counts, listed, -1).astype(jnp.int32)


def draw_far_lists(key, part):
    key = jax.random.fold_in(key, 29)
    key_node, key_count = jax.random.split(key)
    raw_ids = jax.random.randint(key_node, (LEAVES, FAR), 0, N_LEAF + N_SUB - 1)
    own_node = (jnp.arange(LEAVES) // LEAVES_DEV)[:, None]
    node_ids = jnp.where(raw_ids >= own_node, raw_ids + 1, raw_ids)
    counts = jax.random.randint(key_count, (LEAVES, 1), FAR // 2, FAR + 1)
    return jnp.where(jnp.arange(FAR)[None, :] < counts, node_ids, -1).astype(jnp.int32)


def shard_levels(key, shape, cuts, smallest, top_value):
    def one(position, blocks):
        steps = jax.random.uniform(jax.random.fold_in(jax.random.fold_in(key, 6), position), (blocks,), jnp.float32, smallest / len(cuts), top_value / len(cuts))
        return jnp.repeat(jnp.exp(steps), shape[position] // blocks).reshape((-1,) + (1,) * (len(shape) - position - 1))

    factor_of = one(*cuts[0])
    for cut in cuts[1:]:
        factor_of = factor_of * one(*cut)
    return factor_of


def gaussian(key, extent, spread, most, shards=(), held_as=jnp.bfloat16):
    level = shard_levels(key, extent, shards, -0.22, 0.18) if shards else 1.0
    drawn = jax.random.normal(key, extent, jnp.float32) * spread * level
    return jnp.minimum(jnp.maximum(drawn, -most), most).astype(held_as)


def setup_inputs(seed: int = 0, part: int = 0) -> dict:
    key_of = jax.random.split(jax.random.key(seed), 10)
    own_keys = jax.random.split(jax.random.fold_in(key_of[9], part), 10)
    return {
        "coords": gaussian(own_keys[0], (DIM, POINTS), 0.2, 1.1953125, ((1, 16),)),
        "charges": gaussian(own_keys[1], (RHS, POINTS), 1.0, 6.0, ((1, 16),)),
        "near_lists": draw_near_lists(jax.random.fold_in(jax.random.fold_in(key_of[9], part), 71), part),
        "far_lists": draw_far_lists(jax.random.fold_in(jax.random.fold_in(key_of[9], part), 71), part),
        "leaf_interp": gaussian(own_keys[4], (LEAVES * LEAF, SKEL), LEAF ** -0.5, 0.25, ((0, 16),)),
        "node_interp": gaussian(own_keys[5], (LEAVES * SKEL, SKEL), (LEAVES_DEV * SKEL) ** -0.5, 0.375, ((0, 16),)),
        "upper_interp": gaussian(own_keys[6], (N_LEAF * SKEL, SKEL), (BRANCH * SKEL) ** -0.5, 0.125, ((0, 16),)),
        "node_points": gaussian(own_keys[7], (DIM, N_LEAF * SKEL), 0.2, 1.1953125, ((1, 16),)),
        "upper_points": gaussian(own_keys[8], (DIM, N_SUB * SKEL), 0.2, 1.1953125),
    }


def kernel_block(source_coords, target_coords, target_sq):
    source_sq = jnp.sum(source_coords * source_coords, axis=0)
    products = jnp.einsum("dns,dt->nst", source_coords, target_coords)
    distance = source_sq[:, :, None] + target_sq[None, None, :] - 2.0 * products
    return jnp.exp(-distance).astype(jnp.bfloat16)


def kernel_product(coords, weights_in, near_lists, far_lists, leaf_interp, node_interp, upper_interp, table_points):
    leaves = near_lists.shape[0]
    points = coords.astype(jnp.float32).reshape(DIM, leaves, LEAF)
    charge_blocks = weights_in.astype(jnp.float32).reshape(RHS, leaves, LEAF)
    target_sq = jnp.sum(points * points, axis=0)
    leaf_maps = leaf_interp.astype(jnp.float32).reshape(leaves, LEAF, SKEL)
    leaf_weights = jnp.einsum("rls,lsk->rlk", charge_blocks, leaf_maps).astype(jnp.bfloat16)
    stacked_leaf = leaf_weights.astype(jnp.float32).reshape(RHS, N_LEAF, LEAVES_DEV * SKEL)
    node_maps = node_interp.astype(jnp.float32).reshape(N_LEAF, LEAVES_DEV * SKEL, SKEL)
    device_weights = jnp.einsum("rdk,dkj->rdj", stacked_leaf, node_maps).astype(jnp.bfloat16)
    upper_maps = upper_interp.astype(jnp.float32).reshape(N_LEAF, SKEL, SKEL)
    upper_terms = jnp.einsum("rdk,dkj->rdj", device_weights.astype(jnp.float32), upper_maps).astype(jnp.bfloat16)
    upper_weights = jnp.sum(upper_terms.astype(jnp.float32).reshape(RHS, N_SUB, BRANCH, SKEL), axis=2).astype(jnp.bfloat16)
    table_weights = jnp.concatenate([device_weights, upper_weights], axis=1).astype(jnp.float32)

    def one_leaf(leaf_id):
        target = points[:, leaf_id]
        own_sq = target_sq[leaf_id]
        near_ids = near_lists[leaf_id]
        near_safe = jnp.maximum(near_ids, 0)
        near_valid = (near_ids >= 0).astype(jnp.float32)
        source_coords = points[:, near_safe]
        source_charges = charge_blocks[:, near_safe] * near_valid[None, :, None]
        weights = kernel_block(source_coords, target, own_sq).astype(jnp.float32)
        near_part = jnp.einsum("rns,nst->rt", source_charges, weights)
        far_ids = far_lists[leaf_id]
        far_safe = jnp.maximum(far_ids, 0)
        far_valid = (far_ids >= 0).astype(jnp.float32)
        skeleton_coords = table_points[:, far_safe]
        skeleton_charges = table_weights[:, far_safe] * far_valid[None, :, None]
        far_weights = kernel_block(skeleton_coords, target, own_sq).astype(jnp.float32)
        far_part = jnp.einsum("rns,nst->rt", skeleton_charges, far_weights)
        return near_part + far_part

    result = lax.map(one_leaf, jnp.arange(leaves))
    return jnp.transpose(result, (1, 0, 2)).reshape(RHS, leaves * LEAF).astype(jnp.bfloat16)


def reference(coords, charges, near_lists, far_lists, leaf_interp, node_interp, upper_interp, node_points, upper_points):
    device_points = node_points.astype(jnp.float32).reshape(DIM, N_LEAF, SKEL)
    top_points = upper_points.astype(jnp.float32).reshape(DIM, N_SUB, SKEL)
    table_points = jnp.concatenate([device_points, top_points], axis=1)
    first_pass = kernel_product(coords, charges, near_lists, far_lists, leaf_interp, node_interp, upper_interp, table_points)
    second_pass = kernel_product(coords, first_pass, near_lists, far_lists, leaf_interp, node_interp, upper_interp, table_points)
    return (first_pass, second_pass)
```

```python
import functools

import jax
import jax.numpy as jnp
from jax import lax
from jax.experimental import pallas as pl
from jax.experimental.pallas import tpu as pltpu
from jax.sharding import PartitionSpec as P

BRANCH = 16
EXTRA = 16
DEPTH = 128
GROUP = 4

bf16 = jnp.bfloat16
f32 = jnp.float32

CONTRACT_LAST = (((1,), (1,)), ((), ()))


def matmul(left, right):
    return jnp.dot(left, right, preferred_element_type=f32)


def square_parts(points):
    minus = -jnp.sum(points * points, axis=0, keepdims=True)
    high = minus.astype(bf16).astype(f32)
    rest = minus - high
    middle = rest.astype(bf16).astype(f32)
    low = rest - middle
    return high, middle, low


def extra_rows(parts, first, width):
    row = lax.broadcasted_iota(jnp.int32, (EXTRA, width), 0)
    rows = jnp.where(row < 6, 1.0, 0.0).astype(f32)
    for offset, part in enumerate(parts):
        rows = jnp.where(row == first + offset, jnp.broadcast_to(part, (EXTRA, width)), rows)
    return rows


def put_sources(sources_ref, place, points):
    dim, width = points.shape
    columns = pl.ds(place, width)
    sources_ref[0:dim, columns] = points
    parts = square_parts(points.astype(f32))
    sources_ref[dim : dim + EXTRA, columns] = extra_rows(parts, 3, width).astype(bf16)


def put_targets(targets_ref, coords_ref, leaves_dev, leaf_points):
    dim = coords_ref.shape[0]
    for leaf in range(leaves_dev):
        points = coords_ref[:, leaf * leaf_points : (leaf + 1) * leaf_points].astype(f32)
        extra = extra_rows(square_parts(points), 0, leaf_points)
        blank = jnp.zeros((DEPTH - dim - EXTRA, leaf_points), f32)
        stacked = jnp.concatenate([2.0 * points, extra, blank], axis=0)
        targets_ref[leaf] = stacked.T.astype(bf16)


def skeleton_weights(charges, leaf_interp_ref, node_interp_ref, upper_interp_ref, leaves_dev):
    leaf_points = charges.shape[1] // leaves_dev
    parts = []
    for leaf in range(leaves_dev):
        span = slice(leaf * leaf_points, (leaf + 1) * leaf_points)
        parts.append(matmul(charges[:, span], leaf_interp_ref[span, :]).astype(bf16))
    device_weights = matmul(jnp.concatenate(parts, axis=1), node_interp_ref[...]).astype(bf16)
    upper_term = matmul(device_weights, upper_interp_ref[...]).astype(bf16)
    return device_weights, upper_term


def message_kernel(
    leaves_dev,
    coords_ref,
    charges_ref,
    points_ref,
    leaf_interp_ref,
    node_interp_ref,
    upper_interp_ref,
    out_ref,
):
    local = coords_ref.shape[1]
    skeleton = points_ref.shape[1]
    charges = charges_ref[...]
    weights, term = skeleton_weights(
        charges, leaf_interp_ref, node_interp_ref, upper_interp_ref, leaves_dev
    )
    out_ref[:, 0:local] = coords_ref[...]
    out_ref[:, local : 2 * local] = charges
    place = 2 * local
    out_ref[:, place : place + skeleton] = points_ref[...]
    out_ref[:, place + skeleton : place + 2 * skeleton] = weights
    out_ref[:, place + 2 * skeleton : place + 3 * skeleton] = term


def kernel_sum(targets, sources, charges):
    total = targets.shape[0]
    step = min(total, 256)
    out = []
    for begin in range(0, total, step):
        exponent = matmul(targets[begin : begin + step], sources)
        kernel = jnp.exp(exponent).astype(bf16)
        out.append(
            lax.dot_general(kernel, charges, CONTRACT_LAST, preferred_element_type=f32)
        )
    return jnp.concatenate(out, axis=0)


def product_kernel(
    dims,
    near_ref,
    far_ref,
    coords_pool_ref,
    charges_pool_ref,
    coords_ref,
    upper_points_ref,
    *rest,
):
    (leaves_dev, leaf_points, skeleton, peers, charges_at, weights_at, last) = dims
    if last:
        out_ref, targets_ref, sources_ref, far_weights_ref, upper_ref, total_ref, counts_ref = rest
    else:
        (
            leaf_interp_ref,
            node_interp_ref,
            upper_interp_ref,
            out_ref,
            message_ref,
            targets_ref,
            sources_ref,
            far_weights_ref,
            upper_ref,
            total_ref,
            counts_ref,
        ) = rest
    dim = coords_ref.shape[0]
    columns = coords_pool_ref.shape[1]
    near_slots = near_ref.shape[1]
    far_slots = far_ref.shape[1]
    n_sub = peers // BRANCH
    nodes = peers + n_sub
    points_at = 2 * leaves_dev * leaf_points
    terms_at = weights_at + skeleton

    put_targets(targets_ref, coords_ref, leaves_dev, leaf_points)
    sources_ref[...] = jnp.zeros_like(sources_ref)

    for sub in range(n_sub):
        span = slice(terms_at, terms_at + skeleton)
        terms = [
            charges_pool_ref[sub * BRANCH + child, :, span].astype(f32) for child in range(BRANCH)
        ]
        while len(terms) > 1:
            terms = [a + b for a, b in zip(terms[::2], terms[1::2])]
        upper_ref[sub] = terms[0].astype(bf16)

    for leaf in range(leaves_dev):
        for node in range(nodes):
            counts_ref[leaf, node] = 0
        for slot in range(far_slots):
            named = far_ref[leaf, slot]

            @pl.when(named >= 0)
            def _():
                counts_ref[leaf, named] = counts_ref[leaf, named] + 1

    group_width = GROUP * skeleton
    full_groups = -(-nodes // GROUP)

    def far_points(node):
        if isinstance(node, int) and node >= peers:
            begin = (node - peers) * skeleton
            return upper_points_ref[:, begin : begin + skeleton], upper_ref[node - peers]
        return (
            coords_pool_ref[node, :, points_at : points_at + skeleton],
            charges_pool_ref[node, :, weights_at : weights_at + skeleton],
        )

    def far_group(members, fresh):
        width = len(members) * skeleton
        weights_of = []
        for position, node in enumerate(members):
            points, weights = far_points(node)
            put_sources(sources_ref, position * skeleton, points)
            weights_of.append(weights.astype(f32))
        for leaf in range(leaves_dev):
            for position, node in enumerate(members):
                scaled = weights_of[position] * counts_ref[leaf, node].astype(f32)
                high = scaled.astype(bf16)
                low = (scaled - high.astype(f32)).astype(bf16)
                place = pl.ds(position * skeleton, skeleton)
                far_weights_ref[0:columns, place] = high
                far_weights_ref[columns : 2 * columns, place] = low
            both = kernel_sum(
                targets_ref[leaf], sources_ref[:, 0:width], far_weights_ref[:, 0:width]
            )
            added = both[:, 0:columns] + both[:, columns : 2 * columns]
            total_ref[leaf] = added if fresh else total_ref[leaf] + added

    upper_nodes = list(range(peers, nodes))
    for begin in range(0, len(upper_nodes), GROUP):
        far_group(upper_nodes[begin : begin + GROUP], begin == 0)

    def far_step(turn, carry):
        far_group([turn * GROUP + member for member in range(GROUP)], False)
        return carry

    lax.fori_loop(0, peers // GROUP, far_step, 0)

    def used(leaf):
        count = jnp.int32(0)
        for slot in range(near_slots):
            count = count + (near_ref[leaf, slot] >= 0).astype(jnp.int32)
        return count

    for leaf in range(leaves_dev):

        def near_step(slot, carry):
            named = near_ref[leaf, slot]
            device = named // leaves_dev
            begin = pl.multiple_of((named - device * leaves_dev) * leaf_points, leaf_points)
            points = coords_pool_ref[device, :, pl.ds(begin, leaf_points)]
            put_sources(sources_ref, 0, points)
            charges = charges_pool_ref[device, :, pl.ds(charges_at + begin, leaf_points)]
            total_ref[leaf] += kernel_sum(targets_ref[leaf], sources_ref[...], charges)
            return carry

        lax.fori_loop(0, used(leaf), near_step, 0)

    parts = [total_ref[leaf].T.astype(bf16) for leaf in range(leaves_dev)]
    result = jnp.concatenate(parts, axis=1)
    out_ref[...] = result
    if not last:
        local = leaves_dev * leaf_points
        weights, term = skeleton_weights(
            result, leaf_interp_ref, node_interp_ref, upper_interp_ref, leaves_dev
        )
        message_ref[:, 0:local] = result
        message_ref[:, local : local + skeleton] = weights
        message_ref[:, local + skeleton : local + 2 * skeleton] = term


def on_device(
    coords,
    charges,
    near_lists,
    far_lists,
    leaf_interp,
    node_interp,
    upper_interp,
    node_points,
    upper_points,
):
    dim, local = coords.shape
    columns = charges.shape[0]
    leaves_dev = near_lists.shape[0]
    leaf_points = local // leaves_dev
    skeleton = leaf_interp.shape[1]
    peers = lax.axis_size("leaf")
    nodes = peers + peers // BRANCH

    vmem = pl.BlockSpec(memory_space=pltpu.VMEM)
    smem = pl.BlockSpec(memory_space=pltpu.SMEM)
    params = pltpu.CompilerParams(vmem_limit_bytes=48 * 1024 * 1024)

    message = pl.pallas_call(
        functools.partial(message_kernel, leaves_dev),
        out_shape=jax.ShapeDtypeStruct((dim, 2 * local + 3 * skeleton), bf16),
        in_specs=[vmem] * 6,
        out_specs=vmem,
        compiler_params=params,
    )(coords, charges, node_points, leaf_interp, node_interp, upper_interp)
    pool = lax.all_gather(message, "leaf", axis=0)

    scratch = [
        pltpu.VMEM((leaves_dev, leaf_points, DEPTH), bf16),
        pltpu.VMEM((DEPTH, leaf_points), bf16),
        pltpu.VMEM((2 * columns, GROUP * skeleton), bf16),
        pltpu.VMEM((peers // BRANCH, columns, skeleton), bf16),
        pltpu.VMEM((leaves_dev, leaf_points, columns), f32),
        pltpu.SMEM((leaves_dev, nodes), jnp.int32),
    ]
    flat = jax.ShapeDtypeStruct((columns, local), bf16)
    sent = jax.ShapeDtypeStruct((columns, local + 2 * skeleton), bf16)

    dims = (leaves_dev, leaf_points, skeleton, peers)
    first, message = pl.pallas_call(
        functools.partial(product_kernel, dims + (local, 2 * local + skeleton, False)),
        out_shape=(flat, sent),
        in_specs=[smem] * 2 + [vmem] * 7,
        out_specs=(vmem, vmem),
        scratch_shapes=scratch,
        compiler_params=params,
    )(
        near_lists,
        far_lists,
        pool,
        pool,
        coords,
        upper_points,
        leaf_interp,
        node_interp,
        upper_interp,
    )
    again = lax.all_gather(message, "leaf", axis=0)
    second = pl.pallas_call(
        functools.partial(product_kernel, dims + (0, local, True)),
        out_shape=flat,
        in_specs=[smem] * 2 + [vmem] * 4,
        out_specs=vmem,
        scratch_shapes=scratch,
        compiler_params=params,
    )(near_lists, far_lists, pool, again, coords, upper_points)
    return (first, second)


def solution(mesh):
    placed = (
        P(None, ("groups", "leaf")),
        P(None, ("groups", "leaf")),
        P(("groups", "leaf"), None),
        P(("groups", "leaf"), None),
        P(("groups", "leaf"), None),
        P(("groups", "leaf"), None),
        P(("groups", "leaf"), None),
        P(None, ("groups", "leaf")),
        P(None, "groups"),
    )
    return jax.shard_map(
        on_device,
        mesh=mesh,
        in_specs=placed,
        out_specs=(P(None, ("groups", "leaf")), P(None, ("groups", "leaf"))),
        check_vma=False,
    )
```

```python
import functools

import jax
import jax.numpy as jnp
import numpy as np
from jax import lax
from jax.experimental import pallas as pl
from jax.experimental.pallas import tpu as pltpu
from jax.sharding import PartitionSpec as P

BRANCH = 16
EXTRA = 16
DEPTH = 128
CORES = 2

bf16 = jnp.bfloat16
f32 = jnp.float32
i32 = jnp.int32

CONTRACT_LAST = (((1,), (1,)), ((), ()))


def matmul(left, right):
    return jnp.dot(left, right, preferred_element_type=f32)


def square_parts(points):
    minus = -jnp.sum(points * points, axis=0, keepdims=True)
    high = minus.astype(bf16).astype(f32)
    rest = minus - high
    middle = rest.astype(bf16).astype(f32)
    low = rest - middle
    return high, middle, low


def extra_rows(parts, first, width):
    row = lax.broadcasted_iota(i32, (EXTRA, width), 0)
    rows = jnp.where(row < 6, 1.0, 0.0).astype(f32)
    for offset, part in enumerate(parts):
        rows = jnp.where(row == first + offset, jnp.broadcast_to(part, (EXTRA, width)), rows)
    return rows


def put_sources(sources_ref, points):
    dim, width = points.shape
    sources_ref[0:dim, :] = points
    parts = square_parts(points.astype(f32))
    sources_ref[dim : dim + EXTRA, :] = extra_rows(parts, 3, width).astype(bf16)
    sources_ref[dim + EXTRA :, :] = jnp.zeros((DEPTH - dim - EXTRA, width), bf16)


def target_rows(points):
    dim, width = points.shape
    points = points.astype(f32)
    extra = extra_rows(square_parts(points), 0, width)
    blank = jnp.zeros((DEPTH - dim - EXTRA, width), f32)
    return jnp.concatenate([2.0 * points, extra, blank], axis=0).T.astype(bf16)


def split(values):
    high = values.astype(bf16)
    return high, (values - high.astype(f32)).astype(bf16)


def kernel_sum(targets, sources, charges):
    total = targets.shape[0]
    step = min(total, 256)
    out = []
    for begin in range(0, total, step):
        exponent = matmul(targets[begin : begin + step], sources)
        kernel = jnp.exp(exponent).astype(bf16)
        out.append(lax.dot_general(kernel, charges, CONTRACT_LAST, preferred_element_type=f32))
    return jnp.concatenate(out, axis=0)


def skeleton_weights(charges, leaf_interp_ref, node_interp_ref, upper_interp_ref):
    leaf_points = charges[0].shape[1]
    parts = []
    for leaf, block in enumerate(charges):
        span = slice(leaf * leaf_points, (leaf + 1) * leaf_points)
        parts.append(matmul(block, leaf_interp_ref[span, :]).astype(bf16))
    device_weights = matmul(jnp.concatenate(parts, axis=1), node_interp_ref[...]).astype(bf16)
    upper_term = matmul(device_weights, upper_interp_ref[...]).astype(bf16)
    return device_weights, upper_term


def message_kernel(
    coords_ref, charges_ref, points_ref, leaf_ref, node_ref, upper_ref, part0_ref, part1_ref
):
    half = coords_ref.shape[1] // 2
    skeleton = points_ref.shape[1]
    charges = [charges_ref[:, 0:half], charges_ref[:, half:]]
    weights, term = skeleton_weights(charges, leaf_ref, node_ref, upper_ref)
    part0_ref[:, 0:half] = charges[0]
    part0_ref[:, half : half + skeleton] = weights
    part0_ref[:, half + skeleton : 2 * half + skeleton] = coords_ref[:, 0:half]
    part0_ref[:, 2 * half + skeleton :] = points_ref[...]
    part1_ref[:, 0:half] = charges[1]
    part1_ref[:, half : half + skeleton] = term
    part1_ref[:, half + skeleton :] = coords_ref[:, half:]


def joined_kernel(mine_ref, other_ref, leaf_ref, node_ref, upper_ref, out_ref, part0_ref, part1_ref):
    half = mine_ref.shape[1] // 2
    skeleton = node_ref.shape[1]
    result = (mine_ref[...] + other_ref[...]).astype(bf16)
    out_ref[...] = result
    charges = [result[:, 0:half], result[:, half:]]
    weights, term = skeleton_weights(charges, leaf_ref, node_ref, upper_ref)
    part0_ref[:, 0:half] = charges[0]
    part0_ref[:, half : half + skeleton] = weights
    part1_ref[:, 0:half] = charges[1]
    part1_ref[:, half : half + skeleton] = term


def added_kernel(mine_ref, other_ref, out_ref):
    out_ref[...] = (mine_ref[...] + other_ref[...]).astype(bf16)


def stage_kernel(stage, *refs):
    spots, n_spots, n_sub, leaf_points, skeleton, first, last, with_targets = stage
    refs = list(refs)
    table_ref = refs.pop(0)
    pairs = [(refs.pop(0), refs.pop(0)) for _ in spots]
    charge_pairs = [(refs.pop(0), refs.pop(0)) for _ in spots]
    if with_targets:
        coords_refs = (refs.pop(0), refs.pop(0))
    else:
        targets_ref = refs.pop(0)
    if not first:
        total_in_ref, sums_in_ref = refs.pop(0), refs.pop(0)
    if last:
        upper_points_ref = refs.pop(0)
    if with_targets:
        targets_ref = refs.pop(0)
    if last:
        mine_ref, other_ref, total_ref, sums_ref = (refs.pop(0) for _ in range(4))
    else:
        total_ref, sums_ref = refs.pop(0), refs.pop(0)
    near_ref, far_ref, far_charges_ref, charges_ref = refs

    columns = charge_pairs[0][0].shape[0]
    points_at = leaf_points + skeleton
    skeletons_at = points_at + leaf_points
    targets = 2 * CORES

    if with_targets:
        for core in range(CORES):
            for leaf in range(2):
                span = slice(leaf * leaf_points, (leaf + 1) * leaf_points)
                targets_ref[core * 2 + leaf] = target_rows(coords_refs[core][:, span])
    if first:
        total_ref[...] = jnp.zeros_like(total_ref)
        sums_ref[...] = jnp.zeros_like(sums_ref)
    else:
        total_ref[...] = total_in_ref[...]
        sums_ref[...] = sums_in_ref[...]

    def far_part(points, weights, entries):
        width = len(points) * skeleton
        put_sources(far_ref.at[:, 0:width], jnp.concatenate(points, axis=1))
        for target in range(targets):
            for position, (block, entry) in enumerate(zip(weights, entries)):
                high, low = split(block * table_ref[target, entry].astype(f32))
                span = slice(position * skeleton, (position + 1) * skeleton)
                far_charges_ref[0:columns, span] = high
                far_charges_ref[columns:, span] = low
            total_ref[target] += kernel_sum(
                targets_ref[target], far_ref[:, 0:width], far_charges_ref[:, 0:width]
            )

    for position, spot in enumerate(spots):
        part0_ref, part1_ref = charge_pairs[position]
        term = part1_ref[:, leaf_points : leaf_points + skeleton].astype(f32)
        sums_ref[table_ref[targets, spot]] += term
        for leaf in range(2):
            place = position * 2 + leaf
            put_sources(
                near_ref.at[place], pairs[position][leaf][:, points_at : points_at + leaf_points]
            )
            charges_ref[place] = charge_pairs[position][leaf][:, 0:leaf_points]

    far_part(
        [pair[0][:, skeletons_at : skeletons_at + skeleton] for pair in pairs],
        [
            pair[0][:, leaf_points : leaf_points + skeleton].astype(f32)
            for pair in charge_pairs
        ],
        [2 * n_spots + spot for spot in spots],
    )
    if last:
        for begin in range(0, n_sub, 2):
            subs = range(begin, min(begin + 2, n_sub))
            far_part(
                [upper_points_ref[:, sub * skeleton : (sub + 1) * skeleton] for sub in subs],
                [sums_ref[sub] for sub in subs],
                [3 * n_spots + sub for sub in subs],
            )

    def near_step(turn, carry):
        place, target = turn // targets, turn % targets
        times = table_ref[target, spots[0] * 2 + place]

        def once(_, carry):
            total_ref[target, :, 0:columns] += kernel_sum(
                targets_ref[target], near_ref[place], charges_ref[place]
            )
            return carry

        return lax.fori_loop(0, times, once, carry)

    lax.fori_loop(0, 2 * len(spots) * targets, near_step, 0)

    if last:
        for core, ref in enumerate((mine_ref, other_ref)):
            for leaf in range(2):
                total = total_ref[core * 2 + leaf].T
                span = slice(leaf * leaf_points, (leaf + 1) * leaf_points)
                ref[:, span] = total[0:columns] + total[columns:]


def whole_block(shape):
    return pl.BlockSpec(shape, lambda i: (0,) * len(shape))


def call(body, args, out_shapes, scratch=(), flops=0):
    specs = [
        pl.BlockSpec(memory_space=pltpu.SMEM) if arg.dtype == i32 else whole_block(arg.shape)
        for arg in args
    ]
    moved = sum(arg.size * arg.dtype.itemsize for arg in args)
    return pl.pallas_call(
        body,
        grid=(1,),
        out_shape=out_shapes,
        in_specs=specs,
        out_specs=[whole_block(out.shape) for out in out_shapes],
        scratch_shapes=list(scratch),
        compiler_params=pltpu.CompilerParams(vmem_limit_bytes=56 * 1024 * 1024),
        cost_estimate=pl.CostEstimate(flops=flops, bytes_accessed=moved, transcendentals=0),
    )(*args)


def ring_order(chips):
    if chips == 8:
        return [0, 2, 4, 6, 7, 5, 3, 1]
    return list(range(chips))


def spots_of(peers):
    ring = ring_order(peers // CORES)
    chips = len(ring)
    found = np.zeros((peers, chips), np.int32)
    for place, chip in enumerate(ring):
        met = [chip]
        for hop in range(1, chips // 2):
            met += [ring[(place - hop) % chips], ring[(place + hop) % chips]]
        met.append(ring[(place + chips // 2) % chips])
        for core in range(CORES):
            found[chip * CORES + core] = [other * CORES + core for other in met]
    return found


def on_device(
    coords,
    charges,
    near_lists,
    far_lists,
    leaf_interp,
    node_interp,
    upper_interp,
    node_points,
    upper_points,
):
    dim, local = coords.shape
    columns = charges.shape[0]
    leaf_points = local // 2
    skeleton = leaf_interp.shape[1]
    peers = lax.axis_size("leaf")
    me = lax.axis_index("leaf")
    n_sub = peers // BRANCH
    ring = ring_order(peers // CORES)
    chips = len(ring)
    near_slots = near_lists.shape[1]

    def along(step):
        return [
            (ring[place] * CORES + core, ring[(place + step) % chips] * CORES + core)
            for place in range(chips)
            for core in range(CORES)
        ]

    to_right = functools.partial(lax.ppermute, axis_name="leaf", perm=along(1))
    to_left = functools.partial(lax.ppermute, axis_name="leaf", perm=along(-1))
    to_sibling = functools.partial(
        lax.ppermute, axis_name="leaf", perm=[(device, device ^ 1) for device in range(peers)]
    )

    def shape(*extent, dtype=bf16):
        return jax.ShapeDtypeStruct(extent, dtype)

    maps = [leaf_interp, node_interp, upper_interp]
    parts = call(
        message_kernel,
        [coords, charges, node_points] + maps,
        [
            shape(dim, 2 * leaf_points + 2 * skeleton),
            shape(dim, 2 * leaf_points + skeleton),
        ],
    )

    lists = jnp.concatenate([near_lists, far_lists], axis=1)
    lists = jnp.concatenate([lists, to_sibling(lists)], axis=0)
    sibling_coords = to_sibling(coords)
    spots = lax.dynamic_index_in_dim(jnp.asarray(spots_of(peers)), me, 0, keepdims=False)
    near_ids = (spots[:, None] * 2 + jnp.arange(2)[None, :]).reshape(-1)
    far_ids = jnp.concatenate([spots, peers + jnp.arange(n_sub)])
    counts = jnp.concatenate(
        [
            jnp.sum((lists[:, :near_slots, None] == near_ids).astype(i32), axis=1),
            jnp.sum((lists[:, near_slots:, None] == far_ids).astype(i32), axis=1),
        ],
        axis=1,
    )
    branch = jnp.pad(spots // BRANCH, (0, counts.shape[1] - chips))
    table = jnp.concatenate([counts, branch[None, :]], axis=0)

    total_shape = shape(2 * CORES, leaf_points, 2 * columns, dtype=f32)
    sums_shape = shape(n_sub, columns, skeleton, dtype=f32)
    flat_shape = shape(columns, local, dtype=f32)
    targets_shape = shape(2 * CORES, leaf_points, DEPTH)

    def stage(places, points, weights, targets, carried, last):
        first = carried is None
        with_targets = targets is None
        args = [table]
        args += [part for pair in points for part in pair]
        args += [part for pair in weights for part in pair]
        args += [coords, sibling_coords] if with_targets else [targets]
        args += [] if first else list(carried)
        args += [upper_points] if last else []
        scratch = [
            pltpu.VMEM((2 * len(places), DEPTH, leaf_points), bf16),
            pltpu.VMEM((DEPTH, 2 * skeleton), bf16),
            pltpu.VMEM((2 * columns, 2 * skeleton), bf16),
            pltpu.VMEM((2 * len(places), columns, leaf_points), bf16),
        ]
        outs = [targets_shape] if with_targets else []
        if last:
            outs += [flat_shape, flat_shape]
            scratch = [pltpu.VMEM(total_shape.shape, f32), pltpu.VMEM(sums_shape.shape, f32)] + scratch
        else:
            outs += [total_shape, sums_shape]
        static = (places, chips, n_sub, leaf_points, skeleton, first, last, with_targets)
        return call(
            functools.partial(stage_kernel, static), args, outs, scratch, flops=len(places) * 2 * 10**9
        )

    def around(parts, points, targets):
        met = [[parts]]
        right = left = parts
        for hop in range(1, chips // 2):
            right = [to_right(part) for part in right]
            left = [to_left(part) for part in left]
            met.append([right, left])
        met.append([[to_right(right[0]), to_left(left[1])]])
        points = met if points is None else points
        carried = None
        place = 0
        for turn, messages in enumerate(met):
            places = tuple(range(place, place + len(messages)))
            place += len(messages)
            last = turn == len(met) - 1
            carried = stage(places, points[turn], messages, targets, carried, last)
            if targets is None:
                targets, *carried = carried
        return met, targets, carried

    points, targets, (mine, other) = around(parts, None, None)
    first, *parts = call(
        joined_kernel,
        [mine, to_sibling(other)] + maps,
        [shape(columns, local)] + [shape(columns, leaf_points + skeleton)] * 2,
    )
    _, _, (mine, other) = around(parts, points, targets)
    (second,) = call(added_kernel, [mine, to_sibling(other)], [shape(columns, local)])
    return (first, second)


def solution(mesh):
    placed = (
        P(None, ("groups", "leaf")),
        P(None, ("groups", "leaf")),
        P(("groups", "leaf"), None),
        P(("groups", "leaf"), None),
        P(("groups", "leaf"), None),
        P(("groups", "leaf"), None),
        P(("groups", "leaf"), None),
        P(None, ("groups", "leaf")),
        P(None, "groups"),
    )
    return jax.shard_map(
        on_device,
        mesh=mesh,
        in_specs=placed,
        out_specs=(P(None, ("groups", "leaf")), P(None, ("groups", "leaf"))),
        check_vma=False,
    )
```

```python
import functools

import jax
import jax.numpy as jnp
import numpy as np
from jax import lax
from jax.experimental import pallas as pl
from jax.experimental.pallas import tpu as pltpu
from jax.sharding import PartitionSpec as P

BRANCH = 16
EXTRA = 16
LANES = 128
CORES = 2
LEAVES = 2
TARGETS = CORES * LEAVES

bf16 = jnp.bfloat16
f32 = jnp.float32
i32 = jnp.int32


def matmul(left, right):
    return jnp.dot(left, right, preferred_element_type=f32)


def square_parts(points):
    minus = -jnp.sum(points * points, axis=0, keepdims=True)
    high = minus.astype(bf16).astype(f32)
    rest = minus - high
    middle = rest.astype(bf16).astype(f32)
    low = rest - middle
    return high, middle, low


def extra_rows(parts, first, width):
    row = lax.broadcasted_iota(i32, (EXTRA, width), 0)
    rows = jnp.where(row < 6, 1.0, 0.0).astype(f32)
    for offset, part in enumerate(parts):
        rows = jnp.where(row == first + offset, jnp.broadcast_to(part, (EXTRA, width)), rows)
    return rows


def put_sources(sources_ref, points):
    dim, width = points.shape
    sources_ref[0:dim, :] = points
    parts = square_parts(points.astype(f32))
    sources_ref[dim : dim + EXTRA, :] = extra_rows(parts, 3, width).astype(bf16)
    sources_ref[dim + EXTRA :, :] = jnp.zeros((LANES - dim - EXTRA, width), bf16)


def target_rows(points):
    dim, width = points.shape
    points = points.astype(f32)
    extra = extra_rows(square_parts(points), 0, width)
    blank = jnp.zeros((LANES - dim - EXTRA, width), f32)
    return jnp.concatenate([2.0 * points, extra, blank], axis=0).T.astype(bf16)


def in_low_half(shape):
    return lax.broadcasted_iota(i32, shape, 1) < LANES // 2


def swapped(values):
    return pltpu.roll(values, LANES // 2, 1)


def kernel_sum(targets, sources, charges):
    total = None
    width = sources.shape[1]
    step = min(width, 256)
    for begin in range(0, width, step):
        kernel = jnp.exp(matmul(targets, sources[:, begin : begin + step])).astype(bf16)
        added = matmul(kernel, charges[begin : begin + step])
        total = added if total is None else total + added
    return total


def skeleton_rows(charges, leaf_ref, node_ref, upper_ref):
    points = charges[0].shape[1]
    parts = []
    for leaf, block in enumerate(charges):
        span = slice(leaf * points, (leaf + 1) * points)
        parts.append(matmul(block, leaf_ref[span, :]).astype(bf16))
    weights = matmul(jnp.concatenate(parts, axis=1), node_ref[...]).astype(bf16)
    term = matmul(weights, upper_ref[...])
    return jnp.concatenate([weights.astype(f32), term], axis=0).T.astype(bf16)


def message_kernel(
    coords_ref, charges_ref, points_ref, leaf_ref, node_ref, upper_ref, message_ref
):
    dim, local = coords_ref.shape
    half = local // LEAVES
    charges = [charges_ref[:, 0:half], charges_ref[:, half:]]
    message_ref[0:half, :] = jnp.concatenate(charges, axis=0).astype(f32).T.astype(bf16)
    message_ref[half : half + LANES, :] = skeleton_rows(charges, leaf_ref, node_ref, upper_ref)
    place = half + LANES
    for block in range(local // LANES):
        message_ref[place : place + dim, :] = coords_ref[:, block * LANES : (block + 1) * LANES]
        place += dim
    message_ref[place : place + dim, :] = points_ref[...]


def joined_kernel(mine_ref, other_ref, leaf_ref, node_ref, upper_ref, out_ref, message_ref):
    half = mine_ref.shape[0]
    columns = LANES // LEAVES
    result = mine_ref[...] + other_ref[...]
    message_ref[0:half, :] = result.astype(bf16)
    flat = result.T.astype(bf16)
    charges = [flat[0:columns], flat[columns:]]
    out_ref[...] = jnp.concatenate(charges, axis=1)
    message_ref[half : half + LANES, :] = skeleton_rows(charges, leaf_ref, node_ref, upper_ref)


def added_kernel(mine_ref, other_ref, out_ref):
    columns = LANES // LEAVES
    flat = (mine_ref[...] + other_ref[...]).T.astype(bf16)
    out_ref[...] = jnp.concatenate([flat[0:columns], flat[columns:]], axis=1)


def stage_kernel(stage, *refs):
    spots, n_spots, n_sub, dim, points, first, last, with_targets = stage
    refs = list(refs)
    table_ref = refs.pop(0)
    place_refs = [refs.pop(0) for _ in spots]
    charge_refs = [refs.pop(0) for _ in spots]
    if with_targets:
        coords_refs = (refs.pop(0), refs.pop(0))
    else:
        targets_ref = refs.pop(0)
    if not first:
        total_in_ref, sums_in_ref = refs.pop(0), refs.pop(0)
    if last:
        upper_points_ref = refs.pop(0)
    if with_targets:
        targets_ref = refs.pop(0)
    if last:
        half_refs = refs.pop(0), refs.pop(0)
    total_ref, sums_ref, near_ref, far_ref, far_charges_ref, charges_ref = refs

    coords_at = points + LANES
    blocks = points // LANES
    low_half = in_low_half((LANES, LANES))

    if with_targets:
        for core in range(CORES):
            for leaf in range(LEAVES):
                span = slice(leaf * points, (leaf + 1) * points)
                targets_ref[core * LEAVES + leaf] = target_rows(coords_refs[core][:, span])
    if first:
        total_ref[...] = jnp.zeros_like(total_ref)
        sums_ref[...] = jnp.zeros_like(sums_ref)
    elif last:
        total_ref[...] = total_in_ref[...]
        sums_ref[...] = sums_in_ref[...]

    def far_part(skeletons, weights, entries):
        width = len(skeletons) * LANES
        put_sources(far_ref.at[:, 0:width], jnp.concatenate(skeletons, axis=1))

        def step(core, carry):
            for leaf in range(LEAVES):
                target = core * LEAVES + leaf
                for position, (block, entry) in enumerate(zip(weights, entries)):
                    scaled = block * table_ref[target, entry].astype(f32)
                    high = scaled.astype(bf16).astype(f32)
                    rows = pl.ds(position * LANES, LANES)
                    far_charges_ref[leaf, rows, :] = jnp.where(
                        low_half, high, scaled - high
                    ).astype(bf16)
                total_ref[target] += kernel_sum(
                    targets_ref[target], far_ref[:, 0:width], far_charges_ref[leaf, 0:width]
                )
            return carry

        lax.fori_loop(0, CORES, step, 0)

    weights = []
    for position, spot in enumerate(spots):
        rows = charge_refs[position][points : points + LANES, :].astype(f32)
        weights.append(jnp.where(low_half, rows, swapped(rows)))
        sums_ref[table_ref[TARGETS, spot]] += rows
        lane = lax.broadcasted_iota(i32, (1, LANES), 1) // (LANES // LEAVES)
        for leaf in range(LEAVES):
            place = position * LEAVES + leaf
            begin = coords_at + leaf * blocks * dim
            own = [
                place_refs[position][begin + block * dim : begin + (block + 1) * dim, :]
                for block in range(blocks)
            ]
            put_sources(near_ref.at[place], jnp.concatenate(own, axis=1))
            chosen = jnp.where(lane == leaf, 1.0, 0.0).astype(bf16)
            charges_ref[place] = charge_refs[position][0:points, :] * chosen

    skeletons_at = coords_at + LEAVES * blocks * dim
    far_part(
        [ref[skeletons_at : skeletons_at + dim, :] for ref in place_refs],
        weights,
        [LEAVES * n_spots + spot for spot in spots],
    )
    if last:
        for begin in range(0, n_sub, 2):
            subs = range(begin, min(begin + 2, n_sub))
            far_part(
                [upper_points_ref[:, sub * LANES : (sub + 1) * LANES] for sub in subs],
                [jnp.where(low_half, swapped(sums_ref[sub]), sums_ref[sub]) for sub in subs],
                [(LEAVES + 1) * n_spots + sub for sub in subs],
            )

    def near_part(position, spot, core, leaf):
        targets = [core * LEAVES + own for own in range(LEAVES)]
        if leaf is None:
            named = sum(table_ref[target, spot * LEAVES + 1] for target in targets)
            leaf = jnp.where(named > 0, 1, 0)
        place = position * LEAVES + leaf
        times = [table_ref[target, spot * LEAVES + leaf] for target in targets]

        @pl.when(sum(times) > 0)
        def _():
            for target, count in zip(targets, times):
                total_ref[target] += count.astype(f32) * kernel_sum(
                    targets_ref[target], near_ref[place], charges_ref[place]
                )

    if first:
        def near_step(turn, carry):
            named = table_ref[LEAVES, 1] + table_ref[LEAVES + 1, 1]
            other = jnp.where(named > 0, 1, 0)
            near_part(0, 0, turn // LEAVES, jnp.where(turn < LEAVES, turn, other))
            return carry

        lax.fori_loop(0, LEAVES + 1, near_step, 0)
    else:

        def near_step(turn, carry):
            position = turn // CORES
            near_part(position, spots[0] + position, turn % CORES, None)
            return carry

        lax.fori_loop(0, len(spots) * CORES, near_step, 0)

    if last:
        for core, ref in enumerate(half_refs):
            both = [total_ref[core * LEAVES + leaf] for leaf in range(LEAVES)]
            both = [total + swapped(total) for total in both]
            ref[...] = jnp.where(in_low_half(both[0].shape), both[0], both[1])


def call(body, args, out_shapes, streamed=(), scratch=(), aliases={}, flops=0, vmem_mib=24):
    vmem = pl.BlockSpec(memory_space=pltpu.VMEM)
    specs = []
    for place, arg in enumerate(args):
        if arg.dtype == i32:
            specs.append(pl.BlockSpec(memory_space=pltpu.SMEM))
        elif place in streamed:
            specs.append(pl.BlockSpec(arg.shape, lambda i: (0,) * 2))
        else:
            specs.append(vmem)
    moved = sum(arg.size * arg.dtype.itemsize for arg in args)
    return pl.pallas_call(
        body,
        grid=(1,),
        out_shape=out_shapes,
        in_specs=specs,
        out_specs=[vmem for _ in out_shapes],
        scratch_shapes=list(scratch),
        input_output_aliases=aliases,
        compiler_params=pltpu.CompilerParams(vmem_limit_bytes=vmem_mib * 1024 * 1024),
        cost_estimate=pl.CostEstimate(flops=flops, bytes_accessed=moved, transcendentals=0),
    )(*args)


def ring_order(chips):
    if chips == 8:
        return [0, 2, 4, 6, 7, 5, 3, 1]
    return list(range(chips))


def spots_of(peers):
    ring = ring_order(peers // CORES)
    chips = len(ring)
    found = np.zeros((peers, chips), np.int32)
    for place, chip in enumerate(ring):
        for core in range(CORES):
            way = 1 - 2 * core
            met = [chip]
            for hop in range(1, chips // 2):
                met += [ring[(place - way * hop) % chips], ring[(place + way * hop) % chips]]
            met.append(ring[(place + chips // 2) % chips])
            found[chip * CORES + core] = [other * CORES + core for other in met]
    return found


def on_device(
    coords,
    charges,
    near_lists,
    far_lists,
    leaf_interp,
    node_interp,
    upper_interp,
    node_points,
    upper_points,
):
    dim, local = coords.shape
    columns = charges.shape[0]
    points = local // LEAVES
    peers = lax.axis_size("leaf")
    me = lax.axis_index("leaf")
    n_sub = peers // BRANCH
    ring = ring_order(peers // CORES)
    chips = len(ring)
    near_slots = near_lists.shape[1]

    def along(step):
        return [
            (ring[place] * CORES + core, ring[(place + step * (1 - 2 * core)) % chips] * CORES + core)
            for place in range(chips)
            for core in range(CORES)
        ]

    one_way = functools.partial(lax.ppermute, axis_name="leaf", perm=along(1))
    other_way = functools.partial(lax.ppermute, axis_name="leaf", perm=along(-1))
    to_sibling = functools.partial(
        lax.ppermute, axis_name="leaf", perm=[(device, device ^ 1) for device in range(peers)]
    )

    def shape(*extent, dtype=bf16):
        return jax.ShapeDtypeStruct(extent, dtype)

    maps = [leaf_interp, node_interp, upper_interp]
    (message,) = call(
        message_kernel,
        [coords, charges, node_points] + maps,
        [shape(points + LANES + LEAVES * points // LANES * dim + dim, LANES)],
        streamed=range(6),
        vmem_mib=60,
    )

    lists = jnp.concatenate([near_lists, far_lists], axis=1)
    lists = jnp.concatenate([lists, to_sibling(lists)], axis=0)
    sibling_coords = to_sibling(coords)
    spots = lax.dynamic_index_in_dim(jnp.asarray(spots_of(peers)), me, 0, keepdims=False)
    near_ids = (spots[:, None] * LEAVES + jnp.arange(LEAVES)[None, :]).reshape(-1)
    far_ids = jnp.concatenate([spots, peers + jnp.arange(n_sub)])
    counts = jnp.concatenate(
        [
            jnp.sum((lists[:, :near_slots, None] == near_ids).astype(i32), axis=1),
            jnp.sum((lists[:, near_slots:, None] == far_ids).astype(i32), axis=1),
        ],
        axis=1,
    )
    branch = jnp.pad(spots // BRANCH, (0, counts.shape[1] - chips))
    table = jnp.concatenate([counts, branch[None, :]], axis=0)

    total_shape = shape(TARGETS, points, LANES, dtype=f32)
    sums_shape = shape(n_sub, LANES, LANES, dtype=f32)
    half_shape = shape(points, LANES, dtype=f32)
    targets_shape = shape(TARGETS, points, LANES)

    def stage(places, placed, charged, targets, carried, last):
        first = carried is None
        with_targets = targets is None
        args = [table] + placed + charged
        streamed = []
        if with_targets:
            streamed = [len(args)]
            args += [coords, sibling_coords]
        else:
            args += [targets]
        carried_at = len(args)
        args += [] if first else list(carried)
        args += [upper_points] if last else []
        scratch = [
            pltpu.VMEM((LEAVES * len(places), LANES, points), bf16),
            pltpu.VMEM((LANES, 2 * LANES), bf16),
            pltpu.VMEM((LEAVES, 2 * LANES, LANES), bf16),
            pltpu.VMEM((LEAVES * len(places), points, LANES), bf16),
        ]
        outs = [targets_shape] if with_targets else []
        aliases = {}
        if last:
            outs += [half_shape, half_shape]
            scratch = [pltpu.VMEM(total_shape.shape, f32), pltpu.VMEM(sums_shape.shape, f32)] + scratch
        else:
            if not first:
                aliases = {carried_at: len(outs), carried_at + 1: len(outs) + 1}
            outs += [total_shape, sums_shape]
        static = (places, chips, n_sub, dim, points, first, last, with_targets)
        return call(
            functools.partial(stage_kernel, static),
            args,
            outs,
            streamed=streamed,
            scratch=scratch,
            aliases=aliases,
            flops=len(places) * 2 * 10**9,
        )

    def around(message, placed, targets):
        met = [[message]]
        one = other = message
        for hop in range(1, chips // 2):
            one, other = one_way(one), other_way(other)
            met.append([one, other])
        met.append([one_way(one)])
        placed = met if placed is None else placed
        carried = None
        place = 0
        for turn, messages in enumerate(met):
            places = tuple(range(place, place + len(messages)))
            place += len(messages)
            last = turn == len(met) - 1
            carried = stage(places, placed[turn], messages, targets, carried, last)
            if targets is None:
                targets, *carried = carried
        return met, targets, carried

    placed, targets, (mine, other) = around(message, None, None)
    first, message = call(
        joined_kernel,
        [mine, to_sibling(other)] + maps,
        [shape(columns, local), shape(points + LANES, LANES)],
    )
    _, _, (mine, other) = around(message, placed, targets)
    (second,) = call(added_kernel, [mine, to_sibling(other)], [shape(columns, local)])
    return (first, second)


def solution(mesh):
    placed = (
        P(None, ("groups", "leaf")),
        P(None, ("groups", "leaf")),
        P(("groups", "leaf"), None),
        P(("groups", "leaf"), None),
        P(("groups", "leaf"), None),
        P(("groups", "leaf"), None),
        P(("groups", "leaf"), None),
        P(None, ("groups", "leaf")),
        P(None, "groups"),
    )
    return jax.shard_map(
        on_device,
        mesh=mesh,
        in_specs=placed,
        out_specs=(P(None, ("groups", "leaf")), P(None, ("groups", "leaf"))),
        check_vma=False,
    )
```

```python
import functools

import jax
import jax.numpy as jnp
import numpy as np
from jax import lax
from jax.experimental import pallas as pl
from jax.experimental.pallas import tpu as pltpu
from jax.sharding import PartitionSpec as P

BRANCH = 16
EXTRA = 16
LANES = 128
CORES = 2
LEAVES = 2
TARGETS = CORES * LEAVES
KEPT_MIB = 30

bf16 = jnp.bfloat16
f32 = jnp.float32
i32 = jnp.int32


def matmul(left, right):
    return jnp.dot(left, right, preferred_element_type=f32)


def square_parts(points):
    minus = -jnp.sum(points * points, axis=0, keepdims=True)
    high = minus.astype(bf16).astype(f32)
    rest = minus - high
    middle = rest.astype(bf16).astype(f32)
    low = rest - middle
    return high, middle, low


def extra_rows(parts, first, width):
    row = lax.broadcasted_iota(i32, (EXTRA, width), 0)
    rows = jnp.where(row < 6, 1.0, 0.0).astype(f32)
    for offset, part in enumerate(parts):
        rows = jnp.where(row == first + offset, jnp.broadcast_to(part, (EXTRA, width)), rows)
    return rows


def put_sources(sources_ref, points):
    dim, width = points.shape
    sources_ref[0:dim, :] = points
    parts = square_parts(points.astype(f32))
    sources_ref[dim : dim + EXTRA, :] = extra_rows(parts, 3, width).astype(bf16)
    sources_ref[dim + EXTRA :, :] = jnp.zeros((LANES - dim - EXTRA, width), bf16)


def target_rows(points):
    dim, width = points.shape
    points = points.astype(f32)
    extra = extra_rows(square_parts(points), 0, width)
    blank = jnp.zeros((LANES - dim - EXTRA, width), f32)
    return jnp.concatenate([2.0 * points, extra, blank], axis=0).T.astype(bf16)


def in_low_half(shape):
    return lax.broadcasted_iota(i32, shape, 1) < LANES // 2


def swapped(values):
    return pltpu.roll(values, LANES // 2, 1)


def kernel_sum(targets, sources, charges, kept_ref):
    total = None
    width = sources.shape[1]
    step = min(width, 256)
    for begin in range(0, width, step):
        kernel = jnp.exp(matmul(targets, sources[:, begin : begin + step])).astype(bf16)
        if kept_ref is not None:
            kept_ref[:, begin : begin + step] = kernel
        added = matmul(kernel, charges[begin : begin + step])
        total = added if total is None else total + added
    return total


def skeleton_rows(charges, leaf_ref, node_ref, upper_ref):
    points = charges[0].shape[1]
    parts = []
    for leaf, block in enumerate(charges):
        span = slice(leaf * points, (leaf + 1) * points)
        parts.append(matmul(block, leaf_ref[span, :]).astype(bf16))
    weights = matmul(jnp.concatenate(parts, axis=1), node_ref[...]).astype(bf16)
    term = matmul(weights, upper_ref[...])
    return jnp.concatenate([weights.astype(f32), term], axis=0).T.astype(bf16)


def message_kernel(
    coords_ref, charges_ref, points_ref, leaf_ref, node_ref, upper_ref, message_ref
):
    dim, local = coords_ref.shape
    half = local // LEAVES
    charges = [charges_ref[:, 0:half], charges_ref[:, half:]]
    message_ref[0:half, :] = jnp.concatenate(charges, axis=0).astype(f32).T.astype(bf16)
    message_ref[half : half + LANES, :] = skeleton_rows(charges, leaf_ref, node_ref, upper_ref)
    place = half + LANES
    for block in range(local // LANES):
        message_ref[place : place + dim, :] = coords_ref[:, block * LANES : (block + 1) * LANES]
        place += dim
    message_ref[place : place + dim, :] = points_ref[...]


def joined_kernel(mine_ref, other_ref, leaf_ref, node_ref, upper_ref, out_ref, message_ref):
    half = mine_ref.shape[0]
    columns = LANES // LEAVES
    result = mine_ref[...] + other_ref[...]
    message_ref[0:half, :] = result.astype(bf16)
    flat = result.T.astype(bf16)
    charges = [flat[0:columns], flat[columns:]]
    out_ref[...] = jnp.concatenate(charges, axis=1)
    message_ref[half : half + LANES, :] = skeleton_rows(charges, leaf_ref, node_ref, upper_ref)


def added_kernel(mine_ref, other_ref, out_ref):
    columns = LANES // LEAVES
    flat = (mine_ref[...] + other_ref[...]).T.astype(bf16)
    out_ref[...] = jnp.concatenate([flat[0:columns], flat[columns:]], axis=1)


def stage_kernel(stage, *refs):
    spots, n_spots, n_sub, dim, points, first, last, with_targets, mode = stage
    refs = list(refs)
    use, keep = mode == "use", mode == "keep"
    table_ref = refs.pop(0)
    place_refs = [] if use else [refs.pop(0) for _ in spots]
    charge_refs = [refs.pop(0) for _ in spots]
    near_kept_ref = far_kept_ref = upper_kept_ref = targets_ref = None
    if use:
        near_kept_ref, far_kept_ref = refs.pop(0), refs.pop(0)
        upper_kept_ref = refs.pop(0) if last else None
    elif with_targets:
        coords_refs = (refs.pop(0), refs.pop(0))
    else:
        targets_ref = refs.pop(0)
    if not first:
        total_in_ref, sums_in_ref = refs.pop(0), refs.pop(0)
    if last and not use:
        upper_points_ref = refs.pop(0)
    if with_targets:
        targets_ref = refs.pop(0)
    if keep:
        near_kept_ref, far_kept_ref = refs.pop(0), refs.pop(0)
        upper_kept_ref = refs.pop(0) if last else None
    if last:
        half_refs = refs.pop(0), refs.pop(0)
    total_ref, sums_ref, far_charges_ref, charges_ref = refs[:4]
    if not use:
        near_ref, far_ref = refs[4:]

    coords_at = points + LANES
    blocks = points // LANES
    low_half = in_low_half((LANES, LANES))

    if with_targets:
        for core in range(CORES):
            for leaf in range(LEAVES):
                span = slice(leaf * points, (leaf + 1) * points)
                targets_ref[core * LEAVES + leaf] = target_rows(coords_refs[core][:, span])
    if first:
        total_ref[...] = jnp.zeros_like(total_ref)
        sums_ref[...] = jnp.zeros_like(sums_ref)
    elif last:
        total_ref[...] = total_in_ref[...]
        sums_ref[...] = sums_in_ref[...]

    def added(target, sources_ref, charges, kept_ref):
        if use:
            return matmul(kept_ref[...], charges)
        return kernel_sum(targets_ref[target], sources_ref[...], charges, kept_ref)

    def far_part(skeletons, weights, entries, kept_ref, kept_at):
        width = len(weights) * LANES
        sources_ref = None
        if not use:
            sources_ref = far_ref.at[:, 0:width]
            put_sources(sources_ref, jnp.concatenate(skeletons, axis=1))

        def step(core, carry):
            for leaf in range(LEAVES):
                target = core * LEAVES + leaf
                for position, (block, entry) in enumerate(zip(weights, entries)):
                    scaled = block * table_ref[target, entry].astype(f32)
                    high = scaled.astype(bf16).astype(f32)
                    rows = pl.ds(position * LANES, LANES)
                    far_charges_ref[leaf, rows, :] = jnp.where(
                        low_half, high, scaled - high
                    ).astype(bf16)
                kept = None
                if kept_ref is not None:
                    kept = kept_ref.at[target, :, kept_at : kept_at + width]
                total_ref[target] += added(
                    target, sources_ref, far_charges_ref[leaf, 0:width], kept
                )
            return carry

        lax.fori_loop(0, CORES, step, 0)

    weights = []
    for position, spot in enumerate(spots):
        rows = charge_refs[position][points : points + LANES, :].astype(f32)
        weights.append(jnp.where(low_half, rows, swapped(rows)))
        sums_ref[table_ref[TARGETS, spot]] += rows
        lane = lax.broadcasted_iota(i32, (1, LANES), 1) // (LANES // LEAVES)
        for leaf in range(LEAVES):
            place = position * LEAVES + leaf
            if not use:
                begin = coords_at + leaf * blocks * dim
                own = [
                    place_refs[position][begin + block * dim : begin + (block + 1) * dim, :]
                    for block in range(blocks)
                ]
                put_sources(near_ref.at[place], jnp.concatenate(own, axis=1))
            chosen = jnp.where(lane == leaf, 1.0, 0.0).astype(bf16)
            charges_ref[place] = charge_refs[position][0:points, :] * chosen

    skeletons_at = coords_at + LEAVES * blocks * dim
    far_part(
        [ref[skeletons_at : skeletons_at + dim, :] for ref in place_refs],
        weights,
        [LEAVES * n_spots + spot for spot in spots],
        far_kept_ref,
        0,
    )
    if last:
        for begin in range(0, n_sub, 2):
            subs = range(begin, min(begin + 2, n_sub))
            skeletons = []
            if not use:
                skeletons = [upper_points_ref[:, sub * LANES : (sub + 1) * LANES] for sub in subs]
            far_part(
                skeletons,
                [jnp.where(low_half, swapped(sums_ref[sub]), sums_ref[sub]) for sub in subs],
                [(LEAVES + 1) * n_spots + sub for sub in subs],
                upper_kept_ref,
                begin * LANES,
            )

    def near_part(turn, position, spot, core, leaf):
        targets = [core * LEAVES + own for own in range(LEAVES)]
        if leaf is None:
            named = sum(table_ref[target, spot * LEAVES + 1] for target in targets)
            leaf = jnp.where(named > 0, 1, 0)
        place = position * LEAVES + leaf
        times = [table_ref[target, spot * LEAVES + leaf] for target in targets]

        @pl.when(sum(times) > 0)
        def _():
            for own, (target, count) in enumerate(zip(targets, times)):
                kept = None if near_kept_ref is None else near_kept_ref.at[turn * LEAVES + own]
                sources_ref = None if use else near_ref.at[place]
                total_ref[target] += count.astype(f32) * added(
                    target, sources_ref, charges_ref[place], kept
                )

    if first:
        def near_step(turn, carry):
            named = table_ref[LEAVES, 1] + table_ref[LEAVES + 1, 1]
            other = jnp.where(named > 0, 1, 0)
            near_part(turn, 0, 0, turn // LEAVES, jnp.where(turn < LEAVES, turn, other))
            return carry

        lax.fori_loop(0, LEAVES + 1, near_step, 0)
    else:

        def near_step(turn, carry):
            position = turn // CORES
            near_part(turn, position, spots[0] + position, turn % CORES, None)
            return carry

        lax.fori_loop(0, len(spots) * CORES, near_step, 0)

    if last:
        for core, ref in enumerate(half_refs):
            both = [total_ref[core * LEAVES + leaf] for leaf in range(LEAVES)]
            both = [total + swapped(total) for total in both]
            ref[...] = jnp.where(in_low_half(both[0].shape), both[0], both[1])


def call(body, args, out_shapes, streamed=(), scratch=(), aliases={}, flops=0, vmem_mib=16):
    vmem = pl.BlockSpec(memory_space=pltpu.VMEM)
    specs = []
    for place, arg in enumerate(args):
        if arg.dtype == i32:
            specs.append(pl.BlockSpec(memory_space=pltpu.SMEM))
        elif place in streamed:
            specs.append(pl.BlockSpec(arg.shape, lambda i: (0,) * 2))
        else:
            specs.append(vmem)
    moved = sum(arg.size * arg.dtype.itemsize for arg in args)
    return pl.pallas_call(
        body,
        grid=(1,),
        out_shape=out_shapes,
        in_specs=specs,
        out_specs=[vmem for _ in out_shapes],
        scratch_shapes=list(scratch),
        input_output_aliases=aliases,
        compiler_params=pltpu.CompilerParams(vmem_limit_bytes=vmem_mib * 1024 * 1024),
        cost_estimate=pl.CostEstimate(flops=flops, bytes_accessed=moved, transcendentals=0),
    )(*args)


def ring_order(chips):
    if chips == 8:
        return [0, 2, 4, 6, 7, 5, 3, 1]
    return list(range(chips))


def spots_of(peers):
    ring = ring_order(peers // CORES)
    chips = len(ring)
    found = np.zeros((peers, chips), np.int32)
    for place, chip in enumerate(ring):
        for core in range(CORES):
            way = 1 - 2 * core
            met = [chip]
            for hop in range(1, chips // 2):
                met += [ring[(place - way * hop) % chips], ring[(place + way * hop) % chips]]
            met.append(ring[(place + chips // 2) % chips])
            found[chip * CORES + core] = [other * CORES + core for other in met]
    return found


def on_device(
    coords,
    charges,
    near_lists,
    far_lists,
    leaf_interp,
    node_interp,
    upper_interp,
    node_points,
    upper_points,
):
    dim, local = coords.shape
    columns = charges.shape[0]
    points = local // LEAVES
    peers = lax.axis_size("leaf")
    me = lax.axis_index("leaf")
    n_sub = peers // BRANCH
    ring = ring_order(peers // CORES)
    chips = len(ring)
    near_slots = near_lists.shape[1]

    def along(step):
        return [
            (ring[place] * CORES + core, ring[(place + step * (1 - 2 * core)) % chips] * CORES + core)
            for place in range(chips)
            for core in range(CORES)
        ]

    one_way = functools.partial(lax.ppermute, axis_name="leaf", perm=along(1))
    other_way = functools.partial(lax.ppermute, axis_name="leaf", perm=along(-1))
    to_sibling = functools.partial(
        lax.ppermute, axis_name="leaf", perm=[(device, device ^ 1) for device in range(peers)]
    )

    def shape(*extent, dtype=bf16):
        return jax.ShapeDtypeStruct(extent, dtype)

    maps = [leaf_interp, node_interp, upper_interp]
    (message,) = call(
        message_kernel,
        [coords, charges, node_points] + maps,
        [shape(points + LANES + LEAVES * points // LANES * dim + dim, LANES)],
        streamed=range(6),
        vmem_mib=60,
    )

    lists = jnp.concatenate([near_lists, far_lists], axis=1)
    lists = jnp.concatenate([lists, to_sibling(lists)], axis=0)
    sibling_coords = to_sibling(coords)
    spots = lax.dynamic_index_in_dim(jnp.asarray(spots_of(peers)), me, 0, keepdims=False)
    near_ids = (spots[:, None] * LEAVES + jnp.arange(LEAVES)[None, :]).reshape(-1)
    far_ids = jnp.concatenate([spots, peers + jnp.arange(n_sub)])
    counts = jnp.concatenate(
        [
            jnp.sum((lists[:, :near_slots, None] == near_ids).astype(i32), axis=1),
            jnp.sum((lists[:, near_slots:, None] == far_ids).astype(i32), axis=1),
        ],
        axis=1,
    )
    branch = jnp.pad(spots // BRANCH, (0, counts.shape[1] - chips))
    table = jnp.concatenate([counts, branch[None, :]], axis=0)

    total_shape = shape(TARGETS, points, LANES, dtype=f32)
    sums_shape = shape(n_sub, LANES, LANES, dtype=f32)
    half_shape = shape(points, LANES, dtype=f32)
    targets_shape = shape(TARGETS, points, LANES)

    steps = LEAVES + 1 + CORES * (chips - 1)
    kept_bytes = 2 * points * (steps * LEAVES * points + TARGETS * (chips + n_sub) * LANES)
    keeping = kept_bytes <= KEPT_MIB * 2**20

    def stage(places, placed, charged, targets, carried, last, kept):
        first = carried is None
        with_targets = targets is None
        mode = "use" if kept else "keep" if keeping else "make"
        args = [table] + ([] if kept else placed) + charged
        streamed = []
        if kept:
            args += kept
        elif with_targets:
            streamed = [len(args)]
            args += [coords, sibling_coords]
        else:
            args += [targets]
        carried_at = len(args)
        args += [] if first else list(carried)
        args += [upper_points] if last and not kept else []
        scratch = [
            pltpu.VMEM((LEAVES, 2 * LANES, LANES), bf16),
            pltpu.VMEM((LEAVES * len(places), points, LANES), bf16),
        ]
        if not kept:
            scratch += [
                pltpu.VMEM((LEAVES * len(places), LANES, points), bf16),
                pltpu.VMEM((LANES, 2 * LANES), bf16),
            ]
        outs = [targets_shape] if with_targets else []
        kept_at = len(outs)
        if mode == "keep":
            turns = LEAVES + 1 if first else CORES * len(places)
            outs += [
                shape(turns * LEAVES, points, points),
                shape(TARGETS, points, len(places) * LANES),
            ]
            outs += [shape(TARGETS, points, n_sub * LANES)] if last else []
        kept_to = len(outs)
        aliases = {}
        if last:
            outs += [half_shape, half_shape]
            scratch = [pltpu.VMEM(total_shape.shape, f32), pltpu.VMEM(sums_shape.shape, f32)] + scratch
        else:
            if not first:
                aliases = {carried_at: len(outs), carried_at + 1: len(outs) + 1}
            outs += [total_shape, sums_shape]
        static = (places, chips, n_sub, dim, points, first, last, with_targets, mode)
        results = call(
            functools.partial(stage_kernel, static),
            args,
            outs,
            streamed=streamed,
            scratch=scratch,
            aliases=aliases,
            flops=len(places) * (1 if kept else 2) * 10**9,
        )
        if with_targets:
            targets = results[0]
        return targets, list(results[kept_at:kept_to]), results[kept_to:]

    def around(message, placed, targets, kept):
        met = [[message]]
        one = other = message
        for hop in range(1, chips // 2):
            one, other = one_way(one), other_way(other)
            met.append([one, other])
        met.append([one_way(one)])
        placed = met if placed is None else placed
        carried = None
        place = 0
        made = []
        for turn, messages in enumerate(met):
            places = tuple(range(place, place + len(messages)))
            place += len(messages)
            last = turn == len(met) - 1
            given = kept[turn] if kept else []
            targets, values, carried = stage(
                places, placed[turn], messages, targets, carried, last, given
            )
            made.append(values)
        return met, targets, made, carried

    placed, targets, kept, (mine, other) = around(message, None, None, None)
    first, message = call(
        joined_kernel,
        [mine, to_sibling(other)] + maps,
        [shape(columns, local), shape(points + LANES, LANES)],
    )
    *_, (mine, other) = around(message, placed, targets, kept if keeping else None)
    (second,) = call(added_kernel, [mine, to_sibling(other)], [shape(columns, local)])
    return (first, second)


def solution(mesh):
    placed = (
        P(None, ("groups", "leaf")),
        P(None, ("groups", "leaf")),
        P(("groups", "leaf"), None),
        P(("groups", "leaf"), None),
        P(("groups", "leaf"), None),
        P(("groups", "leaf"), None),
        P(("groups", "leaf"), None),
        P(None, ("groups", "leaf")),
        P(None, "groups"),
    )
    return jax.shard_map(
        on_device,
        mesh=mesh,
        in_specs=placed,
        out_specs=(P(None, ("groups", "leaf")), P(None, ("groups", "leaf"))),
        check_vma=False,
    )
```

```python
import functools

import jax
import jax.numpy as jnp
from jax import lax
from jax.experimental import pallas as pl
from jax.experimental.pallas import tpu as pltpu
from jax.sharding import PartitionSpec as P

BRANCH = 16
EXTRA = 16
LANES = 128
CORES = 2
LEAVES = 2
TARGETS = CORES * LEAVES
KEPT_MIB = 30

bf16 = jnp.bfloat16
f32 = jnp.float32
i32 = jnp.int32


def matmul(left, right):
    return jnp.dot(left, right, preferred_element_type=f32)


def square_parts(points):
    minus = -jnp.sum(points * points, axis=0, keepdims=True)
    high = minus.astype(bf16).astype(f32)
    rest = minus - high
    middle = rest.astype(bf16).astype(f32)
    low = rest - middle
    return high, middle, low


def extra_rows(parts, first, width):
    row = lax.broadcasted_iota(i32, (EXTRA, width), 0)
    rows = jnp.where(row < 6, 1.0, 0.0).astype(f32)
    for offset, part in enumerate(parts):
        rows = jnp.where(row == first + offset, jnp.broadcast_to(part, (EXTRA, width)), rows)
    return rows


def put_sources(sources_ref, points):
    dim, width = points.shape
    sources_ref[0:dim, :] = points
    parts = square_parts(points.astype(f32))
    sources_ref[dim : dim + EXTRA, :] = extra_rows(parts, 3, width).astype(bf16)
    sources_ref[dim + EXTRA :, :] = jnp.zeros((LANES - dim - EXTRA, width), bf16)


def target_rows(points):
    dim, width = points.shape
    points = points.astype(f32)
    extra = extra_rows(square_parts(points), 0, width)
    blank = jnp.zeros((LANES - dim - EXTRA, width), f32)
    return jnp.concatenate([2.0 * points, extra, blank], axis=0).T.astype(bf16)


def in_low_half(shape):
    return lax.broadcasted_iota(i32, shape, 1) < LANES // 2


def swapped(values):
    return pltpu.roll(values, LANES // 2, 1)


def kernel_sum(targets, sources, charges, kept_ref):
    kernel = jnp.exp(matmul(targets, sources)).astype(bf16)
    if kept_ref is not None:
        kept_ref[...] = kernel
    return matmul(kernel, charges)


def skeleton_rows(charges, leaf_ref, node_ref, upper_ref):
    points = charges[0].shape[1]
    parts = []
    for leaf, block in enumerate(charges):
        span = slice(leaf * points, (leaf + 1) * points)
        parts.append(matmul(block, leaf_ref[span, :]).astype(bf16))
    weights = matmul(jnp.concatenate(parts, axis=1), node_ref[...]).astype(bf16)
    term = matmul(weights, upper_ref[...])
    return jnp.concatenate([weights.astype(f32), term], axis=0).T.astype(bf16)


def count_rows(ring, near_ref, far_ref):
    shape = (8, LANES)
    row, lane = lax.broadcasted_iota(i32, shape, 0), lax.broadcasted_iota(i32, shape, 1)
    table = jnp.zeros(shape, i32)
    for leaf in range(LEAVES):
        for first, ref in ((0, near_ref), (LEAVES, far_ref)):
            for slot in range(ref.shape[1]):
                hit = (row == first + leaf) & (lane == ref[leaf, slot])
                table = table + jnp.where(hit, 1, 0)
    chips = len(ring)
    me = lax.axis_index("leaf")
    core = me % CORES
    place = jnp.int32(0)
    for at, chip in enumerate(ring):
        place = jnp.where(me // CORES == chip, at, place)
    hop = (lane + 1) // 2
    way = jnp.where(lane % 2 == 1, -1, 1) * (1 - 2 * core)
    met = (place + way * hop + chips) % chips
    device = jnp.zeros(shape, i32)
    for at, chip in enumerate(ring):
        device = jnp.where(met == at, chip * CORES + core, device)
    return jnp.where(row == 2 * LEAVES, device, table)


def message_kernel(
    ring,
    near_ref,
    far_ref,
    coords_ref,
    charges_ref,
    points_ref,
    leaf_ref,
    node_ref,
    upper_ref,
    message_ref,
    table_ref,
):
    dim, local = coords_ref.shape
    half = local // LEAVES
    charges = [charges_ref[:, 0:half], charges_ref[:, half:]]
    message_ref[0:half, :] = jnp.concatenate(charges, axis=0).astype(f32).T.astype(bf16)
    message_ref[half : half + LANES, :] = skeleton_rows(charges, leaf_ref, node_ref, upper_ref)
    place = half + LANES
    for block in range(local // LANES):
        message_ref[place : place + dim, :] = coords_ref[:, block * LANES : (block + 1) * LANES]
        place += dim
    message_ref[place : place + dim, :] = points_ref[...]
    table_ref[...] = count_rows(ring, near_ref, far_ref)


def joined_kernel(mine_ref, other_ref, leaf_ref, node_ref, upper_ref, out_ref, message_ref):
    half = mine_ref.shape[0]
    columns = LANES // LEAVES
    result = mine_ref[...] + other_ref[...]
    message_ref[0:half, :] = result.astype(bf16)
    flat = result.T.astype(bf16)
    charges = [flat[0:columns], flat[columns:]]
    out_ref[...] = jnp.concatenate(charges, axis=1)
    message_ref[half : half + LANES, :] = skeleton_rows(charges, leaf_ref, node_ref, upper_ref)


def added_kernel(mine_ref, other_ref, out_ref):
    columns = LANES // LEAVES
    flat = (mine_ref[...] + other_ref[...]).T.astype(bf16)
    out_ref[...] = jnp.concatenate([flat[0:columns], flat[columns:]], axis=1)


def stage_kernel(stage, *refs):
    spots, n_spots, n_sub, dim, points, first, last, with_targets, mode = stage
    refs = list(refs)
    use, keep = mode == "use", mode == "keep"
    table_refs = refs.pop(0), refs.pop(0)
    place_refs = [] if use else [refs.pop(0) for _ in spots]
    charge_refs = [refs.pop(0) for _ in spots]
    near_kept_ref = far_kept_ref = upper_kept_ref = targets_ref = None
    if use:
        near_kept_ref, far_kept_ref = refs.pop(0), refs.pop(0)
        upper_kept_ref = refs.pop(0) if last else None
    elif with_targets:
        sibling_ref = refs.pop(0)
    else:
        targets_ref = refs.pop(0)
    if not first:
        total_in_ref, sums_in_ref = refs.pop(0), refs.pop(0)
    if last and not use:
        upper_points_ref = refs.pop(0)
    if with_targets:
        targets_ref = refs.pop(0)
    if keep:
        near_kept_ref, far_kept_ref = refs.pop(0), refs.pop(0)
        upper_kept_ref = refs.pop(0) if last else None
    if last:
        half_refs = refs.pop(0), refs.pop(0)
    total_ref, sums_ref, far_charges_ref, charges_ref = refs[:4]
    if not use:
        near_ref, far_ref = refs[4:]

    coords_at = points + LANES
    blocks = points // LANES
    low_half = in_low_half((LANES, LANES))

    def count(core, row, entry):
        mine, other = (ref[row, entry] for ref in table_refs)
        return jnp.where(core == 0, mine, other)

    def points_of(ref, leaf):
        begin = coords_at + leaf * blocks * dim
        own = [ref[begin + block * dim : begin + (block + 1) * dim, :] for block in range(blocks)]
        return jnp.concatenate(own, axis=1)

    devices = [table_refs[0][2 * LEAVES, spot] for spot in spots]

    if with_targets:
        for leaf in range(LEAVES):
            span = slice(leaf * points, (leaf + 1) * points)
            targets_ref[leaf] = target_rows(points_of(place_refs[0], leaf))
            targets_ref[LEAVES + leaf] = target_rows(sibling_ref[:, span])
    if first:
        total_ref[...] = jnp.zeros_like(total_ref)
        sums_ref[...] = jnp.zeros_like(sums_ref)
    elif last:
        total_ref[...] = total_in_ref[...]
        sums_ref[...] = sums_in_ref[...]

    def added(target, sources_ref, charges, kept_ref):
        if use:
            return matmul(kept_ref[...], charges)
        return kernel_sum(targets_ref[target], sources_ref[...], charges, kept_ref)

    def far_part(skeletons, weights, nodes, kept_ref, kept_at):
        width = len(weights) * LANES
        sources_ref = None
        if not use:
            sources_ref = far_ref.at[:, 0:width]
            put_sources(sources_ref, jnp.concatenate(skeletons, axis=1))

        def step(core, carry):
            for leaf in range(LEAVES):
                target = core * LEAVES + leaf
                for position, (block, node) in enumerate(zip(weights, nodes)):
                    scaled = block * count(core, LEAVES + leaf, node).astype(f32)
                    high = scaled.astype(bf16).astype(f32)
                    rows = pl.ds(position * LANES, LANES)
                    far_charges_ref[leaf, rows, :] = jnp.where(
                        low_half, high, scaled - high
                    ).astype(bf16)
                kept = None
                if kept_ref is not None:
                    kept = kept_ref.at[target, :, kept_at : kept_at + width]
                total_ref[target] += added(
                    target, sources_ref, far_charges_ref[leaf, 0:width], kept
                )
            return carry

        lax.fori_loop(0, CORES, step, 0)

    weights = []
    for position in range(len(spots)):
        rows = charge_refs[position][points : points + LANES, :].astype(f32)
        weights.append(jnp.where(low_half, rows, swapped(rows)))
        sums_ref[devices[position] // BRANCH] += rows
        lane = lax.broadcasted_iota(i32, (1, LANES), 1) // (LANES // LEAVES)
        for leaf in range(LEAVES):
            place = position * LEAVES + leaf
            if not use:
                put_sources(near_ref.at[place], points_of(place_refs[position], leaf))
            chosen = jnp.where(lane == leaf, 1.0, 0.0).astype(bf16)
            charges_ref[place] = charge_refs[position][0:points, :] * chosen

    skeletons_at = coords_at + LEAVES * blocks * dim
    far_part(
        [ref[skeletons_at : skeletons_at + dim, :] for ref in place_refs],
        weights,
        devices,
        far_kept_ref,
        0,
    )
    if last:
        for begin in range(0, n_sub, 2):
            subs = range(begin, min(begin + 2, n_sub))
            skeletons = []
            if not use:
                skeletons = [upper_points_ref[:, sub * LANES : (sub + 1) * LANES] for sub in subs]
            far_part(
                skeletons,
                [jnp.where(low_half, swapped(sums_ref[sub]), sums_ref[sub]) for sub in subs],
                [CORES * n_spots + sub for sub in subs],
                upper_kept_ref,
                begin * LANES,
            )

    def near_part(turn, position, core, leaf):
        device = table_refs[0][2 * LEAVES, spots[0] + position]
        if leaf is None:
            named = sum(count(core, own, device * LEAVES + 1) for own in range(LEAVES))
            leaf = jnp.where(named > 0, 1, 0)
        place = position * LEAVES + leaf
        times = [count(core, own, device * LEAVES + leaf) for own in range(LEAVES)]

        @pl.when(sum(times) > 0)
        def _():
            for own in range(LEAVES):
                target = core * LEAVES + own
                kept = None if near_kept_ref is None else near_kept_ref.at[turn * LEAVES + own]
                sources_ref = None if use else near_ref.at[place]
                total_ref[target] += times[own].astype(f32) * added(
                    target, sources_ref, charges_ref[place], kept
                )

    def near_step(turn, carry):
        if first:
            device = table_refs[0][2 * LEAVES, 0]
            named = sum(count(1, own, device * LEAVES + 1) for own in range(LEAVES))
            other = jnp.where(named > 0, 1, 0)
            near_part(turn, 0, turn // LEAVES, jnp.where(turn < LEAVES, turn, other))
        else:
            near_part(turn, turn // CORES, turn % CORES, None)
        return carry

    lax.fori_loop(0, LEAVES + 1 if first else len(spots) * CORES, near_step, 0)

    if last:
        for core, ref in enumerate(half_refs):
            both = [total_ref[core * LEAVES + leaf] for leaf in range(LEAVES)]
            both = [total + swapped(total) for total in both]
            ref[...] = jnp.where(in_low_half(both[0].shape), both[0], both[1])


def call(body, args, out_shapes, streamed=(), scratch=(), aliases={}, flops=0, vmem_mib=16):
    vmem = pl.BlockSpec(memory_space=pltpu.VMEM)
    specs = []
    for place, arg in enumerate(args):
        if arg.dtype == i32:
            specs.append(pl.BlockSpec(memory_space=pltpu.SMEM))
        elif place in streamed:
            specs.append(pl.BlockSpec(arg.shape, lambda i: (0,) * 2))
        else:
            specs.append(vmem)
    moved = sum(arg.size * arg.dtype.itemsize for arg in args)
    return pl.pallas_call(
        body,
        grid=(1,),
        out_shape=out_shapes,
        in_specs=specs,
        out_specs=[vmem for _ in out_shapes],
        scratch_shapes=list(scratch),
        input_output_aliases=aliases,
        compiler_params=pltpu.CompilerParams(vmem_limit_bytes=vmem_mib * 1024 * 1024),
        cost_estimate=pl.CostEstimate(flops=flops, bytes_accessed=moved, transcendentals=0),
    )(*args)


def ring_order(chips):
    if chips == 8:
        return [0, 2, 4, 6, 7, 5, 3, 1]
    return list(range(chips))


def on_device(
    coords,
    charges,
    near_lists,
    far_lists,
    leaf_interp,
    node_interp,
    upper_interp,
    node_points,
    upper_points,
):
    dim, local = coords.shape
    columns = charges.shape[0]
    points = local // LEAVES
    peers = lax.axis_size("leaf")
    n_sub = peers // BRANCH
    ring = ring_order(peers // CORES)
    chips = len(ring)

    def along(step):
        return [
            (ring[place] * CORES + core, ring[(place + step * (1 - 2 * core)) % chips] * CORES + core)
            for place in range(chips)
            for core in range(CORES)
        ]

    one_way = functools.partial(lax.ppermute, axis_name="leaf", perm=along(1))
    other_way = functools.partial(lax.ppermute, axis_name="leaf", perm=along(-1))
    to_sibling = functools.partial(
        lax.ppermute, axis_name="leaf", perm=[(device, device ^ 1) for device in range(peers)]
    )

    def shape(*extent, dtype=bf16):
        return jax.ShapeDtypeStruct(extent, dtype)

    maps = [leaf_interp, node_interp, upper_interp]
    message, table = call(
        functools.partial(message_kernel, ring),
        [near_lists, far_lists, coords, charges, node_points] + maps,
        [
            shape(points + LANES + LEAVES * points // LANES * dim + dim, LANES),
            shape(8, LANES, dtype=i32),
        ],
        streamed=range(2, 8),
        vmem_mib=60,
    )
    tables = [table, to_sibling(table)]
    sibling_coords = to_sibling(coords)

    total_shape = shape(TARGETS, points, LANES, dtype=f32)
    sums_shape = shape(n_sub, LANES, LANES, dtype=f32)
    half_shape = shape(points, LANES, dtype=f32)
    targets_shape = shape(TARGETS, points, LANES)

    steps = LEAVES + 1 + CORES * (chips - 1)
    kept_bytes = 2 * points * (steps * LEAVES * points + TARGETS * (chips + n_sub) * LANES)
    keeping = kept_bytes <= KEPT_MIB * 2**20

    def stage(places, placed, charged, targets, carried, last, kept):
        first = carried is None
        with_targets = targets is None
        mode = "use" if kept else "keep" if keeping else "make"
        args = tables + ([] if kept else placed) + charged
        if kept:
            args += kept
        elif with_targets:
            args += [sibling_coords]
        else:
            args += [targets]
        carried_at = len(args)
        args += [] if first else list(carried)
        args += [upper_points] if last and not kept else []
        scratch = [
            pltpu.VMEM((LEAVES, 2 * LANES, LANES), bf16),
            pltpu.VMEM((LEAVES * len(places), points, LANES), bf16),
        ]
        if not kept:
            scratch += [
                pltpu.VMEM((LEAVES * len(places), LANES, points), bf16),
                pltpu.VMEM((LANES, 2 * LANES), bf16),
            ]
        outs = [targets_shape] if with_targets else []
        kept_at = len(outs)
        if mode == "keep":
            turns = LEAVES + 1 if first else CORES * len(places)
            outs += [
                shape(turns * LEAVES, points, points),
                shape(TARGETS, points, len(places) * LANES),
            ]
            outs += [shape(TARGETS, points, n_sub * LANES)] if last else []
        kept_to = len(outs)
        aliases = {}
        if last:
            outs += [half_shape, half_shape]
            scratch = [pltpu.VMEM(total_shape.shape, f32), pltpu.VMEM(sums_shape.shape, f32)] + scratch
        else:
            if not first:
                aliases = {carried_at: len(outs), carried_at + 1: len(outs) + 1}
            outs += [total_shape, sums_shape]
        static = (places, chips, n_sub, dim, points, first, last, with_targets, mode)
        results = call(
            functools.partial(stage_kernel, static),
            args,
            outs,
            scratch=scratch,
            aliases=aliases,
            flops=len(places) * (1 if kept else 2) * 10**9,
        )
        if with_targets:
            targets = results[0]
        return targets, list(results[kept_at:kept_to]), results[kept_to:]

    def around(message, placed, targets, kept):
        met = [[message]]
        one = other = message
        for hop in range(1, chips // 2):
            one, other = one_way(one), other_way(other)
            met.append([one, other])
        met.append([one_way(one)])
        placed = met if placed is None else placed
        carried = None
        place = 0
        made = []
        for turn, messages in enumerate(met):
            places = tuple(range(place, place + len(messages)))
            place += len(messages)
            last = turn == len(met) - 1
            given = kept[turn] if kept else []
            targets, values, carried = stage(
                places, placed[turn], messages, targets, carried, last, given
            )
            made.append(values)
        return met, targets, made, carried

    placed, targets, kept, (mine, other) = around(message, None, None, None)
    first, message = call(
        joined_kernel,
        [mine, to_sibling(other)] + maps,
        [shape(columns, local), shape(points + LANES, LANES)],
    )
    *_, (mine, other) = around(message, placed, targets, kept if keeping else None)
    (second,) = call(added_kernel, [mine, to_sibling(other)], [shape(columns, local)])
    return (first, second)


def solution(mesh):
    placed = (
        P(None, ("groups", "leaf")),
        P(None, ("groups", "leaf")),
        P(("groups", "leaf"), None),
        P(("groups", "leaf"), None),
        P(("groups", "leaf"), None),
        P(("groups", "leaf"), None),
        P(("groups", "leaf"), None),
        P(None, ("groups", "leaf")),
        P(None, "groups"),
    )
    return jax.shard_map(
        on_device,
        mesh=mesh,
        in_specs=placed,
        out_specs=(P(None, ("groups", "leaf")), P(None, ("groups", "leaf"))),
        check_vma=False,
    )
```

```python
import functools

import jax
import jax.numpy as jnp
from jax import lax
from jax.experimental import pallas as pl
from jax.experimental.pallas import tpu as pltpu
from jax.sharding import PartitionSpec as P

BRANCH = 16
EXTRA = 16
LANES = 128
CORES = 2
LEAVES = 2
KEPT_MIB = 30

bf16 = jnp.bfloat16
f32 = jnp.float32
i32 = jnp.int32


def matmul(left, right):
    return jnp.dot(left, right, preferred_element_type=f32)


def square_parts(points):
    minus = -jnp.sum(points * points, axis=0, keepdims=True)
    high = minus.astype(bf16).astype(f32)
    rest = minus - high
    middle = rest.astype(bf16).astype(f32)
    low = rest - middle
    return high, middle, low


def extra_rows(parts, first, width):
    row = lax.broadcasted_iota(i32, (EXTRA, width), 0)
    rows = jnp.where(row < 6, 1.0, 0.0).astype(f32)
    for offset, part in enumerate(parts):
        rows = jnp.where(row == first + offset, jnp.broadcast_to(part, (EXTRA, width)), rows)
    return rows


def put_sources(sources_ref, points):
    dim, width = points.shape
    sources_ref[0:dim, :] = points
    parts = square_parts(points.astype(f32))
    sources_ref[dim : dim + EXTRA, :] = extra_rows(parts, 3, width).astype(bf16)
    sources_ref[dim + EXTRA :, :] = jnp.zeros((LANES - dim - EXTRA, width), bf16)


def target_rows(points):
    dim, width = points.shape
    points = points.astype(f32)
    extra = extra_rows(square_parts(points), 0, width)
    blank = jnp.zeros((LANES - dim - EXTRA, width), f32)
    return jnp.concatenate([2.0 * points, extra, blank], axis=0).T.astype(bf16)


def in_low_half(shape):
    return lax.broadcasted_iota(i32, shape, 1) < LANES // 2


def swapped(values):
    return pltpu.roll(values, LANES // 2, 1)


def kernel_values(targets, sources):
    return jnp.exp(matmul(targets, sources)).astype(bf16)


def skeleton_rows(charges, leaf_ref, node_ref, upper_ref):
    points = charges[0].shape[1]
    parts = []
    for leaf, block in enumerate(charges):
        span = slice(leaf * points, (leaf + 1) * points)
        parts.append(matmul(block, leaf_ref[span, :]).astype(bf16))
    weights = matmul(jnp.concatenate(parts, axis=1), node_ref[...]).astype(bf16)
    term = matmul(weights, upper_ref[...])
    return jnp.concatenate([weights.astype(f32), term], axis=0).T.astype(bf16)


def count_rows(ring, near_ref, far_ref):
    shape = (8, LANES)
    row, lane = lax.broadcasted_iota(i32, shape, 0), lax.broadcasted_iota(i32, shape, 1)
    table = jnp.zeros(shape, i32)
    for leaf in range(LEAVES):
        for first, ref in ((0, near_ref), (LEAVES, far_ref)):
            for slot in range(ref.shape[1]):
                hit = (row == first + leaf) & (lane == ref[leaf, slot])
                table = table + jnp.where(hit, 1, 0)
    chips = len(ring)
    me = lax.axis_index("leaf")
    core = me % CORES
    place = jnp.int32(0)
    for at, chip in enumerate(ring):
        place = jnp.where(me // CORES == chip, at, place)
    hop = (lane + 1) // 2
    way = jnp.where(lane % 2 == 1, -1, 1) * (1 - 2 * core)
    met = (place + way * hop + chips) % chips
    device = jnp.zeros(shape, i32)
    for at, chip in enumerate(ring):
        device = jnp.where(met == at, chip * CORES + core, device)
    return jnp.where(row == 2 * LEAVES, device, table)


def message_kernel(
    ring,
    near_ref,
    far_ref,
    coords_ref,
    charges_ref,
    points_ref,
    leaf_ref,
    node_ref,
    upper_ref,
    message_ref,
    table_ref,
):
    dim, local = coords_ref.shape
    half = local // LEAVES
    charges = [charges_ref[:, 0:half], charges_ref[:, half:]]
    message_ref[0:half, :] = jnp.concatenate(charges, axis=0).astype(f32).T.astype(bf16)
    message_ref[half : half + LANES, :] = skeleton_rows(charges, leaf_ref, node_ref, upper_ref)
    place = half + LANES
    for block in range(local // LANES):
        message_ref[place : place + dim, :] = coords_ref[:, block * LANES : (block + 1) * LANES]
        place += dim
    message_ref[place : place + dim, :] = points_ref[...]
    table_ref[...] = count_rows(ring, near_ref, far_ref)


def joined_kernel(mine_ref, other_ref, leaf_ref, node_ref, upper_ref, out_ref, message_ref):
    half = mine_ref.shape[0]
    columns = LANES // LEAVES
    result = mine_ref[...] + other_ref[...]
    message_ref[0:half, :] = result.astype(bf16)
    flat = result.T.astype(bf16)
    charges = [flat[0:columns], flat[columns:]]
    out_ref[...] = jnp.concatenate(charges, axis=1)
    message_ref[half : half + LANES, :] = skeleton_rows(charges, leaf_ref, node_ref, upper_ref)


def added_kernel(mine_ref, other_ref, out_ref):
    columns = LANES // LEAVES
    flat = (mine_ref[...] + other_ref[...]).T.astype(bf16)
    out_ref[...] = jnp.concatenate([flat[0:columns], flat[columns:]], axis=1)


def stage_kernel(stage, *refs):
    spots, n_spots, n_sub, dim, points, first, last, with_targets, mode = stage
    refs = list(refs)
    use, keep = mode == "use", mode == "keep"
    table_refs = refs.pop(0), refs.pop(0)
    place_refs = [] if use else [refs.pop(0) for _ in spots]
    charge_refs = [refs.pop(0) for _ in spots]
    near_kept_ref = far_kept_ref = upper_kept_ref = targets_ref = None
    if use:
        near_kept_ref, far_kept_ref = refs.pop(0), refs.pop(0)
        upper_kept_ref = refs.pop(0) if last else None
    elif with_targets:
        sibling_ref = refs.pop(0)
    else:
        targets_ref = refs.pop(0)
    if not first:
        total_in_ref, sums_in_ref = refs.pop(0), refs.pop(0)
    if last and not use:
        upper_points_ref = refs.pop(0)
    if with_targets:
        targets_ref = refs.pop(0)
    if keep:
        near_kept_ref, far_kept_ref = refs.pop(0), refs.pop(0)
        upper_kept_ref = refs.pop(0) if last else None
    if last:
        half_refs = refs.pop(0), refs.pop(0)
    total_ref, sums_ref, far_charges_ref, charges_ref = refs[:4]
    if not use:
        near_ref, far_ref = refs[4:]

    coords_at = points + LANES
    blocks = points // LANES
    low_half = in_low_half((LANES, LANES))

    def count(core, row, entry):
        mine, other = (ref[row, entry] for ref in table_refs)
        return jnp.where(core == 0, mine, other)

    def points_of(ref, leaf):
        begin = coords_at + leaf * blocks * dim
        own = [ref[begin + block * dim : begin + (block + 1) * dim, :] for block in range(blocks)]
        return jnp.concatenate(own, axis=1)

    devices = [table_refs[0][2 * LEAVES, spot] for spot in spots]

    if with_targets:
        for leaf in range(LEAVES):
            span = slice(leaf * points, (leaf + 1) * points)
            targets_ref[0, span, :] = target_rows(points_of(place_refs[0], leaf))
            targets_ref[1, span, :] = target_rows(sibling_ref[:, span])
    if first:
        total_ref[...] = jnp.zeros_like(total_ref)
        sums_ref[...] = jnp.zeros_like(sums_ref)

    def values(core, sources_ref, kept_ref):
        if use:
            return kept_ref[...]
        made = kernel_values(targets_ref[core], sources_ref[...])
        if kept_ref is not None:
            kept_ref[...] = made
        return made

    def far_part(skeletons, weights, nodes, kept_ref, kept_at):
        width = len(weights) * LANES
        sources_ref = None
        if not use:
            sources_ref = far_ref.at[:, 0:width]
            put_sources(sources_ref, jnp.concatenate(skeletons, axis=1))

        def step(core, carry):
            kept = None
            if kept_ref is not None:
                kept = kept_ref.at[core, :, kept_at : kept_at + width]
            kernel = values(core, sources_ref, kept)
            for leaf in range(LEAVES):
                for position, (block, node) in enumerate(zip(weights, nodes)):
                    scaled = block * count(core, LEAVES + leaf, node).astype(f32)
                    high = scaled.astype(bf16).astype(f32)
                    rows = pl.ds(position * LANES, LANES)
                    far_charges_ref[leaf, rows, :] = jnp.where(
                        low_half, high, scaled - high
                    ).astype(bf16)
                span = slice(leaf * points, (leaf + 1) * points)
                total_ref[core, span, :] += matmul(
                    kernel[span], far_charges_ref[leaf, 0:width]
                )
            return carry

        lax.fori_loop(0, CORES, step, 0)

    weights = []
    for position in range(len(spots)):
        rows = charge_refs[position][points : points + LANES, :].astype(f32)
        weights.append(jnp.where(low_half, rows, swapped(rows)))
        sums_ref[devices[position] // BRANCH] += rows
        lane = lax.broadcasted_iota(i32, (1, LANES), 1) // (LANES // LEAVES)
        for leaf in range(LEAVES):
            place = position * LEAVES + leaf
            if not use:
                put_sources(near_ref.at[place], points_of(place_refs[position], leaf))
            chosen = jnp.where(lane == leaf, 1.0, 0.0).astype(bf16)
            charges_ref[place] = charge_refs[position][0:points, :] * chosen

    skeletons_at = coords_at + LEAVES * blocks * dim
    far_part(
        [ref[skeletons_at : skeletons_at + dim, :] for ref in place_refs],
        weights,
        devices,
        far_kept_ref,
        0,
    )
    if last:
        for begin in range(0, n_sub, 2):
            subs = range(begin, min(begin + 2, n_sub))
            skeletons = []
            if not use:
                skeletons = [upper_points_ref[:, sub * LANES : (sub + 1) * LANES] for sub in subs]
            far_part(
                skeletons,
                [jnp.where(low_half, swapped(sums_ref[sub]), sums_ref[sub]) for sub in subs],
                [CORES * n_spots + sub for sub in subs],
                upper_kept_ref,
                begin * LANES,
            )

    def near_part(turn, position, core, leaf):
        device = table_refs[0][2 * LEAVES, spots[0] + position]
        if leaf is None:
            named = sum(count(core, own, device * LEAVES + 1) for own in range(LEAVES))
            leaf = jnp.where(named > 0, 1, 0)
        place = position * LEAVES + leaf
        times = [count(core, own, device * LEAVES + leaf) for own in range(LEAVES)]

        @pl.when(sum(times) > 0)
        def _():
            kept = None if near_kept_ref is None else near_kept_ref.at[turn]
            kernel = values(core, None if use else near_ref.at[place], kept)
            added = matmul(kernel, charges_ref[place])
            for own in range(LEAVES):
                span = slice(own * points, (own + 1) * points)
                total_ref[core, span, :] += times[own].astype(f32) * added[span]

    def near_step(turn, carry):
        if first:
            device = table_refs[0][2 * LEAVES, 0]
            named = sum(count(1, own, device * LEAVES + 1) for own in range(LEAVES))
            other = jnp.where(named > 0, 1, 0)
            near_part(turn, 0, turn // LEAVES, jnp.where(turn < LEAVES, turn, other))
        else:
            near_part(turn, turn // CORES, turn % CORES, None)
        return carry

    lax.fori_loop(0, LEAVES + 1 if first else len(spots) * CORES, near_step, 0)

    if last:
        for core, ref in enumerate(half_refs):
            both = [
                total_ref[core, leaf * points : (leaf + 1) * points, :] for leaf in range(LEAVES)
            ]
            both = [total + swapped(total) for total in both]
            ref[...] = jnp.where(in_low_half(both[0].shape), both[0], both[1])


def call(body, args, out_shapes, streamed=(), scratch=(), aliases={}, flops=0, vmem_mib=16):
    vmem = pl.BlockSpec(memory_space=pltpu.VMEM)
    specs = []
    for place, arg in enumerate(args):
        if arg.dtype == i32:
            specs.append(pl.BlockSpec(memory_space=pltpu.SMEM))
        elif place in streamed:
            specs.append(pl.BlockSpec(arg.shape, lambda i: (0,) * 2))
        else:
            specs.append(vmem)
    moved = sum(arg.size * arg.dtype.itemsize for arg in args)
    return pl.pallas_call(
        body,
        grid=(1,),
        out_shape=out_shapes,
        in_specs=specs,
        out_specs=[vmem for _ in out_shapes],
        scratch_shapes=list(scratch),
        input_output_aliases=aliases,
        compiler_params=pltpu.CompilerParams(vmem_limit_bytes=vmem_mib * 1024 * 1024),
        cost_estimate=pl.CostEstimate(flops=flops, bytes_accessed=moved, transcendentals=0),
    )(*args)


def ring_order(chips):
    if chips == 8:
        return [0, 2, 4, 6, 7, 5, 3, 1]
    return list(range(chips))


def on_device(
    coords,
    charges,
    near_lists,
    far_lists,
    leaf_interp,
    node_interp,
    upper_interp,
    node_points,
    upper_points,
):
    dim, local = coords.shape
    columns = charges.shape[0]
    points = local // LEAVES
    peers = lax.axis_size("leaf")
    n_sub = peers // BRANCH
    ring = ring_order(peers // CORES)
    chips = len(ring)

    def along(step):
        return [
            (ring[place] * CORES + core, ring[(place + step * (1 - 2 * core)) % chips] * CORES + core)
            for place in range(chips)
            for core in range(CORES)
        ]

    one_way = functools.partial(lax.ppermute, axis_name="leaf", perm=along(1))
    other_way = functools.partial(lax.ppermute, axis_name="leaf", perm=along(-1))
    to_sibling = functools.partial(
        lax.ppermute, axis_name="leaf", perm=[(device, device ^ 1) for device in range(peers)]
    )

    def shape(*extent, dtype=bf16):
        return jax.ShapeDtypeStruct(extent, dtype)

    maps = [leaf_interp, node_interp, upper_interp]
    message, table = call(
        functools.partial(message_kernel, ring),
        [near_lists, far_lists, coords, charges, node_points] + maps,
        [
            shape(points + LANES + LEAVES * points // LANES * dim + dim, LANES),
            shape(8, LANES, dtype=i32),
        ],
        streamed=range(2, 8),
        vmem_mib=60,
    )
    tables = [table, to_sibling(table)]
    sibling_coords = to_sibling(coords)

    total_shape = shape(CORES, local, LANES, dtype=f32)
    sums_shape = shape(n_sub, LANES, LANES, dtype=f32)
    half_shape = shape(points, LANES, dtype=f32)
    targets_shape = shape(CORES, local, LANES)

    steps = LEAVES + 1 + CORES * (chips - 1)
    kept_bytes = 2 * points * (steps * local + CORES * LEAVES * (chips + n_sub) * LANES)
    keeping = kept_bytes <= KEPT_MIB * 2**20

    def stage(places, placed, charged, targets, carried, last, kept):
        first = carried is None
        with_targets = targets is None
        mode = "use" if kept else "keep" if keeping else "make"
        args = tables + ([] if kept else placed) + charged
        if kept:
            args += kept
        elif with_targets:
            args += [sibling_coords]
        else:
            args += [targets]
        carried_at = len(args)
        args += [] if first else list(carried)
        args += [upper_points] if last and not kept else []
        scratch = [
            pltpu.VMEM((LEAVES, 2 * LANES, LANES), bf16),
            pltpu.VMEM((LEAVES * len(places), points, LANES), bf16),
        ]
        if not kept:
            scratch += [
                pltpu.VMEM((LEAVES * len(places), LANES, points), bf16),
                pltpu.VMEM((LANES, 2 * LANES), bf16),
            ]
        outs = [targets_shape] if with_targets else []
        kept_at = len(outs)
        if mode == "keep":
            turns = LEAVES + 1 if first else CORES * len(places)
            outs += [
                shape(turns, local, points),
                shape(CORES, local, len(places) * LANES),
            ]
            outs += [shape(CORES, local, n_sub * LANES)] if last else []
        kept_to = len(outs)
        outs += [half_shape, half_shape] if last else []
        aliases = {} if first else {carried_at + k: len(outs) + k for k in range(2)}
        outs += [total_shape, sums_shape]
        static = (places, chips, n_sub, dim, points, first, last, with_targets, mode)
        results = call(
            functools.partial(stage_kernel, static),
            args,
            outs,
            scratch=scratch,
            aliases=aliases,
            flops=len(places) * (1 if kept else 2) * 10**9,
        )
        if with_targets:
            targets = results[0]
        return targets, list(results[kept_at:kept_to]), results[kept_to : kept_to + 2]

    def around(message, placed, targets, kept):
        met = [[message]]
        one = other = message
        for hop in range(1, chips // 2):
            one, other = one_way(one), other_way(other)
            met.append([one, other])
        met.append([one_way(one)])
        placed = met if placed is None else placed
        carried = None
        place = 0
        made = []
        for turn, messages in enumerate(met):
            places = tuple(range(place, place + len(messages)))
            place += len(messages)
            last = turn == len(met) - 1
            given = kept[turn] if kept else []
            targets, values, carried = stage(
                places, placed[turn], messages, targets, carried, last, given
            )
            made.append(values)
        return met, targets, made, carried

    placed, targets, kept, (mine, other) = around(message, None, None, None)
    first, message = call(
        joined_kernel,
        [mine, to_sibling(other)] + maps,
        [shape(columns, local), shape(points + LANES, LANES)],
    )
    *_, (mine, other) = around(message, placed, targets, kept if keeping else None)
    (second,) = call(added_kernel, [mine, to_sibling(other)], [shape(columns, local)])
    return (first, second)


def solution(mesh):
    placed = (
        P(None, ("groups", "leaf")),
        P(None, ("groups", "leaf")),
        P(("groups", "leaf"), None),
        P(("groups", "leaf"), None),
        P(("groups", "leaf"), None),
        P(("groups", "leaf"), None),
        P(("groups", "leaf"), None),
        P(None, ("groups", "leaf")),
        P(None, "groups"),
    )
    return jax.shard_map(
        on_device,
        mesh=mesh,
        in_specs=placed,
        out_specs=(P(None, ("groups", "leaf")), P(None, ("groups", "leaf"))),
        check_vma=False,
    )
```

```python
import functools

import jax
import jax.numpy as jnp
from jax import lax
from jax.experimental import pallas as pl
from jax.experimental.pallas import tpu as pltpu
from jax.sharding import PartitionSpec as P

BRANCH = 16
EXTRA = 16
LANES = 128
CORES = 2
LEAVES = 2
KEPT_MIB = 30

bf16 = jnp.bfloat16
f32 = jnp.float32
i32 = jnp.int32


def matmul(left, right):
    return jnp.dot(left, right, preferred_element_type=f32)


def square_parts(points):
    minus = -jnp.sum(points * points, axis=0, keepdims=True)
    high = minus.astype(bf16).astype(f32)
    rest = minus - high
    middle = rest.astype(bf16).astype(f32)
    low = rest - middle
    return high, middle, low


def extra_rows(parts, first, width):
    row = lax.broadcasted_iota(i32, (EXTRA, width), 0)
    rows = jnp.where(row < 6, 1.0, 0.0).astype(f32)
    for offset, part in enumerate(parts):
        rows = jnp.where(row == first + offset, jnp.broadcast_to(part, (EXTRA, width)), rows)
    return rows


def put_sources(sources_ref, points):
    dim, width = points.shape
    sources_ref[0:dim, :] = points
    parts = square_parts(points.astype(f32))
    sources_ref[dim : dim + EXTRA, :] = extra_rows(parts, 3, width).astype(bf16)
    sources_ref[dim + EXTRA :, :] = jnp.zeros((LANES - dim - EXTRA, width), bf16)


def target_rows(points):
    dim, width = points.shape
    points = points.astype(f32)
    extra = extra_rows(square_parts(points), 0, width)
    blank = jnp.zeros((LANES - dim - EXTRA, width), f32)
    return jnp.concatenate([2.0 * points, extra, blank], axis=0).T.astype(bf16)


def in_low_half(shape):
    return lax.broadcasted_iota(i32, shape, 1) < LANES // 2


def swapped(values):
    return pltpu.roll(values, LANES // 2, 1)


def kernel_values(targets, sources):
    return jnp.exp(matmul(targets, sources)).astype(bf16)


def skeleton_rows(charges, leaf_ref, node_ref, upper_ref):
    points = charges[0].shape[1]
    parts = []
    for leaf, block in enumerate(charges):
        span = slice(leaf * points, (leaf + 1) * points)
        parts.append(matmul(block, leaf_ref[span, :]).astype(bf16))
    weights = matmul(jnp.concatenate(parts, axis=1), node_ref[...]).astype(bf16)
    term = matmul(weights, upper_ref[...])
    return jnp.concatenate([weights.astype(f32), term], axis=0).T.astype(bf16)


def ring_offset(lane):
    pair = (lane - 2) // 2
    far = pair + 1 + lane % 2
    return jnp.where(lane < 2, lane, jnp.where(pair % 2 == 0, -far, far))


def count_rows(ring, near_ref, far_ref):
    shape = (8, LANES)
    row, lane = lax.broadcasted_iota(i32, shape, 0), lax.broadcasted_iota(i32, shape, 1)
    table = jnp.zeros(shape, i32)
    for leaf in range(LEAVES):
        for first, ref in ((0, near_ref), (LEAVES, far_ref)):
            for slot in range(ref.shape[1]):
                hit = (row == first + leaf) & (lane == ref[leaf, slot])
                table = table + jnp.where(hit, 1, 0)
    chips = len(ring)
    me = lax.axis_index("leaf")
    core = me % CORES
    place = jnp.int32(0)
    for at, chip in enumerate(ring):
        place = jnp.where(me // CORES == chip, at, place)
    sense = jnp.where(place % 2 == core, 1, -1)
    met = (place + sense * ring_offset(lane) + 2 * LANES * chips) % chips
    device = jnp.zeros(shape, i32)
    for at, chip in enumerate(ring):
        device = jnp.where(met == at, chip * CORES + core, device)
    return jnp.where(row == 2 * LEAVES, device, table)


def message_kernel(
    ring,
    near_ref,
    far_ref,
    coords_ref,
    charges_ref,
    points_ref,
    leaf_ref,
    node_ref,
    upper_ref,
    place_ref,
    message_ref,
    table_ref,
    charges_buf,
    leaf_buf,
    node_buf,
    upper_buf,
    sems,
):
    dim, local = charges_ref.shape
    half = local // LEAVES
    copies = [
        pltpu.make_async_copy(source, target, sems.at[k])
        for k, (source, target) in enumerate(
            [
                (charges_ref, charges_buf),
                (leaf_ref, leaf_buf),
                (node_ref, node_buf),
                (upper_ref, upper_buf),
                (coords_ref, place_ref.at[0]),
                (points_ref, message_ref.at[0, half + LANES : half + LANES + dim, :]),
            ]
        )
    ]
    for copy in copies:
        copy.start()
    table_ref[...] = count_rows(ring, near_ref, far_ref)
    copies[0].wait()
    charges = [charges_buf[:, 0:half], charges_buf[:, half:]]
    message_ref[0, 0:half, :] = jnp.concatenate(charges, axis=0).astype(f32).T.astype(bf16)
    for copy in copies[1:4]:
        copy.wait()
    message_ref[0, half : half + LANES, :] = skeleton_rows(charges, leaf_buf, node_buf, upper_buf)
    for copy in copies[4:]:
        copy.wait()


def joined_kernel(mine_ref, other_ref, leaf_ref, node_ref, upper_ref, out_ref, message_ref):
    half = mine_ref.shape[0]
    columns = LANES // LEAVES
    result = mine_ref[...] + other_ref[...]
    message_ref[0, 0:half, :] = result.astype(bf16)
    flat = result.T.astype(bf16)
    charges = [flat[0:columns], flat[columns:]]
    out_ref[...] = jnp.concatenate(charges, axis=1)
    message_ref[0, half : half + LANES, :] = skeleton_rows(charges, leaf_ref, node_ref, upper_ref)


def added_kernel(mine_ref, other_ref, out_ref):
    columns = LANES // LEAVES
    flat = (mine_ref[...] + other_ref[...]).T.astype(bf16)
    out_ref[...] = jnp.concatenate([flat[0:columns], flat[columns:]], axis=1)


def stage_kernel(stage, *refs):
    spots, n_spots, n_sub, dim, points, first, last, near, far = stage
    refs = list(refs)
    makes_near, makes_far = near != "use", far in ("make", "keep")
    table_refs = refs.pop(0), refs.pop(0)
    place_ref = refs.pop(0) if makes_near else None
    skeleton_ref = refs.pop(0) if makes_far else None
    charge_ref = refs.pop(0) if near != "only" else None
    near_kept_ref = far_kept_ref = upper_kept_ref = targets_ref = None
    if near == "use":
        near_kept_ref = refs.pop(0)
    if far == "use":
        far_kept_ref = refs.pop(0)
        upper_kept_ref = refs.pop(0) if last else None
    sibling_ref = refs.pop(0) if first and makes_near else None
    if (makes_near or makes_far) and not first:
        targets_ref = refs.pop(0)
    if not first and near != "only":
        refs.pop(0), refs.pop(0)
    upper_points_ref = refs.pop(0) if last and makes_far else None
    if sibling_ref is not None:
        targets_ref = refs.pop(0)
    if near in ("keep", "only"):
        near_kept_ref = refs.pop(0)
    if far == "keep":
        far_kept_ref = refs.pop(0)
        upper_kept_ref = refs.pop(0) if last else None
    if last and near != "only":
        half_refs = refs.pop(0), refs.pop(0)
    if near != "only":
        total_ref, sums_ref, far_charges_ref, charges_ref = (refs.pop(0) for _ in range(4))
    near_ref = refs.pop(0) if makes_near else None
    far_ref = refs.pop(0) if makes_far else None

    low_half = in_low_half((LANES, LANES))
    devices = [table_refs[0][2 * LEAVES, spot] for spot in spots]

    def count(core, row, entry):
        mine, other = (ref[row, entry] for ref in table_refs)
        return jnp.where(core == 0, mine, other)

    def span_of(leaf):
        return slice(leaf * points, (leaf + 1) * points)

    if sibling_ref is not None:
        for leaf in range(LEAVES):
            targets_ref[0, span_of(leaf), :] = target_rows(place_ref[0, :, span_of(leaf)])
            targets_ref[1, span_of(leaf), :] = target_rows(sibling_ref[:, span_of(leaf)])
    if first:
        total_ref[...] = jnp.zeros_like(total_ref)
        sums_ref[...] = jnp.zeros_like(sums_ref)

    def values(makes, core, sources_ref, kept_ref):
        if not makes:
            return kept_ref[...]
        made = kernel_values(targets_ref[core], sources_ref[...])
        if kept_ref is not None:
            kept_ref[...] = made
        return made

    def far_part(skeletons, weights, nodes, kept_ref, kept_at):
        width = len(weights) * LANES
        sources_ref = None
        if makes_far:
            sources_ref = far_ref.at[:, 0:width]
            put_sources(sources_ref, jnp.concatenate(skeletons, axis=1))

        def step(core, carry):
            kept = None
            if kept_ref is not None:
                kept = kept_ref.at[core, :, kept_at : kept_at + width]
            kernel = values(makes_far, core, sources_ref, kept)
            for leaf in range(LEAVES):
                for position, (block, node) in enumerate(zip(weights, nodes)):
                    scaled = block * count(core, LEAVES + leaf, node).astype(f32)
                    high = scaled.astype(bf16).astype(f32)
                    rows = pl.ds(position * LANES, LANES)
                    far_charges_ref[leaf, rows, :] = jnp.where(
                        low_half, high, scaled - high
                    ).astype(bf16)
                total_ref[core, span_of(leaf), :] += matmul(
                    kernel[span_of(leaf)], far_charges_ref[leaf, 0:width]
                )
            return carry

        lax.fori_loop(0, CORES, step, 0)

    def skeletons_of(position):
        begin = points + LANES
        return skeleton_ref[position, begin : begin + dim, :]

    weights = []
    for position in range(len(spots)):
        if near != "only":
            rows = charge_ref[position, points : points + LANES, :].astype(f32)
            weights.append(jnp.where(low_half, rows, swapped(rows)))
            sums_ref[devices[position] // BRANCH] += rows
        lane = lax.broadcasted_iota(i32, (1, LANES), 1) // (LANES // LEAVES)
        for leaf in range(LEAVES):
            place = position * LEAVES + leaf
            if makes_near:
                put_sources(near_ref.at[place], place_ref[position, :, span_of(leaf)])
            if near != "only":
                chosen = jnp.where(lane == leaf, 1.0, 0.0).astype(bf16)
                charges_ref[place] = charge_ref[position, 0:points, :] * chosen

    if near != "only":
        far_part(
            [skeletons_of(position) for position in range(len(spots))] if makes_far else [],
            weights,
            devices,
            far_kept_ref,
            0,
        )
    if last and near != "only":
        for begin in range(0, n_sub, 2):
            subs = range(begin, min(begin + 2, n_sub))
            skeletons = []
            if makes_far:
                skeletons = [upper_points_ref[:, sub * LANES : (sub + 1) * LANES] for sub in subs]
            far_part(
                skeletons,
                [jnp.where(low_half, swapped(sums_ref[sub]), sums_ref[sub]) for sub in subs],
                [CORES * n_spots + sub for sub in subs],
                upper_kept_ref,
                begin * LANES,
            )

    def near_part(turn, position, core, leaf):
        device = table_refs[0][2 * LEAVES, spots[0] + position]
        if leaf is None:
            named = sum(count(core, own, device * LEAVES + 1) for own in range(LEAVES))
            leaf = jnp.where(named > 0, 1, 0)
        place = position * LEAVES + leaf
        times = [count(core, own, device * LEAVES + leaf) for own in range(LEAVES)]

        @pl.when(sum(times) > 0)
        def _():
            kept = None if near_kept_ref is None else near_kept_ref.at[turn]
            kernel = values(makes_near, core, near_ref.at[place] if makes_near else None, kept)
            if near != "only":
                added = matmul(kernel, charges_ref[place])
                for own in range(LEAVES):
                    total_ref[core, span_of(own), :] += times[own].astype(f32) * added[span_of(own)]

    def near_step(turn, carry):
        if first:
            device = table_refs[0][2 * LEAVES, 0]
            named = sum(count(1, own, device * LEAVES + 1) for own in range(LEAVES))
            other = jnp.where(named > 0, 1, 0)
            near_part(turn, 0, turn // LEAVES, jnp.where(turn < LEAVES, turn, other))
        else:
            near_part(turn, turn // CORES, turn % CORES, None)
        return carry

    lax.fori_loop(0, LEAVES + 1 if first else len(spots) * CORES, near_step, 0)

    if last and near != "only":
        for core, ref in enumerate(half_refs):
            both = [total_ref[core, span_of(leaf), :] for leaf in range(LEAVES)]
            both = [total + swapped(total) for total in both]
            ref[...] = jnp.where(in_low_half(both[0].shape), both[0], both[1])


def call(body, args, out_shapes, scratch=(), aliases={}, flops=0, in_hbm=False):
    vmem = pl.BlockSpec(memory_space=pltpu.VMEM)
    hbm = pl.BlockSpec(memory_space=pltpu.HBM)
    smem = pl.BlockSpec(memory_space=pltpu.SMEM)
    moved = sum(arg.size * arg.dtype.itemsize for arg in args)
    return pl.pallas_call(
        body,
        out_shape=out_shapes,
        in_specs=[smem if arg.dtype == i32 else hbm if in_hbm else vmem for arg in args],
        out_specs=[vmem for _ in out_shapes],
        scratch_shapes=list(scratch),
        input_output_aliases=aliases,
        compiler_params=pltpu.CompilerParams(vmem_limit_bytes=16 * 1024 * 1024),
        cost_estimate=pl.CostEstimate(flops=flops, bytes_accessed=moved, transcendentals=0),
    )(*args)


def ring_order(chips):
    if chips == 8:
        return [0, 2, 4, 6, 7, 5, 3, 1]
    return list(range(chips))


def on_device(
    coords,
    charges,
    near_lists,
    far_lists,
    leaf_interp,
    node_interp,
    upper_interp,
    node_points,
    upper_points,
):
    dim, local = coords.shape
    columns = charges.shape[0]
    points = local // LEAVES
    peers = lax.axis_size("leaf")
    n_sub = peers // BRANCH
    ring = ring_order(peers // CORES)
    chips = len(ring)

    def swap(turn):
        pairs = []
        for place, chip in enumerate(ring):
            for core in range(CORES):
                step = 1 if (place + core + turn) % 2 == 0 else -1
                pairs.append((chip * CORES + core, ring[(place + step) % chips] * CORES + core))
        return functools.partial(lax.ppermute, axis_name="leaf", perm=pairs)

    def gathered(message):
        met = [message, swap(0)(message)]
        sent = jnp.concatenate(met, axis=0)
        for turn in range(1, chips // 2):
            sent = swap(turn)(sent)
            met.append(sent)
        return met

    to_sibling = functools.partial(
        lax.ppermute, axis_name="leaf", perm=[(device, device ^ 1) for device in range(peers)]
    )

    def shape(*extent, dtype=bf16):
        return jax.ShapeDtypeStruct(extent, dtype)

    maps = [leaf_interp, node_interp, upper_interp]
    place, message, table = call(
        functools.partial(message_kernel, ring),
        [near_lists, far_lists, coords, charges, node_points] + maps,
        [
            shape(1, dim, local),
            shape(1, points + LANES + dim, LANES),
            shape(8, LANES, dtype=i32),
        ],
        scratch=[pltpu.VMEM(arg.shape, bf16) for arg in [charges] + maps]
        + [pltpu.SemaphoreType.DMA((6,))],
        in_hbm=True,
    )
    sibling_coords = to_sibling(coords)
    partner = swap(0)(coords)[None]
    tables = [table, to_sibling(table)]

    total_shape = shape(CORES, local, LANES, dtype=f32)
    sums_shape = shape(n_sub, LANES, LANES, dtype=f32)
    half_shape = shape(points, LANES, dtype=f32)
    targets_shape = shape(CORES, local, LANES)

    steps = LEAVES + 1 + CORES * (chips - 1)
    kept_bytes = 2 * points * (steps * local + CORES * LEAVES * (chips + n_sub) * LANES)
    keeping = kept_bytes <= KEPT_MIB * 2**20

    def stage(spots, near, far, places, skeletons, charged, targets, carried, last, kept):
        first = spots[0] == 0
        adds = near != "only"
        makes_near, makes_far = near != "use", far in ("make", "keep")
        makes_targets = first and makes_near
        args = list(tables)
        args += [places] if makes_near else []
        args += [skeletons] if makes_far else []
        args += [charged] if adds else []
        args += kept
        args += [sibling_coords] if makes_targets else []
        args += [targets] if (makes_near or makes_far) and not first else []
        carried_at = len(args)
        args += carried if not first and adds else []
        args += [upper_points] if last and makes_far else []
        scratch = []
        if adds:
            scratch += [
                pltpu.VMEM((LEAVES, 2 * LANES, LANES), bf16),
                pltpu.VMEM((LEAVES * len(spots), points, LANES), bf16),
            ]
        scratch += [pltpu.VMEM((LEAVES * len(spots), LANES, points), bf16)] if makes_near else []
        scratch += [pltpu.VMEM((LANES, 2 * LANES), bf16)] if makes_far else []
        outs = [targets_shape] if makes_targets else []
        near_at = len(outs)
        if near in ("keep", "only"):
            outs.append(shape(LEAVES + 1 if first else CORES * len(spots), local, points))
        far_at = len(outs)
        if far == "keep":
            outs.append(shape(CORES, local, len(spots) * LANES))
            outs += [shape(CORES, local, n_sub * LANES)] if last else []
        carried_to = len(outs)
        aliases = {}
        if adds:
            outs += [half_shape, half_shape] if last else []
            aliases = {} if first else {carried_at + k: len(outs) + k for k in range(2)}
            outs += [total_shape, sums_shape]
        static = (spots, chips, n_sub, dim, points, first, last, near, far)
        results = call(
            functools.partial(stage_kernel, static),
            args,
            outs,
            scratch=scratch,
            aliases=aliases,
            flops=len(spots) * (2 if makes_near else 1) * 10**9,
        )
        targets = results[0] if makes_targets else targets
        carried = results[carried_to : carried_to + 2]
        return targets, results[near_at:far_at], results[far_at:carried_to], carried

    def around(places, skeletons, charged, targets, kept):
        carried = []
        made = []
        spots = (0,)
        for turn, messages in enumerate(charged):
            last = turn == len(charged) - 1
            given = list(kept[turn][0]) + list(kept[turn][1]) if kept else []
            near = far = "use" if kept else "keep" if keeping else "make"
            near_values = []
            if last and near == "keep":
                _, near_values, _, _ = stage(
                    spots, "only", "none", places[turn], None, None, targets, carried, last, []
                )
                near, given = "use", list(near_values)
            targets, more_near, far_values, carried = stage(
                spots, near, far, places[turn], skeletons[turn], messages, targets, carried, last, given
            )
            made.append((list(near_values) + list(more_near), far_values))
            count = min(2, spots[-1] + 1)
            spots = tuple(range(spots[-1] + 1, spots[-1] + 1 + count))
        return targets, made, carried

    places = [place, partner]
    sent = jnp.concatenate(places, axis=0)
    for turn in range(1, chips // 2):
        sent = swap(turn)(sent)
        places.append(sent)
    charged = gathered(message)
    targets, kept, (mine, other) = around(places, charged, charged, None, None)
    first, message = call(
        joined_kernel,
        [mine, to_sibling(other)] + maps,
        [shape(columns, local), shape(1, points + LANES, LANES)],
    )
    again = gathered(message)
    *_, (mine, other) = around(places, charged, again, targets, kept if keeping else None)
    (second,) = call(added_kernel, [mine, to_sibling(other)], [shape(columns, local)])
    return (first, second)


def solution(mesh):
    placed = (
        P(None, ("groups", "leaf")),
        P(None, ("groups", "leaf")),
        P(("groups", "leaf"), None),
        P(("groups", "leaf"), None),
        P(("groups", "leaf"), None),
        P(("groups", "leaf"), None),
        P(("groups", "leaf"), None),
        P(None, ("groups", "leaf")),
        P(None, "groups"),
    )
    return jax.shard_map(
        on_device,
        mesh=mesh,
        in_specs=placed,
        out_specs=(P(None, ("groups", "leaf")), P(None, ("groups", "leaf"))),
        check_vma=False,
    )
```

```python
import functools

import jax
import jax.numpy as jnp
from jax import lax
from jax.experimental import pallas as pl
from jax.experimental.pallas import tpu as pltpu
from jax.sharding import PartitionSpec as P

BRANCH = 16
EXTRA = 16
LANES = 128
CORES = 2
LEAVES = 2
KEPT_MIB = 30

bf16 = jnp.bfloat16
f32 = jnp.float32
i32 = jnp.int32


def matmul(left, right):
    return jnp.dot(left, right, preferred_element_type=f32)


def square_parts(points):
    minus = -jnp.sum(points * points, axis=0, keepdims=True)
    high = minus.astype(bf16).astype(f32)
    rest = minus - high
    middle = rest.astype(bf16).astype(f32)
    low = rest - middle
    return high, middle, low


def extra_rows(parts, first, width):
    row = lax.broadcasted_iota(i32, (EXTRA, width), 0)
    rows = jnp.where(row < 6, 1.0, 0.0).astype(f32)
    for offset, part in enumerate(parts):
        rows = jnp.where(row == first + offset, jnp.broadcast_to(part, (EXTRA, width)), rows)
    return rows


def put_sources(sources_ref, points):
    dim, width = points.shape
    sources_ref[0:dim, :] = points
    parts = square_parts(points.astype(f32))
    sources_ref[dim : dim + EXTRA, :] = extra_rows(parts, 3, width).astype(bf16)
    sources_ref[dim + EXTRA :, :] = jnp.zeros((LANES - dim - EXTRA, width), bf16)


def target_rows(points):
    dim, width = points.shape
    points = points.astype(f32)
    extra = extra_rows(square_parts(points), 0, width)
    blank = jnp.zeros((LANES - dim - EXTRA, width), f32)
    return jnp.concatenate([2.0 * points, extra, blank], axis=0).T.astype(bf16)


def in_low_half(shape):
    return lax.broadcasted_iota(i32, shape, 1) < LANES // 2


def swapped(values):
    return pltpu.roll(values, LANES // 2, 1)


def kernel_values(targets, sources):
    return jnp.exp(matmul(targets, sources)).astype(bf16)


def skeleton_rows(charges, leaf_ref, node_ref, upper_ref):
    points = charges[0].shape[1]
    parts = []
    for leaf, block in enumerate(charges):
        span = slice(leaf * points, (leaf + 1) * points)
        parts.append(matmul(block, leaf_ref[span, :]).astype(bf16))
    weights = matmul(jnp.concatenate(parts, axis=1), node_ref[...]).astype(bf16)
    term = matmul(weights, upper_ref[...])
    return jnp.concatenate([weights.astype(f32), term], axis=0).T.astype(bf16)


def count_rows(near_ref, far_ref):
    shape = (8, LANES)
    row, lane = lax.broadcasted_iota(i32, shape, 0), lax.broadcasted_iota(i32, shape, 1)
    table = jnp.zeros(shape, f32)
    for leaf in range(LEAVES):
        for first, ref in ((0, near_ref), (LEAVES, far_ref)):
            for slot in range(ref.shape[1]):
                hit = (row == first + leaf) & (lane == ref[leaf, slot])
                table = table + jnp.where(hit, 1.0, 0.0)
    return table


def device_of(ring, spot):
    chips = len(ring)
    me = lax.axis_index("leaf")
    core = me % CORES
    place = jnp.int32(0)
    for at, chip in enumerate(ring):
        place = jnp.where(me // CORES == chip, at, place)
    hop = (spot + 1) // 2
    step = hop if spot % 2 == 0 else -hop
    met = (place + step * (1 - 2 * core) + chips) % chips
    device = jnp.int32(0)
    for at, chip in enumerate(ring):
        device = jnp.where(met == at, chip * CORES + core, device)
    return device


def message_kernel(
    near_ref,
    far_ref,
    coords_ref,
    charges_ref,
    points_ref,
    leaf_ref,
    node_ref,
    upper_ref,
    message_ref,
    table_ref,
):
    dim, local = coords_ref.shape
    half = local // LEAVES
    charges = [charges_ref[:, 0:half], charges_ref[:, half:]]
    message_ref[0:half, :] = jnp.concatenate(charges, axis=0).astype(f32).T.astype(bf16)
    message_ref[half : half + LANES, :] = skeleton_rows(charges, leaf_ref, node_ref, upper_ref)
    place = half + LANES
    for block in range(local // LANES):
        message_ref[place : place + dim, :] = coords_ref[:, block * LANES : (block + 1) * LANES]
        place += dim
    message_ref[place : place + dim, :] = points_ref[...]
    table_ref[...] = count_rows(near_ref, far_ref)


def joined_kernel(mine_ref, other_ref, leaf_ref, node_ref, upper_ref, out_ref, message_ref):
    half = mine_ref.shape[0]
    columns = LANES // LEAVES
    result = mine_ref[...] + other_ref[...]
    message_ref[0:half, :] = result.astype(bf16)
    flat = result.T.astype(bf16)
    charges = [flat[0:columns], flat[columns:]]
    out_ref[...] = jnp.concatenate(charges, axis=1)
    message_ref[half : half + LANES, :] = skeleton_rows(charges, leaf_ref, node_ref, upper_ref)


def added_kernel(mine_ref, other_ref, out_ref):
    columns = LANES // LEAVES
    flat = (mine_ref[...] + other_ref[...]).T.astype(bf16)
    out_ref[...] = jnp.concatenate([flat[0:columns], flat[columns:]], axis=1)


def stage_kernel(stage, *refs):
    ring, spots, far_of, n_sub, dim, points, first, last, mode = stage
    refs = list(refs)
    use, keep = mode == "use", mode == "keep"
    table_refs = refs.pop(0), refs.pop(0)
    place_refs = [] if use else [refs.pop(0) for _ in spots]
    charge_refs = [refs.pop(0) for _ in spots]
    near_kept_ref = far_kept_ref = targets_ref = None
    has_far = bool(far_of)
    if use:
        near_kept_ref = refs.pop(0)
        far_kept_ref = refs.pop(0) if has_far else None
    elif first:
        sibling_ref = refs.pop(0)
    else:
        targets_ref = refs.pop(0)
    if not first:
        refs.pop(0), refs.pop(0)
    upper_points_ref = refs.pop(0) if last and not use else None
    if first and not use:
        targets_ref = refs.pop(0)
    if keep:
        near_kept_ref = refs.pop(0)
        far_kept_ref = refs.pop(0) if has_far else None
    if last:
        half_refs = refs.pop(0), refs.pop(0)
    total_ref, sums_ref, far_charges_ref, charges_ref = refs[:4]
    if not use:
        near_ref, far_ref = refs[4:]

    coords_at = points + LANES
    blocks = points // LANES
    skeletons_at = coords_at + LEAVES * blocks * dim
    low_half = in_low_half((LANES, LANES))
    lane = lax.broadcasted_iota(i32, (8, LANES), 1)

    def span_of(leaf):
        return slice(leaf * points, (leaf + 1) * points)

    def points_of(leaf):
        begin = coords_at + leaf * blocks * dim
        ref = place_refs[-1]
        own = [ref[begin + block * dim : begin + (block + 1) * dim, :] for block in range(blocks)]
        return jnp.concatenate(own, axis=1)

    if first and not use:
        for leaf in range(LEAVES):
            targets_ref[0, span_of(leaf), :] = target_rows(points_of(leaf))
            targets_ref[1, span_of(leaf), :] = target_rows(sibling_ref[:, span_of(leaf)])
    if first:
        total_ref[...] = jnp.zeros_like(total_ref)
        sums_ref[...] = jnp.zeros_like(sums_ref)

    def table_of(core):
        mine, other = (ref[...] for ref in table_refs)
        return jnp.where(core == 0, mine, other)

    def picked(table, entry):
        return jnp.sum(jnp.where(lane == entry, table, 0.0), axis=1, keepdims=True)

    def values(core, sources_ref, kept_ref):
        if use:
            return kept_ref[...]
        made = kernel_values(targets_ref[core], sources_ref[...])
        if kept_ref is not None:
            kept_ref[...] = made
        return made

    device = device_of(ring, spots[-1])

    def near_part(turn, core, leaf):
        table = table_of(core)
        named = [picked(table, device * LEAVES + which)[0:LEAVES] for which in range(LEAVES)]
        if leaf is None:
            second = jnp.where(jnp.sum(named[1], axis=0, keepdims=True) > 0.0, 1.0, 0.0)
        else:
            second = jnp.full((1, 1), float(leaf), f32)
        times = named[0] * (1.0 - second) + named[1] * second
        if not use:
            chosen = points_of(0) * (1.0 - second).astype(bf16) + points_of(1) * second.astype(bf16)
            put_sources(near_ref, chosen)
        half = jnp.where(lane[0:1] < LANES // LEAVES, 1.0 - second, second).astype(bf16)
        charges_ref[...] = charge_refs[-1][0:points, :] * half
        kept = None if near_kept_ref is None else near_kept_ref.at[turn]
        added = matmul(values(core, None if use else near_ref, kept), charges_ref[...])
        return [times[own : own + 1] * added[span_of(own)] for own in range(LEAVES)]

    weights = []
    skeletons = []
    for at in far_of:
        rows = charge_refs[at][points : points + LANES, :].astype(f32)
        node = device_of(ring, spots[at])
        weights.append((jnp.where(low_half, rows, swapped(rows)), node))
        sums_ref[node // BRANCH] += rows
        if not use:
            skeletons.append(place_refs[at][skeletons_at : skeletons_at + dim, :])
    if last:
        for sub in range(n_sub):
            rows = sums_ref[sub]
            weights.append((jnp.where(low_half, swapped(rows), rows), len(ring) * CORES + sub))
            if not use:
                skeletons.append(upper_points_ref[:, sub * LANES : (sub + 1) * LANES])
    if has_far and not use:
        put_sources(far_ref, jnp.concatenate(skeletons, axis=1))

    def far_part(core):
        table = table_of(core)
        kernel = values(
            core,
            None if use else far_ref,
            None if far_kept_ref is None else far_kept_ref.at[core],
        )
        added = []
        for own in range(LEAVES):
            for position, (block, node) in enumerate(weights):
                scaled = block * picked(table, node)[LEAVES + own : LEAVES + own + 1]
                high = scaled.astype(bf16).astype(f32)
                rows = slice(position * LANES, (position + 1) * LANES)
                far_charges_ref[own, rows, :] = jnp.where(low_half, high, scaled - high).astype(bf16)
            added.append(matmul(kernel[span_of(own)], far_charges_ref[own]))
        return added

    def add(core, parts):
        for own in range(LEAVES):
            total = total_ref[core, span_of(own), :]
            for part in parts:
                total = total + part[own]
            total_ref[core, span_of(own), :] = total

    if first:
        for leaf in range(LEAVES):
            add(0, [near_part(leaf, 0, leaf)])
        add(1, [near_part(LEAVES, 1, None), far_part(1)])
    else:

        def step(core, carry):
            parts = [near_part(core, core, None)]
            add(core, parts + ([far_part(core)] if has_far else []))
            return carry

        lax.fori_loop(0, CORES, step, 0)

    if last:
        for core, ref in enumerate(half_refs):
            both = [total_ref[core, span_of(leaf), :] for leaf in range(LEAVES)]
            both = [total + swapped(total) for total in both]
            ref[...] = jnp.where(in_low_half(both[0].shape), both[0], both[1])


def gate_kernel(message_ref, after_ref, out_ref):
    pass


def gated(message, after):
    anywhere = pl.BlockSpec(memory_space=pl.ANY)
    return pl.pallas_call(
        gate_kernel,
        out_shape=jax.ShapeDtypeStruct(message.shape, message.dtype),
        in_specs=[anywhere] * 2,
        out_specs=anywhere,
        input_output_aliases={0: 0},
    )(message, after)


def call(body, args, out_shapes, streamed=(), scratch=(), aliases={}, flops=0, vmem_mib=16):
    vmem = pl.BlockSpec(memory_space=pltpu.VMEM)
    specs = []
    for place, arg in enumerate(args):
        if arg.dtype == i32:
            specs.append(pl.BlockSpec(memory_space=pltpu.SMEM))
        elif place in streamed:
            specs.append(pl.BlockSpec(arg.shape, lambda i: (0,) * 2))
        else:
            specs.append(vmem)
    moved = sum(arg.size * arg.dtype.itemsize for arg in args)
    return pl.pallas_call(
        body,
        grid=(1,),
        out_shape=out_shapes,
        in_specs=specs,
        out_specs=[vmem for _ in out_shapes],
        scratch_shapes=list(scratch),
        input_output_aliases=aliases,
        compiler_params=pltpu.CompilerParams(vmem_limit_bytes=vmem_mib * 1024 * 1024),
        cost_estimate=pl.CostEstimate(flops=flops, bytes_accessed=moved, transcendentals=0),
    )(*args)


def ring_order(chips):
    if chips == 8:
        return [0, 2, 4, 6, 7, 5, 3, 1]
    return list(range(chips))


def on_device(
    coords,
    charges,
    near_lists,
    far_lists,
    leaf_interp,
    node_interp,
    upper_interp,
    node_points,
    upper_points,
):
    dim, local = coords.shape
    columns = charges.shape[0]
    points = local // LEAVES
    peers = lax.axis_size("leaf")
    n_sub = peers // BRANCH
    ring = ring_order(peers // CORES)
    chips = len(ring)

    def along(step):
        return [
            (ring[place] * CORES + core, ring[(place + step * (1 - 2 * core)) % chips] * CORES + core)
            for place in range(chips)
            for core in range(CORES)
        ]

    one_way = functools.partial(lax.ppermute, axis_name="leaf", perm=along(1))
    other_way = functools.partial(lax.ppermute, axis_name="leaf", perm=along(-1))
    to_sibling = functools.partial(
        lax.ppermute, axis_name="leaf", perm=[(device, device ^ 1) for device in range(peers)]
    )

    def shape(*extent, dtype=bf16):
        return jax.ShapeDtypeStruct(extent, dtype)

    maps = [leaf_interp, node_interp, upper_interp]
    message, table = call(
        message_kernel,
        [near_lists, far_lists, coords, charges, node_points] + maps,
        [
            shape(points + LANES + LEAVES * points // LANES * dim + dim, LANES),
            shape(8, LANES, dtype=f32),
        ],
        streamed=range(2, 8),
        vmem_mib=60,
    )
    tables = [table, to_sibling(table)]
    sibling_coords = to_sibling(coords)

    total_shape = shape(CORES, local, LANES, dtype=f32)
    sums_shape = shape(n_sub, LANES, LANES, dtype=f32)
    half_shape = shape(points, LANES, dtype=f32)
    targets_shape = shape(CORES, local, LANES)

    steps = LEAVES + 1 + CORES * (chips - 1)
    kept_bytes = 2 * points * (steps * local + CORES * LEAVES * (chips + n_sub) * LANES)
    keeping = kept_bytes <= KEPT_MIB * 2**20

    def stage(spots, far_of, placed, charged, targets, carried, last, kept):
        first = not carried
        mode = "use" if kept else "keep" if keeping else "make"
        args = tables + ([] if kept else placed) + charged
        if kept:
            args += kept
        else:
            args += [sibling_coords] if first else [targets]
        carried_at = len(args)
        args += carried
        args += [upper_points] if last and not kept else []
        far_width = LANES * (len(far_of) + (n_sub if last else 0))
        scratch = [
            pltpu.VMEM((LEAVES, max(far_width, LANES), LANES), bf16),
            pltpu.VMEM((points, LANES), bf16),
        ]
        if not kept:
            scratch += [
                pltpu.VMEM((LANES, points), bf16),
                pltpu.VMEM((LANES, max(far_width, LANES)), bf16),
            ]
        outs = [targets_shape] if first and not kept else []
        kept_at = len(outs)
        if mode == "keep":
            outs.append(shape(LEAVES + 1 if first else CORES, local, points))
            outs += [shape(CORES, local, far_width)] if far_of else []
        kept_to = len(outs)
        outs += [half_shape, half_shape] if last else []
        aliases = {carried_at + k: len(outs) + k for k in range(len(carried))}
        outs += [total_shape, sums_shape]
        static = (ring, spots, far_of, n_sub, dim, points, first, last, mode)
        results = call(
            functools.partial(stage_kernel, static),
            args,
            outs,
            scratch=scratch,
            aliases=aliases,
            flops=(1 if kept else 2) * 10**9,
        )
        targets = results[0] if first and not kept else targets
        return targets, list(results[kept_at:kept_to]), list(results[kept_to : kept_to + 2])

    def around(message, placed, targets, kept):
        met = []
        made = []
        carried = []

        def arrived(message):
            nonlocal targets, carried
            met.append(message)
            spot = len(met) - 1
            last = spot == chips - 1
            spots = (spot - 1, spot) if spot % 2 == 0 and spot > 0 else (spot,)
            far_of = () if spot % 2 == 1 and not last else tuple(range(len(spots)))
            charged = [met[at] for at in spots]
            targets, values, carried = stage(
                spots,
                far_of,
                [placed[at] for at in spots] if placed else charged,
                charged,
                targets,
                carried,
                last,
                kept[spot] if kept else [],
            )
            made.append(values)

        one, other = one_way(message), other_way(message)
        arrived(message)
        for hop in range(1, chips // 2):
            one_next = one_way(one)
            arrived(one)
            other_next = None
            if hop < chips // 2 - 1:
                other = gated(other, carried[1])
                other_next = other_way(other)
            arrived(other)
            one, other = one_next, other_next
        arrived(one)
        placed = met if placed is None else placed
        return placed, targets, made, carried

    placed, targets, kept, (mine, other) = around(message, None, None, None)
    first, message = call(
        joined_kernel,
        [mine, to_sibling(other)] + maps,
        [shape(columns, local), shape(points + LANES, LANES)],
    )
    *_, (mine, other) = around(message, placed, targets, kept if keeping else None)
    (second,) = call(added_kernel, [mine, to_sibling(other)], [shape(columns, local)])
    return (first, second)


def solution(mesh):
    placed = (
        P(None, ("groups", "leaf")),
        P(None, ("groups", "leaf")),
        P(("groups", "leaf"), None),
        P(("groups", "leaf"), None),
        P(("groups", "leaf"), None),
        P(("groups", "leaf"), None),
        P(("groups", "leaf"), None),
        P(None, ("groups", "leaf")),
        P(None, "groups"),
    )
    return jax.shard_map(
        on_device,
        mesh=mesh,
        in_specs=placed,
        out_specs=(P(None, ("groups", "leaf")), P(None, ("groups", "leaf"))),
        check_vma=False,
    )
```

```python
import functools

import jax
import jax.numpy as jnp
from jax import lax
from jax.experimental import pallas as pl
from jax.experimental.pallas import tpu as pltpu
from jax.sharding import PartitionSpec as P

BRANCH = 16
EXTRA = 16
LANES = 128
CORES = 2
LEAVES = 2
KEPT_MIB = 30

bf16 = jnp.bfloat16
f32 = jnp.float32
i32 = jnp.int32


def matmul(left, right):
    return jnp.dot(left, right, preferred_element_type=f32)


def square_parts(points):
    minus = -jnp.sum(points * points, axis=0, keepdims=True)
    high = minus.astype(bf16).astype(f32)
    rest = minus - high
    middle = rest.astype(bf16).astype(f32)
    low = rest - middle
    return high, middle, low


def extra_rows(parts, first, width):
    row = lax.broadcasted_iota(i32, (EXTRA, width), 0)
    rows = jnp.where(row < 6, 1.0, 0.0).astype(f32)
    for offset, part in enumerate(parts):
        rows = jnp.where(row == first + offset, jnp.broadcast_to(part, (EXTRA, width)), rows)
    return rows


def put_sources(sources_ref, points):
    dim, width = points.shape
    sources_ref[0:dim, :] = points
    parts = square_parts(points.astype(f32))
    sources_ref[dim : dim + EXTRA, :] = extra_rows(parts, 3, width).astype(bf16)
    sources_ref[dim + EXTRA :, :] = jnp.zeros((LANES - dim - EXTRA, width), bf16)


def target_rows(points):
    dim, width = points.shape
    points = points.astype(f32)
    extra = extra_rows(square_parts(points), 0, width)
    blank = jnp.zeros((LANES - dim - EXTRA, width), f32)
    return jnp.concatenate([2.0 * points, extra, blank], axis=0).T.astype(bf16)


def in_low_half(shape):
    return lax.broadcasted_iota(i32, shape, 1) < LANES // 2


def swapped(values):
    return pltpu.roll(values, LANES // 2, 1)


def kernel_values(targets, sources):
    return jnp.exp(matmul(targets, sources)).astype(bf16)


def skeleton_rows(charges, leaf_ref, node_ref, upper_ref):
    points = charges[0].shape[1]
    parts = []
    for leaf, block in enumerate(charges):
        span = slice(leaf * points, (leaf + 1) * points)
        parts.append(matmul(block, leaf_ref[span, :]).astype(bf16))
    weights = matmul(jnp.concatenate(parts, axis=1), node_ref[...]).astype(bf16)
    term = matmul(weights, upper_ref[...])
    return jnp.concatenate([weights.astype(f32), term], axis=0).T.astype(bf16)


def count_rows(near_ref, far_ref):
    shape = (8, LANES)
    row, lane = lax.broadcasted_iota(i32, shape, 0), lax.broadcasted_iota(i32, shape, 1)
    table = jnp.zeros(shape, f32)
    for leaf in range(LEAVES):
        for first, ref in ((0, near_ref), (LEAVES, far_ref)):
            for slot in range(ref.shape[1]):
                hit = (row == first + leaf) & (lane == ref[leaf, slot])
                table = table + jnp.where(hit, 1.0, 0.0)
    return table


def device_of(ring, spot):
    chips = len(ring)
    me = lax.axis_index("leaf")
    core = me % CORES
    place = jnp.int32(0)
    for at, chip in enumerate(ring):
        place = jnp.where(me // CORES == chip, at, place)
    hop = (spot + 1) // 2
    step = hop if spot % 2 == 0 else -hop
    met = (place + step * (1 - 2 * core) + chips) % chips
    device = jnp.int32(0)
    for at, chip in enumerate(ring):
        device = jnp.where(met == at, chip * CORES + core, device)
    return device


def message_kernel(
    near_ref,
    far_ref,
    coords_ref,
    charges_ref,
    points_ref,
    leaf_ref,
    node_ref,
    upper_ref,
    message_ref,
    table_ref,
):
    dim, local = coords_ref.shape
    half = local // LEAVES
    charges = [charges_ref[:, 0:half], charges_ref[:, half:]]
    message_ref[0:half, :] = jnp.concatenate(charges, axis=0).astype(f32).T.astype(bf16)
    message_ref[half : half + LANES, :] = skeleton_rows(charges, leaf_ref, node_ref, upper_ref)
    place = half + LANES
    for block in range(local // LANES):
        message_ref[place : place + dim, :] = coords_ref[:, block * LANES : (block + 1) * LANES]
        place += dim
    message_ref[place : place + dim, :] = points_ref[...]
    table_ref[...] = count_rows(near_ref, far_ref)


def joined_kernel(mine_ref, other_ref, leaf_ref, node_ref, upper_ref, out_ref, message_ref):
    half = mine_ref.shape[0]
    columns = LANES // LEAVES
    result = mine_ref[...] + other_ref[...]
    message_ref[0:half, :] = result.astype(bf16)
    flat = result.T.astype(bf16)
    charges = [flat[0:columns], flat[columns:]]
    out_ref[...] = jnp.concatenate(charges, axis=1)
    message_ref[half : half + LANES, :] = skeleton_rows(charges, leaf_ref, node_ref, upper_ref)


def added_kernel(mine_ref, other_ref, out_ref):
    columns = LANES // LEAVES
    flat = (mine_ref[...] + other_ref[...]).T.astype(bf16)
    out_ref[...] = jnp.concatenate([flat[0:columns], flat[columns:]], axis=1)


def stage_kernel(stage, *refs):
    ring, spots, far_of, n_sub, dim, points, first, last, mode = stage
    refs = list(refs)
    use, keep = mode == "use", mode == "keep"
    table_refs = refs.pop(0), refs.pop(0)
    place_refs = [] if use else [refs.pop(0) for _ in spots]
    charge_refs = [refs.pop(0) for _ in spots]
    near_kept_ref = far_kept_ref = targets_ref = None
    has_far = bool(far_of)
    if use:
        near_kept_ref = refs.pop(0)
        far_kept_ref = refs.pop(0) if has_far else None
    elif first:
        sibling_ref = refs.pop(0)
    else:
        targets_ref = refs.pop(0)
    if not first:
        refs.pop(0), refs.pop(0)
    upper_points_ref = refs.pop(0) if last and not use else None
    if first and not use:
        targets_ref = refs.pop(0)
    if keep:
        near_kept_ref = refs.pop(0)
        far_kept_ref = refs.pop(0) if has_far else None
    if last:
        half_refs = refs.pop(0), refs.pop(0)
    total_ref, sums_ref, far_charges_ref, charges_ref = refs[:4]
    if not use:
        near_ref, far_ref = refs[4:]

    coords_at = points + LANES
    blocks = points // LANES
    skeletons_at = coords_at + LEAVES * blocks * dim
    low_half = in_low_half((LANES, LANES))
    lane = lax.broadcasted_iota(i32, (8, LANES), 1)

    def span_of(leaf):
        return slice(leaf * points, (leaf + 1) * points)

    def points_of(leaf):
        begin = coords_at + leaf * blocks * dim
        ref = place_refs[-1]
        own = [ref[begin + block * dim : begin + (block + 1) * dim, :] for block in range(blocks)]
        return jnp.concatenate(own, axis=1)

    if first and not use:
        for leaf in range(LEAVES):
            targets_ref[0, span_of(leaf), :] = target_rows(points_of(leaf))
            targets_ref[1, span_of(leaf), :] = target_rows(sibling_ref[:, span_of(leaf)])
    if first:
        total_ref[...] = jnp.zeros_like(total_ref)
        sums_ref[...] = jnp.zeros_like(sums_ref)

    def table_of(core):
        mine, other = (ref[...] for ref in table_refs)
        return jnp.where(core == 0, mine, other)

    def picked(table, entry):
        return jnp.sum(jnp.where(lane == entry, table, 0.0), axis=1, keepdims=True)

    def values(core, sources_ref, kept_ref):
        if use:
            return kept_ref[...]
        made = kernel_values(targets_ref[core], sources_ref[...])
        if kept_ref is not None:
            kept_ref[...] = made
        return made

    device = device_of(ring, spots[-1])

    def near_part(turn, core, leaf):
        table = table_of(core)
        named = [picked(table, device * LEAVES + which)[0:LEAVES] for which in range(LEAVES)]
        if leaf is None:
            second = jnp.where(jnp.sum(named[1], axis=0, keepdims=True) > 0.0, 1.0, 0.0)
        else:
            second = jnp.full((1, 1), float(leaf), f32)
        times = named[0] * (1.0 - second) + named[1] * second
        if not use:
            chosen = points_of(0) * (1.0 - second).astype(bf16) + points_of(1) * second.astype(bf16)
            put_sources(near_ref, chosen)
        half = jnp.where(lane[0:1] < LANES // LEAVES, 1.0 - second, second).astype(bf16)
        charges_ref[...] = charge_refs[-1][0:points, :] * half
        kept = None if near_kept_ref is None else near_kept_ref.at[turn]
        added = matmul(values(core, None if use else near_ref, kept), charges_ref[...])
        return [times[own : own + 1] * added[span_of(own)] for own in range(LEAVES)]

    weights = []
    skeletons = []
    for at in far_of:
        rows = charge_refs[at][points : points + LANES, :].astype(f32)
        node = device_of(ring, spots[at])
        weights.append((jnp.where(low_half, rows, swapped(rows)), node))
        sums_ref[node // BRANCH] += rows
        if not use:
            skeletons.append(place_refs[at][skeletons_at : skeletons_at + dim, :])
    if last:
        for sub in range(n_sub):
            rows = sums_ref[sub]
            weights.append((jnp.where(low_half, swapped(rows), rows), len(ring) * CORES + sub))
            if not use:
                skeletons.append(upper_points_ref[:, sub * LANES : (sub + 1) * LANES])
    if has_far and not use:
        put_sources(far_ref, jnp.concatenate(skeletons, axis=1))

    def far_part(core):
        table = table_of(core)
        kernel = values(
            core,
            None if use else far_ref,
            None if far_kept_ref is None else far_kept_ref.at[core],
        )
        added = []
        for own in range(LEAVES):
            for position, (block, node) in enumerate(weights):
                scaled = block * picked(table, node)[LEAVES + own : LEAVES + own + 1]
                high = scaled.astype(bf16).astype(f32)
                rows = slice(position * LANES, (position + 1) * LANES)
                far_charges_ref[own, rows, :] = jnp.where(low_half, high, scaled - high).astype(bf16)
            added.append(matmul(kernel[span_of(own)], far_charges_ref[own]))
        return added

    def add(core, parts):
        for own in range(LEAVES):
            total = total_ref[core, span_of(own), :]
            for part in parts:
                total = total + part[own]
            total_ref[core, span_of(own), :] = total

    if first:
        for leaf in range(LEAVES):
            add(0, [near_part(leaf, 0, leaf)])
        add(1, [near_part(LEAVES, 1, None), far_part(1)])
    else:

        def step(core, carry):
            parts = [near_part(core, core, None)]
            add(core, parts + ([far_part(core)] if has_far else []))
            return carry

        lax.fori_loop(0, CORES, step, 0)

    if last:
        for core, ref in enumerate(half_refs):
            both = [total_ref[core, span_of(leaf), :] for leaf in range(LEAVES)]
            both = [total + swapped(total) for total in both]
            ref[...] = jnp.where(in_low_half(both[0].shape), both[0], both[1])


def gate_kernel(message_ref, after_ref, out_ref):
    pass


def gated(message, after):
    anywhere = pl.BlockSpec(memory_space=pl.ANY)
    return pl.pallas_call(
        gate_kernel,
        out_shape=jax.ShapeDtypeStruct(message.shape, message.dtype),
        in_specs=[anywhere] * 2,
        out_specs=anywhere,
        input_output_aliases={0: 0},
        compiler_params=pltpu.CompilerParams(vmem_limit_bytes=2**20),
    )(message, after)


def call(body, args, out_shapes, streamed=(), scratch=(), aliases={}, flops=0, vmem_mib=16):
    vmem = pl.BlockSpec(memory_space=pltpu.VMEM)
    specs = []
    for place, arg in enumerate(args):
        if arg.dtype == i32:
            specs.append(pl.BlockSpec(memory_space=pltpu.SMEM))
        elif place in streamed:
            specs.append(pl.BlockSpec(arg.shape, lambda i: (0,) * 2))
        else:
            specs.append(vmem)
    moved = sum(arg.size * arg.dtype.itemsize for arg in args)
    return pl.pallas_call(
        body,
        grid=(1,),
        out_shape=out_shapes,
        in_specs=specs,
        out_specs=[vmem for _ in out_shapes],
        scratch_shapes=list(scratch),
        input_output_aliases=aliases,
        compiler_params=pltpu.CompilerParams(vmem_limit_bytes=vmem_mib * 1024 * 1024),
        cost_estimate=pl.CostEstimate(flops=flops, bytes_accessed=moved, transcendentals=0),
    )(*args)


def ring_order(chips):
    if chips == 8:
        return [0, 2, 4, 6, 7, 5, 3, 1]
    return list(range(chips))


def on_device(
    coords,
    charges,
    near_lists,
    far_lists,
    leaf_interp,
    node_interp,
    upper_interp,
    node_points,
    upper_points,
):
    dim, local = coords.shape
    columns = charges.shape[0]
    points = local // LEAVES
    peers = lax.axis_size("leaf")
    n_sub = peers // BRANCH
    ring = ring_order(peers // CORES)
    chips = len(ring)

    def along(step):
        return [
            (ring[place] * CORES + core, ring[(place + step * (1 - 2 * core)) % chips] * CORES + core)
            for place in range(chips)
            for core in range(CORES)
        ]

    one_way = functools.partial(lax.ppermute, axis_name="leaf", perm=along(1))
    other_way = functools.partial(lax.ppermute, axis_name="leaf", perm=along(-1))
    to_sibling = functools.partial(
        lax.ppermute, axis_name="leaf", perm=[(device, device ^ 1) for device in range(peers)]
    )

    def shape(*extent, dtype=bf16):
        return jax.ShapeDtypeStruct(extent, dtype)

    maps = [leaf_interp, node_interp, upper_interp]
    message, table = call(
        message_kernel,
        [near_lists, far_lists, coords, charges, node_points] + maps,
        [
            shape(points + LANES + LEAVES * points // LANES * dim + dim, LANES),
            shape(8, LANES, dtype=f32),
        ],
        streamed=range(2, 8),
        vmem_mib=60,
    )
    tables = [table, to_sibling(table)]
    sibling_coords = to_sibling(coords)

    total_shape = shape(CORES, local, LANES, dtype=f32)
    sums_shape = shape(n_sub, LANES, LANES, dtype=f32)
    half_shape = shape(points, LANES, dtype=f32)
    targets_shape = shape(CORES, local, LANES)

    steps = LEAVES + 1 + CORES * (chips - 1)
    kept_bytes = 2 * points * (steps * local + CORES * LEAVES * (chips + n_sub) * LANES)
    keeping = kept_bytes <= KEPT_MIB * 2**20

    def stage(spots, far_of, placed, charged, targets, carried, last, kept):
        first = not carried
        mode = "use" if kept else "keep" if keeping else "make"
        args = tables + ([] if kept else placed) + charged
        if kept:
            args += kept
        else:
            args += [sibling_coords] if first else [targets]
        carried_at = len(args)
        args += carried
        args += [upper_points] if last and not kept else []
        far_width = LANES * (len(far_of) + (n_sub if last else 0))
        scratch = [
            pltpu.VMEM((LEAVES, max(far_width, LANES), LANES), bf16),
            pltpu.VMEM((points, LANES), bf16),
        ]
        if not kept:
            scratch += [
                pltpu.VMEM((LANES, points), bf16),
                pltpu.VMEM((LANES, max(far_width, LANES)), bf16),
            ]
        outs = [targets_shape] if first and not kept else []
        kept_at = len(outs)
        if mode == "keep":
            outs.append(shape(LEAVES + 1 if first else CORES, local, points))
            outs += [shape(CORES, local, far_width)] if far_of else []
        kept_to = len(outs)
        outs += [half_shape, half_shape] if last else []
        aliases = {carried_at + k: len(outs) + k for k in range(len(carried))}
        outs += [total_shape, sums_shape]
        static = (ring, spots, far_of, n_sub, dim, points, first, last, mode)
        results = call(
            functools.partial(stage_kernel, static),
            args,
            outs,
            scratch=scratch,
            aliases=aliases,
            flops=(1 if kept else 2) * 10**9,
        )
        targets = results[0] if first and not kept else targets
        return targets, list(results[kept_at:kept_to]), list(results[kept_to : kept_to + 2])

    def around(message, placed, targets, kept):
        met = []
        made = []
        carried = []

        def arrived(message):
            nonlocal targets, carried
            met.append(message)
            spot = len(met) - 1
            last = spot == chips - 1
            spots = (spot - 1, spot) if spot % 2 == 0 and spot > 0 else (spot,)
            far_of = () if spot % 2 == 1 and not last else tuple(range(len(spots)))
            charged = [met[at] for at in spots]
            targets, values, carried = stage(
                spots,
                far_of,
                [placed[at] for at in spots] if placed else charged,
                charged,
                targets,
                carried,
                last,
                kept[spot] if kept else [],
            )
            made.append(values)

        one, other = one_way(message), other_way(message)
        arrived(message)
        for hop in range(1, chips // 2):
            one_next = one_way(one)
            arrived(one)
            other_next = None
            if hop < chips // 2 - 1:
                other = gated(other, carried[1])
                other_next = other_way(other)
            arrived(other)
            one, other = one_next, other_next
        arrived(one)
        placed = met if placed is None else placed
        return placed, targets, made, carried

    placed, targets, kept, (mine, other) = around(message, None, None, None)
    first, message = call(
        joined_kernel,
        [mine, to_sibling(other)] + maps,
        [shape(columns, local), shape(points + LANES, LANES)],
    )
    *_, (mine, other) = around(message, placed, targets, kept if keeping else None)
    (second,) = call(added_kernel, [mine, to_sibling(other)], [shape(columns, local)])
    return (first, second)


def solution(mesh):
    placed = (
        P(None, ("groups", "leaf")),
        P(None, ("groups", "leaf")),
        P(("groups", "leaf"), None),
        P(("groups", "leaf"), None),
        P(("groups", "leaf"), None),
        P(("groups", "leaf"), None),
        P(("groups", "leaf"), None),
        P(None, ("groups", "leaf")),
        P(None, "groups"),
    )
    return jax.shard_map(
        on_device,
        mesh=mesh,
        in_specs=placed,
        out_specs=(P(None, ("groups", "leaf")), P(None, ("groups", "leaf"))),
        check_vma=False,
    )
```

```python
import functools

import jax
import jax.numpy as jnp
from jax import lax
from jax.experimental import pallas as pl
from jax.experimental.pallas import tpu as pltpu
from jax.sharding import PartitionSpec as P

BRANCH = 16
EXTRA = 16
LANES = 128
CORES = 2
LEAVES = 2
KEPT_MIB = 30

bf16 = jnp.bfloat16
f32 = jnp.float32
i32 = jnp.int32


def matmul(left, right):
    return jnp.dot(left, right, preferred_element_type=f32)


def square_parts(points):
    minus = -jnp.sum(points * points, axis=0, keepdims=True)
    high = minus.astype(bf16).astype(f32)
    rest = minus - high
    middle = rest.astype(bf16).astype(f32)
    low = rest - middle
    return high, middle, low


def extra_rows(parts, first, width):
    row = lax.broadcasted_iota(i32, (EXTRA, width), 0)
    rows = jnp.where(row < 6, 1.0, 0.0).astype(f32)
    for offset, part in enumerate(parts):
        rows = jnp.where(row == first + offset, jnp.broadcast_to(part, (EXTRA, width)), rows)
    return rows


def put_sources(sources_ref, points):
    dim, width = points.shape
    sources_ref[0:dim, :] = points
    parts = square_parts(points.astype(f32))
    sources_ref[dim : dim + EXTRA, :] = extra_rows(parts, 3, width).astype(bf16)
    sources_ref[dim + EXTRA :, :] = jnp.zeros((LANES - dim - EXTRA, width), bf16)


def target_rows(points):
    dim, width = points.shape
    points = points.astype(f32)
    extra = extra_rows(square_parts(points), 0, width)
    blank = jnp.zeros((LANES - dim - EXTRA, width), f32)
    return jnp.concatenate([2.0 * points, extra, blank], axis=0).T.astype(bf16)


def in_low_half(shape):
    return lax.broadcasted_iota(i32, shape, 1) < LANES // 2


def swapped(values):
    return pltpu.roll(values, LANES // 2, 1)


def kernel_values(targets, sources):
    return jnp.exp(matmul(targets, sources)).astype(bf16)


def skeleton_rows(charges, leaf_ref, node_ref, upper_ref):
    points = charges[0].shape[1]
    parts = []
    for leaf, block in enumerate(charges):
        span = slice(leaf * points, (leaf + 1) * points)
        parts.append(matmul(block, leaf_ref[span, :]).astype(bf16))
    weights = matmul(jnp.concatenate(parts, axis=1), node_ref[...]).astype(bf16)
    term = matmul(weights, upper_ref[...])
    return jnp.concatenate([weights.astype(f32), term], axis=0).T.astype(bf16)


def count_rows(near_ref, far_ref):
    shape = (8, LANES)
    row, lane = lax.broadcasted_iota(i32, shape, 0), lax.broadcasted_iota(i32, shape, 1)
    table = jnp.zeros(shape, f32)
    for leaf in range(LEAVES):
        for first, ref in ((0, near_ref), (LEAVES, far_ref)):
            for slot in range(ref.shape[1]):
                hit = (row == first + leaf) & (lane == ref[leaf, slot])
                table = table + jnp.where(hit, 1.0, 0.0)
    return table


def device_of(ring, spot):
    chips = len(ring)
    me = lax.axis_index("leaf")
    core = me % CORES
    place = jnp.int32(0)
    for at, chip in enumerate(ring):
        place = jnp.where(me // CORES == chip, at, place)
    hop = (spot + 1) // 2
    step = hop if spot % 2 == 0 else -hop
    met = (place + step * (1 - 2 * core) + chips) % chips
    device = jnp.int32(0)
    for at, chip in enumerate(ring):
        device = jnp.where(met == at, chip * CORES + core, device)
    return device


def message_kernel(
    near_ref,
    far_ref,
    coords_ref,
    charges_ref,
    points_ref,
    leaf_ref,
    node_ref,
    upper_ref,
    message_ref,
    local_ref,
    table_ref,
):
    dim, local = coords_ref.shape
    half = local // LEAVES
    charges = [charges_ref[:, 0:half], charges_ref[:, half:]]
    sent = [
        jnp.concatenate(charges, axis=0).astype(f32).T.astype(bf16),
        skeleton_rows(charges, leaf_ref, node_ref, upper_ref),
        points_ref[...],
    ]
    place = 0
    for part in sent:
        rows = slice(place, place + part.shape[0])
        message_ref[rows, :] = part
        local_ref[rows, :] = part
        place += part.shape[0]
    for block in range(local // LANES):
        local_ref[place : place + dim, :] = coords_ref[:, block * LANES : (block + 1) * LANES]
        place += dim
    table = count_rows(near_ref, far_ref)
    table_ref[...] = table
    local_ref[place : place + 16, :] = jnp.concatenate([table, table], axis=0).astype(bf16)


def joined_kernel(mine_ref, other_ref, leaf_ref, node_ref, upper_ref, out_ref, message_ref):
    half = mine_ref.shape[0]
    columns = LANES // LEAVES
    result = mine_ref[...] + other_ref[...]
    message_ref[0:half, :] = result.astype(bf16)
    flat = result.T.astype(bf16)
    charges = [flat[0:columns], flat[columns:]]
    out_ref[...] = jnp.concatenate(charges, axis=1)
    message_ref[half : half + LANES, :] = skeleton_rows(charges, leaf_ref, node_ref, upper_ref)


def added_kernel(mine_ref, other_ref, out_ref):
    columns = LANES // LEAVES
    flat = (mine_ref[...] + other_ref[...]).T.astype(bf16)
    out_ref[...] = jnp.concatenate([flat[0:columns], flat[columns:]], axis=1)


def stage_kernel(stage, *refs):
    ring, near_spots, far_spots, n_sub, dim, points, begins, first, last, mode = stage
    refs = list(refs)
    use, keep = mode == "use", mode == "keep"
    spots = sorted(set(near_spots) | set(far_spots))
    makes = not use
    table_refs = [refs.pop(0) for _ in range(1 if begins else CORES)]
    if begins:
        local_ref = refs.pop(0)
        charge_refs = skeleton_refs = {spots[0]: local_ref}
    else:
        place_refs = {spot: refs.pop(0) for spot in near_spots} if makes else {}
        skeleton_refs = {spot: refs.pop(0) for spot in far_spots} if makes else {}
        charge_refs = {spot: refs.pop(0) for spot in spots}
    kept_refs = {}
    far_kept_ref = None
    if use:
        kept_refs = {spot: refs.pop(0) for spot in near_spots}
        far_kept_ref = refs.pop(0) if far_spots else None
    if begins:
        sibling_ref = refs.pop(0)
    elif makes:
        targets_ref = refs.pop(0)
    if not first:
        refs.pop(0), refs.pop(0)
    upper_points_ref = refs.pop(0) if last and makes else None
    if begins:
        targets_ref, table_ref = refs.pop(0), refs.pop(0)
    if keep:
        kept_refs = {spot: refs.pop(0) for spot in near_spots}
        far_kept_ref = refs.pop(0) if far_spots else None
    if last:
        half_refs = refs.pop(0), refs.pop(0)
    total_ref, sums_ref, far_charges_ref, charges_ref = refs[:4]
    if makes:
        near_ref, far_ref = refs[4:]

    skeletons_at = points + LANES
    blocks = points // LANES
    low_half = in_low_half((LANES, LANES))
    lane = lax.broadcasted_iota(i32, (8, LANES), 1)

    def span_of(leaf):
        return slice(leaf * points, (leaf + 1) * points)

    def points_of(spot, leaf):
        if not begins:
            return place_refs[spot][:, span_of(leaf)]
        begin = skeletons_at + dim + leaf * blocks * dim
        rows = [begin + block * dim for block in range(blocks)]
        return jnp.concatenate([local_ref[row : row + dim, :] for row in rows], axis=1)

    if begins:
        begin = skeletons_at + dim + LEAVES * blocks * dim
        table_ref[...] = local_ref[begin : begin + 16, :].astype(f32)[0:8]
        table_refs = [table_ref] + table_refs
        for leaf in range(LEAVES):
            targets_ref[0, span_of(leaf), :] = target_rows(points_of(0, leaf))
            targets_ref[1, span_of(leaf), :] = target_rows(sibling_ref[:, span_of(leaf)])
    if first:
        total_ref[...] = jnp.zeros_like(total_ref)
        sums_ref[...] = jnp.zeros_like(sums_ref)

    def table_of(core):
        mine, other = (ref[...] for ref in table_refs)
        return jnp.where(core == 0, mine, other)

    def picked(table, entry):
        return jnp.sum(jnp.where(lane == entry, table, 0.0), axis=1, keepdims=True)

    def values(core, sources_ref, kept_ref):
        if use:
            return kept_ref[...]
        made = kernel_values(targets_ref[core], sources_ref[...])
        if kept_ref is not None:
            kept_ref[...] = made
        return made

    devices = {spot: device_of(ring, spot) for spot in spots}

    def near_part(turn, spot, core, leaf):
        at = near_spots.index(spot)
        table = table_of(core)
        named = [
            picked(table, devices[spot] * LEAVES + which)[0:LEAVES] for which in range(LEAVES)
        ]
        if leaf is None:
            second = jnp.where(jnp.sum(named[1], axis=0, keepdims=True) > 0.0, 1.0, 0.0)
        else:
            second = jnp.full((1, 1), float(leaf), f32)
        times = named[0] * (1.0 - second) + named[1] * second
        if makes:
            low, high = (points_of(spot, which) for which in range(LEAVES))
            chosen = low * (1.0 - second).astype(bf16) + high * second.astype(bf16)
            put_sources(near_ref.at[at], chosen)
        half = jnp.where(lane[0:1] < LANES // LEAVES, 1.0 - second, second).astype(bf16)
        charges_ref[at] = charge_refs[spot][0:points, :] * half
        kept = kept_refs[spot].at[turn] if kept_refs else None
        added = matmul(values(core, near_ref.at[at] if makes else None, kept), charges_ref[at])
        return [times[own : own + 1] * added[span_of(own)] for own in range(LEAVES)]

    weights = []
    skeletons = []
    for spot in far_spots:
        rows = charge_refs[spot][points : points + LANES, :].astype(f32)
        weights.append((jnp.where(low_half, rows, swapped(rows)), devices[spot]))
        sums_ref[devices[spot] // BRANCH] += rows
        if makes:
            skeletons.append(skeleton_refs[spot][skeletons_at : skeletons_at + dim, :])
    if last:
        for sub in range(n_sub):
            rows = sums_ref[sub]
            weights.append((jnp.where(low_half, swapped(rows), rows), len(ring) * CORES + sub))
            if makes:
                skeletons.append(upper_points_ref[:, sub * LANES : (sub + 1) * LANES])
    if far_spots and makes:
        put_sources(far_ref, jnp.concatenate(skeletons, axis=1))

    def far_part(core):
        table = table_of(core)
        kernel = values(
            core,
            far_ref if makes else None,
            None if far_kept_ref is None else far_kept_ref.at[core],
        )
        added = []
        for own in range(LEAVES):
            for position, (block, node) in enumerate(weights):
                scaled = block * picked(table, node)[LEAVES + own : LEAVES + own + 1]
                high = scaled.astype(bf16).astype(f32)
                rows = slice(position * LANES, (position + 1) * LANES)
                far_charges_ref[own, rows, :] = jnp.where(low_half, high, scaled - high).astype(bf16)
            added.append(matmul(kernel[span_of(own)], far_charges_ref[own]))
        return added

    def add(core, parts):
        for own in range(LEAVES):
            total = total_ref[core, span_of(own), :]
            for part in parts:
                total = total + part[own]
            total_ref[core, span_of(own), :] = total

    if first:
        for leaf in range(LEAVES):
            add(0, [near_part(leaf, 0, 0, leaf)])
        add(1, [near_part(LEAVES, 0, 1, None), far_part(1)])
    else:

        def step(core, carry):
            parts = [near_part(core, spot, core, None) for spot in near_spots]
            add(core, parts + ([far_part(core)] if far_spots else []))
            return carry

        lax.fori_loop(0, CORES, step, 0)

    if last:
        for core, ref in enumerate(half_refs):
            both = [total_ref[core, span_of(leaf), :] for leaf in range(LEAVES)]
            both = [total + swapped(total) for total in both]
            ref[...] = jnp.where(in_low_half(both[0].shape), both[0], both[1])


def gate_kernel(message_ref, after_ref, out_ref):
    pass


def gated(message, after):
    anywhere = pl.BlockSpec(memory_space=pl.ANY)
    return pl.pallas_call(
        gate_kernel,
        out_shape=jax.ShapeDtypeStruct(message.shape, message.dtype),
        in_specs=[anywhere] * 2,
        out_specs=anywhere,
        input_output_aliases={0: 0},
        compiler_params=pltpu.CompilerParams(vmem_limit_bytes=2**20),
    )(message, after)


def call(body, args, out_shapes, streamed=(), scratch=(), aliases={}, flops=0, vmem_mib=16):
    vmem = pl.BlockSpec(memory_space=pltpu.VMEM)
    specs = []
    for place, arg in enumerate(args):
        if arg.dtype == i32:
            specs.append(pl.BlockSpec(memory_space=pltpu.SMEM))
        elif place in streamed:
            specs.append(pl.BlockSpec(arg.shape, lambda i: (0,) * 2))
        else:
            specs.append(vmem)
    moved = sum(arg.size * arg.dtype.itemsize for arg in args)
    return pl.pallas_call(
        body,
        grid=(1,),
        out_shape=out_shapes,
        in_specs=specs,
        out_specs=[vmem for _ in out_shapes],
        scratch_shapes=list(scratch),
        input_output_aliases=aliases,
        compiler_params=pltpu.CompilerParams(vmem_limit_bytes=vmem_mib * 1024 * 1024),
        cost_estimate=pl.CostEstimate(flops=flops, bytes_accessed=moved, transcendentals=0),
    )(*args)


def ring_order(chips):
    if chips == 8:
        return [0, 2, 4, 6, 7, 5, 3, 1]
    return list(range(chips))


def on_device(
    coords,
    charges,
    near_lists,
    far_lists,
    leaf_interp,
    node_interp,
    upper_interp,
    node_points,
    upper_points,
):
    dim, local = coords.shape
    columns = charges.shape[0]
    points = local // LEAVES
    peers = lax.axis_size("leaf")
    n_sub = peers // BRANCH
    ring = ring_order(peers // CORES)
    chips = len(ring)

    def along(step):
        return [
            (ring[place] * CORES + core, ring[(place + step * (1 - 2 * core)) % chips] * CORES + core)
            for place in range(chips)
            for core in range(CORES)
        ]

    one_way = functools.partial(lax.ppermute, axis_name="leaf", perm=along(1))
    other_way = functools.partial(lax.ppermute, axis_name="leaf", perm=along(-1))
    to_sibling = functools.partial(
        lax.ppermute, axis_name="leaf", perm=[(device, device ^ 1) for device in range(peers)]
    )

    def shape(*extent, dtype=bf16):
        return jax.ShapeDtypeStruct(extent, dtype)

    maps = [leaf_interp, node_interp, upper_interp]
    sibling_coords = to_sibling(coords)
    coords_next = one_way(coords), other_way(coords)
    message, own, table = call(
        message_kernel,
        [near_lists, far_lists, coords, charges, node_points] + maps,
        [
            shape(points + LANES + dim, LANES),
            shape(points + LANES + dim + LEAVES * points // LANES * dim + 16, LANES),
            shape(8, LANES, dtype=f32),
        ],
        streamed=range(2, 8),
        vmem_mib=60,
    )
    sibling_table = to_sibling(table)

    total_shape = shape(CORES, local, LANES, dtype=f32)
    sums_shape = shape(n_sub, LANES, LANES, dtype=f32)
    half_shape = shape(points, LANES, dtype=f32)
    targets_shape = shape(CORES, local, LANES)

    steps = LEAVES + 1 + CORES * (chips - 1)
    kept_bytes = 2 * points * (steps * local + CORES * LEAVES * (chips + n_sub) * LANES)
    keeping = kept_bytes <= KEPT_MIB * 2**20

    def stage(near_spots, far_spots, given, carried, last, mode, begins=False):
        first = not carried
        makes = mode != "use"
        spots = sorted(set(near_spots) | set(far_spots))
        if begins:
            args = [sibling_table, own, sibling_coords]
        else:
            args = list(given["tables"])
            if makes:
                args += [given["places"][spot] for spot in near_spots]
                args += [given["skeletons"][spot] for spot in far_spots]
            args += [given["charges"][spot] for spot in spots]
            if makes:
                args += [given["targets"]]
            else:
                args += [given["near"][spot] for spot in near_spots]
                args += [given["far"][far_spots]] if far_spots else []
        carried_at = len(args)
        args += carried
        args += [upper_points] if last and makes else []
        far_width = max(LANES, LANES * (len(far_spots) + (n_sub if last else 0)))
        scratch = [
            pltpu.VMEM((LEAVES, far_width, LANES), bf16),
            pltpu.VMEM((len(near_spots), points, LANES), bf16),
        ]
        if makes:
            scratch += [
                pltpu.VMEM((len(near_spots), LANES, points), bf16),
                pltpu.VMEM((LANES, far_width), bf16),
            ]
        names, outs = [], []
        if begins:
            names += ["targets", "table"]
            outs += [targets_shape, shape(8, LANES, dtype=f32)]
        if mode == "keep":
            names += [("near", spot) for spot in near_spots]
            outs += [shape(LEAVES + 1 if first else CORES, local, points) for _ in near_spots]
            names += [("far", far_spots)] if far_spots else []
            outs += [shape(CORES, local, far_width)] if far_spots else []
        if last:
            names += ["mine", "other"]
            outs += [half_shape, half_shape]
        aliases = {carried_at + k: len(outs) + k for k in range(len(carried))}
        names += ["total", "sums"]
        outs += [total_shape, sums_shape]
        static = (
            ring, near_spots, far_spots, n_sub, dim, points, begins, first, last, mode
        )
        results = call(
            functools.partial(stage_kernel, static),
            args,
            outs,
            scratch=scratch,
            aliases=aliases,
            flops=len(near_spots) * (2 if makes else 1) * 10**9,
        )
        return dict(zip(names, results))

    def far_spots_of(spot):
        return (spot - 1, spot) if spot % 2 == 0 and spot > 0 else (spot,)

    mode = "keep" if keeping else "make"
    given = {"near": {}, "far": {}, "places": {0: coords}, "skeletons": {0: message}}
    given["charges"] = given["skeletons"]

    def keep_results(results):
        for name, value in results.items():
            if isinstance(name, tuple):
                given[name[0]][name[1]] = value
        return [results["total"], results["sums"]]

    sent = one_way(message), other_way(message)
    results = stage((0,), (0,), given, [], False, mode, begins=True)
    given["targets"], given["tables"] = results["targets"], [results["table"], sibling_table]
    carried = keep_results(results)
    for hop in range(1, chips // 2):
        final = hop == chips // 2 - 1
        spots = (2 * hop - 1, 2 * hop)
        for at, spot in enumerate(spots):
            given["places"][spot] = coords_next[at]
            given["skeletons"][spot] = sent[at]
        coords_next = one_way(coords_next[0]), None if final else other_way(coords_next[1])
        sent = one_way(sent[0]), None if final else other_way(sent[1])
        carried = keep_results(stage(spots, spots, given, carried, False, mode))
    across = (chips - 1,)
    given["places"][across[0]], given["skeletons"][across[0]] = coords_next[0], sent[0]
    results = stage(across, across, given, carried, True, mode)
    keep_results(results)
    first, message = call(
        joined_kernel,
        [results["mine"], to_sibling(results["other"])] + maps,
        [shape(columns, local), shape(points + LANES, LANES)],
    )

    mode = "use" if keeping else "make"
    given["charges"] = {}
    carried = []

    def arrived(spot, message):
        nonlocal carried
        given["charges"][spot] = message
        last = spot == chips - 1
        far_spots = () if spot % 2 == 1 and not last else far_spots_of(spot)
        results = stage((spot,), far_spots, given, carried, last, mode)
        carried = [results["total"], results["sums"]]
        return results

    one, other = one_way(message), other_way(message)
    arrived(0, message)
    for hop in range(1, chips // 2):
        one_next = one_way(one)
        arrived(2 * hop - 1, one)
        other_next = None
        if hop < chips // 2 - 1:
            other = gated(other, carried[1])
            other_next = other_way(other)
        arrived(2 * hop, other)
        one, other = one_next, other_next
    results = arrived(chips - 1, one)
    (second,) = call(
        added_kernel, [results["mine"], to_sibling(results["other"])], [shape(columns, local)]
    )
    return (first, second)


def solution(mesh):
    placed = (
        P(None, ("groups", "leaf")),
        P(None, ("groups", "leaf")),
        P(("groups", "leaf"), None),
        P(("groups", "leaf"), None),
        P(("groups", "leaf"), None),
        P(("groups", "leaf"), None),
        P(("groups", "leaf"), None),
        P(None, ("groups", "leaf")),
        P(None, "groups"),
    )
    return jax.shard_map(
        on_device,
        mesh=mesh,
        in_specs=placed,
        out_specs=(P(None, ("groups", "leaf")), P(None, ("groups", "leaf"))),
        check_vma=False,
    )
```

```python
import functools

import jax
import jax.numpy as jnp
from jax import lax
from jax.experimental import pallas as pl
from jax.experimental.pallas import tpu as pltpu
from jax.sharding import PartitionSpec as P

BRANCH = 16
EXTRA = 16
LANES = 128
CORES = 2
LEAVES = 2
KEPT_MIB = 30

bf16 = jnp.bfloat16
f32 = jnp.float32
i32 = jnp.int32


def matmul(left, right):
    return jnp.dot(left, right, preferred_element_type=f32)


def square_parts(points):
    minus = -jnp.sum(points * points, axis=0, keepdims=True)
    high = minus.astype(bf16).astype(f32)
    rest = minus - high
    middle = rest.astype(bf16).astype(f32)
    low = rest - middle
    return high, middle, low


def extra_rows(parts, first, width):
    row = lax.broadcasted_iota(i32, (EXTRA, width), 0)
    rows = jnp.where(row < 6, 1.0, 0.0).astype(f32)
    for offset, part in enumerate(parts):
        rows = jnp.where(row == first + offset, jnp.broadcast_to(part, (EXTRA, width)), rows)
    return rows


def put_sources(sources_ref, points):
    dim, width = points.shape
    sources_ref[0:dim, :] = points
    parts = square_parts(points.astype(f32))
    sources_ref[dim : dim + EXTRA, :] = extra_rows(parts, 3, width).astype(bf16)
    sources_ref[dim + EXTRA :, :] = jnp.zeros((LANES - dim - EXTRA, width), bf16)


def target_rows(points):
    dim, width = points.shape
    points = points.astype(f32)
    extra = extra_rows(square_parts(points), 0, width)
    blank = jnp.zeros((LANES - dim - EXTRA, width), f32)
    return jnp.concatenate([2.0 * points, extra, blank], axis=0).T.astype(bf16)


def in_low_half(shape):
    return lax.broadcasted_iota(i32, shape, 1) < LANES // 2


def swapped(values):
    return pltpu.roll(values, LANES // 2, 1)


def kernel_values(targets, sources):
    return jnp.exp(matmul(targets, sources)).astype(bf16)


def skeleton_rows(charges, leaf_ref, node_ref, upper_ref):
    points = charges[0].shape[1]
    parts = []
    for leaf, block in enumerate(charges):
        span = slice(leaf * points, (leaf + 1) * points)
        parts.append(matmul(block, leaf_ref[span, :]).astype(bf16))
    weights = matmul(jnp.concatenate(parts, axis=1), node_ref[...]).astype(bf16)
    term = matmul(weights, upper_ref[...])
    return jnp.concatenate([weights.astype(f32), term], axis=0).T.astype(bf16)


def count_rows(near_ref, far_ref):
    shape = (8, LANES)
    row, lane = lax.broadcasted_iota(i32, shape, 0), lax.broadcasted_iota(i32, shape, 1)
    table = jnp.zeros(shape, f32)
    for leaf in range(LEAVES):
        for first, ref in ((0, near_ref), (LEAVES, far_ref)):
            for slot in range(ref.shape[1]):
                hit = (row == first + leaf) & (lane == ref[leaf, slot])
                table = table + jnp.where(hit, 1.0, 0.0)
    return table


def device_of(ring, spot):
    chips = len(ring)
    me = lax.axis_index("leaf")
    core = me % CORES
    place = jnp.int32(0)
    for at, chip in enumerate(ring):
        place = jnp.where(me // CORES == chip, at, place)
    hop = (spot + 1) // 2
    step = hop if spot % 2 == 0 else -hop
    met = (place + step * (1 - 2 * core) + chips) % chips
    device = jnp.int32(0)
    for at, chip in enumerate(ring):
        device = jnp.where(met == at, chip * CORES + core, device)
    return device


def message_kernel(
    near_ref,
    far_ref,
    coords_ref,
    charges_ref,
    points_ref,
    leaf_ref,
    node_ref,
    upper_ref,
    message_ref,
    local_ref,
    table_ref,
):
    dim, local = coords_ref.shape
    half = local // LEAVES
    charges = [charges_ref[:, 0:half], charges_ref[:, half:]]
    sent = [
        jnp.concatenate(charges, axis=0).astype(f32).T.astype(bf16),
        skeleton_rows(charges, leaf_ref, node_ref, upper_ref),
        points_ref[...],
    ]
    place = 0
    for part in sent:
        rows = slice(place, place + part.shape[0])
        message_ref[rows, :] = part
        local_ref[rows, :] = part
        place += part.shape[0]
    for block in range(local // LANES):
        local_ref[place : place + dim, :] = coords_ref[:, block * LANES : (block + 1) * LANES]
        place += dim
    table = count_rows(near_ref, far_ref)
    table_ref[...] = table
    local_ref[place : place + 16, :] = jnp.concatenate([table, table], axis=0).astype(bf16)


def joined_kernel(mine_ref, other_ref, leaf_ref, node_ref, upper_ref, out_ref, *message_refs):
    half = mine_ref.shape[0]
    columns = LANES // LEAVES
    result = mine_ref[...] + other_ref[...]
    flat = result.T.astype(bf16)
    charges = [flat[0:columns], flat[columns:]]
    out_ref[...] = jnp.concatenate(charges, axis=1)
    rows = skeleton_rows(charges, leaf_ref, node_ref, upper_ref)
    for message_ref in message_refs:
        message_ref[0:half, :] = result.astype(bf16)
        message_ref[half : half + LANES, :] = rows


def added_kernel(mine_ref, other_ref, out_ref):
    columns = LANES // LEAVES
    flat = (mine_ref[...] + other_ref[...]).T.astype(bf16)
    out_ref[...] = jnp.concatenate([flat[0:columns], flat[columns:]], axis=1)


def stage_kernel(stage, *refs):
    ring, near_spots, far_spots, n_sub, dim, points, begins, first, last, mode = stage
    refs = list(refs)
    use, keep = mode == "use", mode == "keep"
    spots = sorted(set(near_spots) | set(far_spots))
    makes = not use
    table_refs = [refs.pop(0) for _ in range(1 if begins else CORES)]
    if begins:
        local_ref = refs.pop(0)
        charge_refs = skeleton_refs = {spots[0]: local_ref}
    else:
        place_refs = {spot: refs.pop(0) for spot in near_spots} if makes else {}
        skeleton_refs = {spot: refs.pop(0) for spot in far_spots} if makes else {}
        charge_refs = {spot: refs.pop(0) for spot in spots}
    kept_refs = {}
    far_kept_ref = None
    if use:
        kept_refs = {spot: refs.pop(0) for spot in near_spots}
        far_kept_ref = refs.pop(0) if far_spots else None
    if begins:
        sibling_ref = refs.pop(0)
    elif makes:
        targets_ref = refs.pop(0)
    if not first:
        refs.pop(0), refs.pop(0)
    upper_points_ref = refs.pop(0) if last and makes else None
    if begins:
        targets_ref, table_ref = refs.pop(0), refs.pop(0)
    if keep:
        kept_refs = {spot: refs.pop(0) for spot in near_spots}
        far_kept_ref = refs.pop(0) if far_spots else None
    if last:
        half_refs = refs.pop(0), refs.pop(0)
    total_ref, sums_ref, far_charges_ref, charges_ref = refs[:4]
    if makes:
        near_ref, far_ref = refs[4:]

    skeletons_at = points + LANES
    blocks = points // LANES
    low_half = in_low_half((LANES, LANES))
    lane = lax.broadcasted_iota(i32, (8, LANES), 1)

    def span_of(leaf):
        return slice(leaf * points, (leaf + 1) * points)

    def points_of(spot, leaf):
        if not begins:
            return place_refs[spot][:, span_of(leaf)]
        begin = skeletons_at + dim + leaf * blocks * dim
        rows = [begin + block * dim for block in range(blocks)]
        return jnp.concatenate([local_ref[row : row + dim, :] for row in rows], axis=1)

    if begins:
        begin = skeletons_at + dim + LEAVES * blocks * dim
        table_ref[...] = local_ref[begin : begin + 16, :].astype(f32)[0:8]
        table_refs = [table_ref] + table_refs
        for leaf in range(LEAVES):
            targets_ref[0, span_of(leaf), :] = target_rows(points_of(0, leaf))
            targets_ref[1, span_of(leaf), :] = target_rows(sibling_ref[:, span_of(leaf)])
    if first:
        total_ref[...] = jnp.zeros_like(total_ref)
        sums_ref[...] = jnp.zeros_like(sums_ref)

    def table_of(core):
        mine, other = (ref[...] for ref in table_refs)
        return jnp.where(core == 0, mine, other)

    def picked(table, entry):
        return jnp.sum(jnp.where(lane == entry, table, 0.0), axis=1, keepdims=True)

    def values(core, sources_ref, kept_ref):
        if use:
            return kept_ref[...]
        made = kernel_values(targets_ref[core], sources_ref[...])
        if kept_ref is not None:
            kept_ref[...] = made
        return made

    devices = {spot: device_of(ring, spot) for spot in spots}

    def near_part(turn, spot, core, leaf):
        at = near_spots.index(spot)
        table = table_of(core)
        named = [
            picked(table, devices[spot] * LEAVES + which)[0:LEAVES] for which in range(LEAVES)
        ]
        if leaf is None:
            second = jnp.where(jnp.sum(named[1], axis=0, keepdims=True) > 0.0, 1.0, 0.0)
        else:
            second = jnp.full((1, 1), float(leaf), f32)
        times = named[0] * (1.0 - second) + named[1] * second
        if makes:
            low, high = (points_of(spot, which) for which in range(LEAVES))
            chosen = low * (1.0 - second).astype(bf16) + high * second.astype(bf16)
            put_sources(near_ref.at[at], chosen)
        half = jnp.where(lane[0:1] < LANES // LEAVES, 1.0 - second, second).astype(bf16)
        charges_ref[at] = charge_refs[spot][0:points, :] * half
        kept = kept_refs[spot].at[turn] if kept_refs else None
        added = matmul(values(core, near_ref.at[at] if makes else None, kept), charges_ref[at])
        return [times[own : own + 1] * added[span_of(own)] for own in range(LEAVES)]

    weights = []
    skeletons = []
    for spot in far_spots:
        rows = charge_refs[spot][points : points + LANES, :].astype(f32)
        weights.append((jnp.where(low_half, rows, swapped(rows)), devices[spot]))
        sums_ref[devices[spot] // BRANCH] += rows
        if makes:
            skeletons.append(skeleton_refs[spot][skeletons_at : skeletons_at + dim, :])
    if last:
        for sub in range(n_sub):
            rows = sums_ref[sub]
            weights.append((jnp.where(low_half, swapped(rows), rows), len(ring) * CORES + sub))
            if makes:
                skeletons.append(upper_points_ref[:, sub * LANES : (sub + 1) * LANES])
    if far_spots and makes:
        put_sources(far_ref, jnp.concatenate(skeletons, axis=1))

    def far_part(core):
        table = table_of(core)
        kernel = values(
            core,
            far_ref if makes else None,
            None if far_kept_ref is None else far_kept_ref.at[core],
        )
        added = []
        for own in range(LEAVES):
            for position, (block, node) in enumerate(weights):
                scaled = block * picked(table, node)[LEAVES + own : LEAVES + own + 1]
                high = scaled.astype(bf16).astype(f32)
                rows = slice(position * LANES, (position + 1) * LANES)
                far_charges_ref[own, rows, :] = jnp.where(low_half, high, scaled - high).astype(bf16)
            added.append(matmul(kernel[span_of(own)], far_charges_ref[own]))
        return added

    def add(core, parts):
        for own in range(LEAVES):
            total = total_ref[core, span_of(own), :]
            for part in parts:
                total = total + part[own]
            total_ref[core, span_of(own), :] = total

    if first:
        for leaf in range(LEAVES):
            add(0, [near_part(leaf, 0, 0, leaf)])
        add(1, [near_part(LEAVES, 0, 1, None), far_part(1)])
    else:

        def step(core, carry):
            parts = [near_part(core, spot, core, None) for spot in near_spots]
            add(core, parts + ([far_part(core)] if far_spots else []))
            return carry

        lax.fori_loop(0, CORES, step, 0)

    if last:
        for core, ref in enumerate(half_refs):
            both = [total_ref[core, span_of(leaf), :] for leaf in range(LEAVES)]
            both = [total + swapped(total) for total in both]
            ref[...] = jnp.where(in_low_half(both[0].shape), both[0], both[1])


def gate_kernel(message_ref, after_ref, out_ref):
    pass


def gated(message, after):
    anywhere = pl.BlockSpec(memory_space=pl.ANY)
    return pl.pallas_call(
        gate_kernel,
        out_shape=jax.ShapeDtypeStruct(message.shape, message.dtype),
        in_specs=[anywhere] * 2,
        out_specs=anywhere,
        input_output_aliases={0: 0},
        compiler_params=pltpu.CompilerParams(vmem_limit_bytes=2**20),
    )(message, after)


def call(body, args, out_shapes, streamed=(), scratch=(), aliases={}, flops=0, vmem_mib=16):
    vmem = pl.BlockSpec(memory_space=pltpu.VMEM)
    specs = []
    for place, arg in enumerate(args):
        if arg.dtype == i32:
            specs.append(pl.BlockSpec(memory_space=pltpu.SMEM))
        elif place in streamed:
            specs.append(pl.BlockSpec(arg.shape, lambda i: (0,) * 2))
        else:
            specs.append(vmem)
    moved = sum(arg.size * arg.dtype.itemsize for arg in args)
    return pl.pallas_call(
        body,
        grid=(1,),
        out_shape=out_shapes,
        in_specs=specs,
        out_specs=[vmem for _ in out_shapes],
        scratch_shapes=list(scratch),
        input_output_aliases=aliases,
        compiler_params=pltpu.CompilerParams(vmem_limit_bytes=vmem_mib * 1024 * 1024),
        cost_estimate=pl.CostEstimate(flops=flops, bytes_accessed=moved, transcendentals=0),
    )(*args)


def ring_order(chips):
    if chips == 8:
        return [0, 2, 4, 6, 7, 5, 3, 1]
    return list(range(chips))


def on_device(
    coords,
    charges,
    near_lists,
    far_lists,
    leaf_interp,
    node_interp,
    upper_interp,
    node_points,
    upper_points,
):
    dim, local = coords.shape
    columns = charges.shape[0]
    points = local // LEAVES
    peers = lax.axis_size("leaf")
    n_sub = peers // BRANCH
    ring = ring_order(peers // CORES)
    chips = len(ring)

    def along(step):
        return [
            (ring[place] * CORES + core, ring[(place + step * (1 - 2 * core)) % chips] * CORES + core)
            for place in range(chips)
            for core in range(CORES)
        ]

    one_way = functools.partial(lax.ppermute, axis_name="leaf", perm=along(1))
    other_way = functools.partial(lax.ppermute, axis_name="leaf", perm=along(-1))
    to_sibling = functools.partial(
        lax.ppermute, axis_name="leaf", perm=[(device, device ^ 1) for device in range(peers)]
    )

    def shape(*extent, dtype=bf16):
        return jax.ShapeDtypeStruct(extent, dtype)

    maps = [leaf_interp, node_interp, upper_interp]
    sibling_coords = to_sibling(coords)
    coords_next = one_way(coords), other_way(coords)
    message, own, table = call(
        message_kernel,
        [near_lists, far_lists, coords, charges, node_points] + maps,
        [
            shape(points + LANES + dim, LANES),
            shape(points + LANES + dim + LEAVES * points // LANES * dim + 16, LANES),
            shape(8, LANES, dtype=f32),
        ],
        streamed=range(2, 8),
        vmem_mib=60,
    )
    sibling_table = to_sibling(table)

    total_shape = shape(CORES, local, LANES, dtype=f32)
    sums_shape = shape(n_sub, LANES, LANES, dtype=f32)
    half_shape = shape(points, LANES, dtype=f32)
    targets_shape = shape(CORES, local, LANES)

    steps = LEAVES + 1 + CORES * (chips - 1)
    kept_bytes = 2 * points * (steps * local + CORES * LEAVES * (chips + n_sub) * LANES)
    keeping = kept_bytes <= KEPT_MIB * 2**20

    def stage(near_spots, far_spots, given, carried, last, mode, begins=False):
        first = not carried
        makes = mode != "use"
        spots = sorted(set(near_spots) | set(far_spots))
        if begins:
            args = [sibling_table, own, sibling_coords]
        else:
            args = list(given["tables"])
            if makes:
                args += [given["places"][spot] for spot in near_spots]
                args += [given["skeletons"][spot] for spot in far_spots]
            args += [given["charges"][spot] for spot in spots]
            if makes:
                args += [given["targets"]]
            else:
                args += [given["near"][spot] for spot in near_spots]
                args += [given["far"][far_spots]] if far_spots else []
        carried_at = len(args)
        args += carried
        args += [upper_points] if last and makes else []
        far_width = max(LANES, LANES * (len(far_spots) + (n_sub if last else 0)))
        scratch = [
            pltpu.VMEM((LEAVES, far_width, LANES), bf16),
            pltpu.VMEM((len(near_spots), points, LANES), bf16),
        ]
        if makes:
            scratch += [
                pltpu.VMEM((len(near_spots), LANES, points), bf16),
                pltpu.VMEM((LANES, far_width), bf16),
            ]
        names, outs = [], []
        if begins:
            names += ["targets", "table"]
            outs += [targets_shape, shape(8, LANES, dtype=f32)]
        if mode == "keep":
            names += [("near", spot) for spot in near_spots]
            outs += [shape(LEAVES + 1 if first else CORES, local, points) for _ in near_spots]
            names += [("far", far_spots)] if far_spots else []
            outs += [shape(CORES, local, far_width)] if far_spots else []
        if last:
            names += ["mine", "other"]
            outs += [half_shape, half_shape]
        aliases = {carried_at + k: len(outs) + k for k in range(len(carried))}
        names += ["total", "sums"]
        outs += [total_shape, sums_shape]
        static = (
            ring, near_spots, far_spots, n_sub, dim, points, begins, first, last, mode
        )
        results = call(
            functools.partial(stage_kernel, static),
            args,
            outs,
            scratch=scratch,
            aliases=aliases,
            flops=len(near_spots) * (2 if makes else 1) * 10**9,
        )
        return dict(zip(names, results))

    def far_spots_of(spot):
        return (spot - 1, spot) if spot % 2 == 0 and spot > 0 else (spot,)

    mode = "keep" if keeping else "make"
    given = {"near": {}, "far": {}, "places": {0: coords}, "skeletons": {0: message}}
    given["charges"] = given["skeletons"]

    def keep_results(results):
        for name, value in results.items():
            if isinstance(name, tuple):
                given[name[0]][name[1]] = value
        return [results["total"], results["sums"]]

    sent = one_way(message), other_way(message)
    results = stage((0,), (0,), given, [], False, mode, begins=True)
    given["targets"], given["tables"] = results["targets"], [results["table"], sibling_table]
    carried = keep_results(results)
    for hop in range(1, chips // 2):
        final = hop == chips // 2 - 1
        spots = (2 * hop - 1, 2 * hop)
        for at, spot in enumerate(spots):
            given["places"][spot] = coords_next[at]
            given["skeletons"][spot] = sent[at]
        coords_next = one_way(coords_next[0]), None if final else other_way(coords_next[1])
        sent = one_way(sent[0]), None if final else other_way(sent[1])
        carried = keep_results(stage(spots, spots, given, carried, False, mode))
    across = (chips - 1,)
    given["places"][across[0]], given["skeletons"][across[0]] = coords_next[0], sent[0]
    results = stage(across, across, given, carried, True, mode)
    keep_results(results)
    first, message, again = call(
        joined_kernel,
        [results["mine"], to_sibling(results["other"])] + maps,
        [shape(columns, local)] + [shape(points + LANES, LANES)] * 2,
    )

    mode = "use" if keeping else "make"
    given["charges"] = {}
    carried = []

    def arrived(spot, message):
        nonlocal carried
        given["charges"][spot] = message
        last = spot == chips - 1
        far_spots = () if spot % 2 == 1 and not last else far_spots_of(spot)
        results = stage((spot,), far_spots, given, carried, last, mode)
        carried = [results["total"], results["sums"]]
        return results

    one = one_way(message)
    arrived(0, message)
    other = other_way(gated(again, carried[1]))
    for hop in range(1, chips // 2):
        one_next = one_way(one)
        arrived(2 * hop - 1, one)
        other_next = None
        if hop < chips // 2 - 1:
            other = gated(other, carried[1])
            other_next = other_way(other)
        arrived(2 * hop, other)
        one, other = one_next, other_next
    results = arrived(chips - 1, one)
    (second,) = call(
        added_kernel, [results["mine"], to_sibling(results["other"])], [shape(columns, local)]
    )
    return (first, second)


def solution(mesh):
    placed = (
        P(None, ("groups", "leaf")),
        P(None, ("groups", "leaf")),
        P(("groups", "leaf"), None),
        P(("groups", "leaf"), None),
        P(("groups", "leaf"), None),
        P(("groups", "leaf"), None),
        P(("groups", "leaf"), None),
        P(None, ("groups", "leaf")),
        P(None, "groups"),
    )
    return jax.shard_map(
        on_device,
        mesh=mesh,
        in_specs=placed,
        out_specs=(P(None, ("groups", "leaf")), P(None, ("groups", "leaf"))),
        check_vma=False,
    )
```

```python
import functools

import jax
import jax.numpy as jnp
from jax import lax
from jax.experimental import pallas as pl
from jax.experimental.pallas import tpu as pltpu
from jax.sharding import PartitionSpec as P

BRANCH = 16
EXTRA = 16
LANES = 128
CORES = 2
LEAVES = 2
KEPT_MIB = 30

bf16 = jnp.bfloat16
f32 = jnp.float32
i32 = jnp.int32


def matmul(left, right):
    return jnp.dot(left, right, preferred_element_type=f32)


def square_parts(points):
    minus = -jnp.sum(points * points, axis=0, keepdims=True)
    high = minus.astype(bf16).astype(f32)
    rest = minus - high
    middle = rest.astype(bf16).astype(f32)
    low = rest - middle
    return high, middle, low


def extra_rows(parts, first, width):
    row = lax.broadcasted_iota(i32, (EXTRA, width), 0)
    rows = jnp.where(row < 6, 1.0, 0.0).astype(f32)
    for offset, part in enumerate(parts):
        rows = jnp.where(row == first + offset, jnp.broadcast_to(part, (EXTRA, width)), rows)
    return rows


def put_sources(sources_ref, points):
    dim, width = points.shape
    sources_ref[0:dim, :] = points
    parts = square_parts(points.astype(f32))
    sources_ref[dim : dim + EXTRA, :] = extra_rows(parts, 3, width).astype(bf16)
    sources_ref[dim + EXTRA :, :] = jnp.zeros((LANES - dim - EXTRA, width), bf16)


def target_rows(points):
    dim, width = points.shape
    points = points.astype(f32)
    extra = extra_rows(square_parts(points), 0, width)
    blank = jnp.zeros((LANES - dim - EXTRA, width), f32)
    return jnp.concatenate([2.0 * points, extra, blank], axis=0).T.astype(bf16)


def in_low_half(shape):
    return lax.broadcasted_iota(i32, shape, 1) < LANES // 2


def swapped(values):
    return pltpu.roll(values, LANES // 2, 1)


def kernel_values(targets, sources):
    return jnp.exp(matmul(targets, sources)).astype(bf16)


def skeleton_rows(charges, leaf_ref, node_ref, upper_ref):
    points = charges[0].shape[1]
    parts = []
    for leaf, block in enumerate(charges):
        span = slice(leaf * points, (leaf + 1) * points)
        parts.append(matmul(block, leaf_ref[span, :]).astype(bf16))
    weights = matmul(jnp.concatenate(parts, axis=1), node_ref[...]).astype(bf16)
    term = matmul(weights, upper_ref[...])
    return jnp.concatenate([weights.astype(f32), term], axis=0).T.astype(bf16)


def count_rows(near_ref, far_ref):
    shape = (8, LANES)
    row, lane = lax.broadcasted_iota(i32, shape, 0), lax.broadcasted_iota(i32, shape, 1)
    table = jnp.zeros(shape, f32)
    for leaf in range(LEAVES):
        for first, ref in ((0, near_ref), (LEAVES, far_ref)):
            for slot in range(ref.shape[1]):
                hit = (row == first + leaf) & (lane == ref[leaf, slot])
                table = table + jnp.where(hit, 1.0, 0.0)
    return table


def device_of(ring, spot):
    chips = len(ring)
    me = lax.axis_index("leaf")
    core = me % CORES
    place = jnp.int32(0)
    for at, chip in enumerate(ring):
        place = jnp.where(me // CORES == chip, at, place)
    hop = (spot + 1) // 2
    step = hop if spot % 2 == 0 else -hop
    met = (place + step * (1 - 2 * core) + chips) % chips
    device = jnp.int32(0)
    for at, chip in enumerate(ring):
        device = jnp.where(met == at, chip * CORES + core, device)
    return device


def message_kernel(
    near_ref,
    far_ref,
    coords_ref,
    charges_ref,
    points_ref,
    leaf_ref,
    node_ref,
    upper_ref,
    message_ref,
    places_ref,
    local_ref,
):
    dim, local = coords_ref.shape
    half = local // LEAVES
    charges = [charges_ref[:, 0:half], charges_ref[:, half:]]
    sent = [
        jnp.concatenate(charges, axis=0).astype(f32).T.astype(bf16),
        skeleton_rows(charges, leaf_ref, node_ref, upper_ref),
        points_ref[...],
    ]
    place = 0
    for part in sent:
        rows = slice(place, place + part.shape[0])
        message_ref[rows, :] = part
        local_ref[rows, :] = part
        place += part.shape[0]
    for block in range(local // LANES):
        local_ref[place : place + dim, :] = coords_ref[:, block * LANES : (block + 1) * LANES]
        place += dim
    places_ref[...] = coords_ref[...]
    table = count_rows(near_ref, far_ref)
    local_ref[place : place + 16, :] = jnp.concatenate([table, table], axis=0).astype(bf16)


def joined_kernel(mine_ref, other_ref, leaf_ref, node_ref, upper_ref, out_ref, *message_refs):
    half = mine_ref.shape[0]
    columns = LANES // LEAVES
    result = mine_ref[...] + other_ref[...]
    flat = result.T.astype(bf16)
    charges = [flat[0:columns], flat[columns:]]
    out_ref[...] = jnp.concatenate(charges, axis=1)
    rows = skeleton_rows(charges, leaf_ref, node_ref, upper_ref)
    for message_ref in message_refs:
        message_ref[0:half, :] = result.astype(bf16)
        message_ref[half : half + LANES, :] = rows


def added_kernel(mine_ref, other_ref, out_ref):
    columns = LANES // LEAVES
    flat = (mine_ref[...] + other_ref[...]).T.astype(bf16)
    out_ref[...] = jnp.concatenate([flat[0:columns], flat[columns:]], axis=1)


def stage_kernel(stage, *refs):
    ring, near_spots, far_spots, n_sub, dim, points, begins, first, last, near, far = stage
    refs = list(refs)
    spots = sorted(set(near_spots) | set(far_spots))
    makes_near, makes_far = near != "use", far != "use" and bool(far_spots)
    adds = near != "only"
    if begins:
        local_refs = refs.pop(0), refs.pop(0)
        charge_refs = skeleton_refs = {spots[0]: local_refs[0]}
    else:
        table_refs = refs.pop(0), refs.pop(0)
        place_refs = {spot: refs.pop(0) for spot in near_spots} if makes_near else {}
        skeleton_refs = {spot: refs.pop(0) for spot in far_spots} if makes_far else {}
        charge_refs = {spot: refs.pop(0) for spot in spots} if adds else {}
    kept_refs = {}
    far_kept_ref = None
    if near == "use":
        kept_refs = {spot: refs.pop(0) for spot in near_spots}
    if far == "use" and far_spots:
        far_kept_ref = refs.pop(0)
    if (makes_near or makes_far) and not begins:
        targets_ref = refs.pop(0)
    if not first and adds:
        refs.pop(0), refs.pop(0)
    upper_points_ref = refs.pop(0) if last and makes_far else None
    if begins:
        targets_ref = refs.pop(0)
        table_refs = refs.pop(0), refs.pop(0)
    if near in ("keep", "only"):
        kept_refs = {spot: refs.pop(0) for spot in near_spots}
    if far == "keep" and far_spots:
        far_kept_ref = refs.pop(0)
    if last and adds:
        half_refs = refs.pop(0), refs.pop(0)
    if adds:
        total_ref, sums_ref, far_charges_ref, charges_ref = (refs.pop(0) for _ in range(4))
    near_ref = refs.pop(0) if makes_near else None
    far_ref = refs.pop(0) if makes_far else None

    skeletons_at = points + LANES
    blocks = points // LANES
    low_half = in_low_half((LANES, LANES))
    lane = lax.broadcasted_iota(i32, (8, LANES), 1)

    def span_of(leaf):
        return slice(leaf * points, (leaf + 1) * points)

    def local_points(ref, leaf):
        begin = skeletons_at + dim + leaf * blocks * dim
        rows = [begin + block * dim for block in range(blocks)]
        return jnp.concatenate([ref[row : row + dim, :] for row in rows], axis=1)

    def points_of(spot, leaf):
        if begins:
            return local_points(local_refs[0], leaf)
        return place_refs[spot][:, span_of(leaf)]

    if begins:
        begin = skeletons_at + dim + LEAVES * blocks * dim
        for core, ref in enumerate(local_refs):
            table_refs[core][...] = ref[begin : begin + 16, :].astype(f32)[0:8]
            for leaf in range(LEAVES):
                targets_ref[core, span_of(leaf), :] = target_rows(local_points(ref, leaf))
    if first:
        total_ref[...] = jnp.zeros_like(total_ref)
        sums_ref[...] = jnp.zeros_like(sums_ref)

    def table_of(core):
        mine, other = (ref[...] for ref in table_refs)
        return jnp.where(core == 0, mine, other)

    def picked(table, entry):
        return jnp.sum(jnp.where(lane == entry, table, 0.0), axis=1, keepdims=True)

    def values(makes, core, sources_ref, kept_ref):
        if not makes:
            return kept_ref[...]
        made = kernel_values(targets_ref[core], sources_ref[...])
        if kept_ref is not None:
            kept_ref[...] = made
        return made

    devices = {spot: device_of(ring, spot) for spot in spots}

    def near_part(turn, spot, core, leaf):
        at = near_spots.index(spot)
        table = table_of(core)
        named = [
            picked(table, devices[spot] * LEAVES + which)[0:LEAVES] for which in range(LEAVES)
        ]
        if leaf is None:
            second = jnp.where(jnp.sum(named[1], axis=0, keepdims=True) > 0.0, 1.0, 0.0)
        else:
            second = jnp.full((1, 1), float(leaf), f32)
        times = named[0] * (1.0 - second) + named[1] * second
        if makes_near:
            low, high = (points_of(spot, which) for which in range(LEAVES))
            chosen = low * (1.0 - second).astype(bf16) + high * second.astype(bf16)
            put_sources(near_ref.at[at], chosen)
        kept = kept_refs[spot].at[turn] if kept_refs else None
        kernel = values(makes_near, core, near_ref.at[at] if makes_near else None, kept)
        if not adds:
            return None
        half = jnp.where(lane[0:1] < LANES // LEAVES, 1.0 - second, second).astype(bf16)
        charges_ref[at] = charge_refs[spot][0:points, :] * half
        added = matmul(kernel, charges_ref[at])
        return [times[own : own + 1] * added[span_of(own)] for own in range(LEAVES)]

    weights = []
    skeletons = []
    for spot in far_spots:
        rows = charge_refs[spot][points : points + LANES, :].astype(f32)
        weights.append((jnp.where(low_half, rows, swapped(rows)), devices[spot]))
        sums_ref[devices[spot] // BRANCH] += rows
        if makes_far:
            skeletons.append(skeleton_refs[spot][skeletons_at : skeletons_at + dim, :])
    if last and adds:
        for sub in range(n_sub):
            rows = sums_ref[sub]
            weights.append((jnp.where(low_half, swapped(rows), rows), len(ring) * CORES + sub))
            if makes_far:
                skeletons.append(upper_points_ref[:, sub * LANES : (sub + 1) * LANES])
    if makes_far:
        put_sources(far_ref, jnp.concatenate(skeletons, axis=1))

    def far_part(core):
        table = table_of(core)
        kernel = values(
            makes_far,
            core,
            far_ref if makes_far else None,
            None if far_kept_ref is None else far_kept_ref.at[core],
        )
        added = []
        for own in range(LEAVES):
            for position, (block, node) in enumerate(weights):
                scaled = block * picked(table, node)[LEAVES + own : LEAVES + own + 1]
                high = scaled.astype(bf16).astype(f32)
                rows = slice(position * LANES, (position + 1) * LANES)
                far_charges_ref[own, rows, :] = jnp.where(low_half, high, scaled - high).astype(bf16)
            added.append(matmul(kernel[span_of(own)], far_charges_ref[own]))
        return added

    def add(core, parts):
        for own in range(LEAVES):
            total = total_ref[core, span_of(own), :]
            for part in parts:
                total = total + part[own]
            total_ref[core, span_of(own), :] = total

    if first:
        for leaf in range(LEAVES):
            add(0, [near_part(leaf, 0, 0, leaf)])
        add(1, [near_part(LEAVES, 0, 1, None), far_part(1)])
    else:

        def step(core, carry):
            parts = [near_part(core, spot, core, None) for spot in near_spots]
            if adds:
                add(core, parts + ([far_part(core)] if far_spots else []))
            return carry

        lax.fori_loop(0, CORES, step, 0)

    if last and adds:
        for core, ref in enumerate(half_refs):
            both = [total_ref[core, span_of(leaf), :] for leaf in range(LEAVES)]
            both = [total + swapped(total) for total in both]
            ref[...] = jnp.where(in_low_half(both[0].shape), both[0], both[1])


def gate_kernel(message_ref, after_ref, out_ref):
    pass


def gated(message, after):
    anywhere = pl.BlockSpec(memory_space=pl.ANY)
    return pl.pallas_call(
        gate_kernel,
        out_shape=jax.ShapeDtypeStruct(message.shape, message.dtype),
        in_specs=[anywhere] * 2,
        out_specs=anywhere,
        input_output_aliases={0: 0},
        compiler_params=pltpu.CompilerParams(vmem_limit_bytes=2**20),
    )(message, after)


def call(body, args, out_shapes, streamed=(), scratch=(), aliases={}, flops=0, vmem_mib=16):
    vmem = pl.BlockSpec(memory_space=pltpu.VMEM)
    specs = []
    for place, arg in enumerate(args):
        if arg.dtype == i32:
            specs.append(pl.BlockSpec(memory_space=pltpu.SMEM))
        elif place in streamed:
            specs.append(pl.BlockSpec(arg.shape, lambda i: (0,) * 2))
        else:
            specs.append(vmem)
    moved = sum(arg.size * arg.dtype.itemsize for arg in args)
    return pl.pallas_call(
        body,
        grid=(1,),
        out_shape=out_shapes,
        in_specs=specs,
        out_specs=[vmem for _ in out_shapes],
        scratch_shapes=list(scratch),
        input_output_aliases=aliases,
        compiler_params=pltpu.CompilerParams(vmem_limit_bytes=vmem_mib * 1024 * 1024),
        cost_estimate=pl.CostEstimate(flops=flops, bytes_accessed=moved, transcendentals=0),
    )(*args)


def ring_order(chips):
    if chips == 8:
        return [0, 2, 4, 6, 7, 5, 3, 1]
    return list(range(chips))


def on_device(
    coords,
    charges,
    near_lists,
    far_lists,
    leaf_interp,
    node_interp,
    upper_interp,
    node_points,
    upper_points,
):
    dim, local = coords.shape
    columns = charges.shape[0]
    points = local // LEAVES
    peers = lax.axis_size("leaf")
    n_sub = peers // BRANCH
    ring = ring_order(peers // CORES)
    chips = len(ring)

    def along(step):
        return [
            (ring[place] * CORES + core, ring[(place + step * (1 - 2 * core)) % chips] * CORES + core)
            for place in range(chips)
            for core in range(CORES)
        ]

    one_way = functools.partial(lax.ppermute, axis_name="leaf", perm=along(1))
    other_way = functools.partial(lax.ppermute, axis_name="leaf", perm=along(-1))
    to_sibling = functools.partial(
        lax.ppermute, axis_name="leaf", perm=[(device, device ^ 1) for device in range(peers)]
    )

    def shape(*extent, dtype=bf16):
        return jax.ShapeDtypeStruct(extent, dtype)

    maps = [leaf_interp, node_interp, upper_interp]
    message, places, own = call(
        message_kernel,
        [near_lists, far_lists, coords, charges, node_points] + maps,
        [
            shape(points + LANES + dim, LANES),
            shape(dim, local),
            shape(points + LANES + dim + LEAVES * points // LANES * dim + 16, LANES),
        ],
        streamed=range(2, 8),
        vmem_mib=60,
    )
    sibling_own = to_sibling(own)
    sent = one_way(message), other_way(message)
    places = gated(places, sibling_own)
    coords_next = one_way(places), other_way(places)

    total_shape = shape(CORES, local, LANES, dtype=f32)
    sums_shape = shape(n_sub, LANES, LANES, dtype=f32)
    half_shape = shape(points, LANES, dtype=f32)
    targets_shape = shape(CORES, local, LANES)

    steps = LEAVES + 1 + CORES * (chips - 1)
    kept_bytes = 2 * points * (steps * local + CORES * LEAVES * (chips + n_sub) * LANES)
    keeping = kept_bytes <= KEPT_MIB * 2**20

    def stage(near_spots, far_spots, given, carried, last, near, far, begins=False):
        adds = near != "only"
        first = not carried and adds
        makes_near, makes_far = near != "use", far != "use" and bool(far_spots)
        spots = sorted(set(near_spots) | set(far_spots))
        if begins:
            args = [own, sibling_own]
        else:
            args = list(given["tables"])
            args += [given["places"][spot] for spot in near_spots] if makes_near else []
            args += [given["skeletons"][spot] for spot in far_spots] if makes_far else []
            args += [given["charges"][spot] for spot in spots] if adds else []
        args += [given["near"][spot] for spot in near_spots] if near == "use" else []
        args += [given["far"][far_spots]] if far == "use" and far_spots else []
        args += [given["targets"]] if (makes_near or makes_far) and not begins else []
        carried_at = len(args)
        args += carried
        args += [upper_points] if last and makes_far else []
        far_width = max(LANES, LANES * (len(far_spots) + (n_sub if last else 0)))
        scratch = []
        if adds:
            scratch += [
                pltpu.VMEM((LEAVES, far_width, LANES), bf16),
                pltpu.VMEM((len(near_spots), points, LANES), bf16),
            ]
        scratch += [pltpu.VMEM((len(near_spots), LANES, points), bf16)] if makes_near else []
        scratch += [pltpu.VMEM((LANES, far_width), bf16)] if makes_far else []
        names, outs = [], []
        if begins:
            names += ["targets", "mine", "other"]
            outs += [targets_shape] + [shape(8, LANES, dtype=f32)] * CORES
        if near in ("keep", "only"):
            names += [("near", spot) for spot in near_spots]
            outs += [shape(LEAVES + 1 if first else CORES, local, points) for _ in near_spots]
        if far == "keep" and far_spots:
            names += [("far", far_spots)]
            outs += [shape(CORES, local, far_width)]
        if last and adds:
            names += ["mine", "other"]
            outs += [half_shape, half_shape]
        aliases = {carried_at + k: len(outs) + k for k in range(len(carried))}
        if adds:
            names += ["total", "sums"]
            outs += [total_shape, sums_shape]
        static = (ring, near_spots, far_spots, n_sub, dim, points, begins, first, last, near, far)
        results = call(
            functools.partial(stage_kernel, static),
            args,
            outs,
            scratch=scratch,
            aliases=aliases,
            flops=len(near_spots) * (2 if makes_near else 1) * 10**9,
        )
        return dict(zip(names, results))

    def far_spots_of(spot):
        return (spot - 1, spot) if spot % 2 == 0 and spot > 0 else (spot,)

    mode = "keep" if keeping else "make"
    given = {"near": {}, "far": {}, "places": {0: places}, "skeletons": {0: message}}
    given["charges"] = given["skeletons"]

    def keep_results(results):
        for name, value in results.items():
            if isinstance(name, tuple):
                given[name[0]][name[1]] = value
        return [results["total"], results["sums"]]

    results = stage((0,), (0,), given, [], False, mode, mode, begins=True)
    given["targets"], given["tables"] = results["targets"], [results["mine"], results["other"]]
    carried = keep_results(results)
    for hop in range(1, chips // 2):
        final = hop == chips // 2 - 1
        spots = (2 * hop - 1, 2 * hop)
        coords_next = [gated(part, carried[1]) for part in coords_next]
        sent = [gated(part, carried[1]) for part in sent]
        for at, spot in enumerate(spots):
            given["places"][spot] = coords_next[at]
            given["skeletons"][spot] = sent[at]
        coords_next = one_way(coords_next[0]), None if final else other_way(coords_next[1])
        sent = one_way(sent[0]), None if final else other_way(sent[1])
        carried = keep_results(stage(spots, spots, given, carried, False, mode, mode))
    across = (chips - 1,)
    given["places"][across[0]], given["skeletons"][across[0]] = coords_next[0], sent[0]
    near = mode
    if keeping:
        near = "use"
        results = stage(across, (), given, [], False, "only", "use")
        given["near"][across[0]] = results[("near", across[0])]
    results = stage(across, across, given, carried, True, near, mode)
    keep_results(results)
    first, message, again = call(
        joined_kernel,
        [results["mine"], to_sibling(results["other"])] + maps,
        [shape(columns, local)] + [shape(points + LANES, LANES)] * 2,
    )

    mode = "use" if keeping else "make"
    given["charges"] = {}
    carried = []

    def arrived(spot, message):
        nonlocal carried
        given["charges"][spot] = message
        last = spot == chips - 1
        far_spots = () if spot % 2 == 1 and not last else far_spots_of(spot)
        results = stage((spot,), far_spots, given, carried, last, mode, mode)
        carried = [results["total"], results["sums"]]
        return results

    one = one_way(message)
    arrived(0, message)
    other = other_way(gated(again, carried[1]))
    for hop in range(1, chips // 2):
        one_next = one_way(one)
        arrived(2 * hop - 1, one)
        other_next = None
        if hop < chips // 2 - 1:
            other = gated(other, carried[1])
            other_next = other_way(other)
        arrived(2 * hop, other)
        one, other = one_next, other_next
    results = arrived(chips - 1, one)
    (second,) = call(
        added_kernel, [results["mine"], to_sibling(results["other"])], [shape(columns, local)]
    )
    return (first, second)


def solution(mesh):
    placed = (
        P(None, ("groups", "leaf")),
        P(None, ("groups", "leaf")),
        P(("groups", "leaf"), None),
        P(("groups", "leaf"), None),
        P(("groups", "leaf"), None),
        P(("groups", "leaf"), None),
        P(("groups", "leaf"), None),
        P(None, ("groups", "leaf")),
        P(None, "groups"),
    )
    return jax.shard_map(
        on_device,
        mesh=mesh,
        in_specs=placed,
        out_specs=(P(None, ("groups", "leaf")), P(None, ("groups", "leaf"))),
        check_vma=False,
    )
```

```python
import functools

import jax
import jax.numpy as jnp
from jax import lax
from jax.experimental import pallas as pl
from jax.experimental.pallas import tpu as pltpu
from jax.sharding import PartitionSpec as P

BRANCH = 16
EXTRA = 16
LANES = 128
CORES = 2
LEAVES = 2
KEPT_MIB = 30

bf16 = jnp.bfloat16
f32 = jnp.float32
i32 = jnp.int32


def matmul(left, right):
    return jnp.dot(left, right, preferred_element_type=f32)


def square_parts(points):
    minus = -jnp.sum(points * points, axis=0, keepdims=True)
    high = minus.astype(bf16).astype(f32)
    rest = minus - high
    middle = rest.astype(bf16).astype(f32)
    low = rest - middle
    return high, middle, low


def extra_rows(parts, first, width):
    row = lax.broadcasted_iota(i32, (EXTRA, width), 0)
    rows = jnp.where(row < 6, 1.0, 0.0).astype(f32)
    for offset, part in enumerate(parts):
        rows = jnp.where(row == first + offset, jnp.broadcast_to(part, (EXTRA, width)), rows)
    return rows


def put_sources(sources_ref, points):
    dim, width = points.shape
    sources_ref[0:dim, :] = points
    parts = square_parts(points.astype(f32))
    sources_ref[dim : dim + EXTRA, :] = extra_rows(parts, 3, width).astype(bf16)
    sources_ref[dim + EXTRA :, :] = jnp.zeros((LANES - dim - EXTRA, width), bf16)


def target_rows(points):
    dim, width = points.shape
    points = points.astype(f32)
    extra = extra_rows(square_parts(points), 0, width)
    blank = jnp.zeros((LANES - dim - EXTRA, width), f32)
    return jnp.concatenate([2.0 * points, extra, blank], axis=0).T.astype(bf16)


def in_low_half(shape):
    return lax.broadcasted_iota(i32, shape, 1) < LANES // 2


def swapped(values):
    return pltpu.roll(values, LANES // 2, 1)


def kernel_values(targets, sources):
    return jnp.exp(matmul(targets, sources)).astype(bf16)


def skeleton_rows(charges, leaf_ref, node_ref, upper_ref):
    points = charges[0].shape[1]
    parts = []
    for leaf, block in enumerate(charges):
        span = slice(leaf * points, (leaf + 1) * points)
        parts.append(matmul(block, leaf_ref[span, :]).astype(bf16))
    weights = matmul(jnp.concatenate(parts, axis=1), node_ref[...]).astype(bf16)
    term = matmul(weights, upper_ref[...])
    return jnp.concatenate([weights.astype(f32), term], axis=0).T.astype(bf16)


def count_rows(near_ref, far_ref):
    shape = (8, LANES)
    row, lane = lax.broadcasted_iota(i32, shape, 0), lax.broadcasted_iota(i32, shape, 1)
    table = jnp.zeros(shape, f32)
    for leaf in range(LEAVES):
        for first, ref in ((0, near_ref), (LEAVES, far_ref)):
            for slot in range(ref.shape[1]):
                hit = (row == first + leaf) & (lane == ref[leaf, slot])
                table = table + jnp.where(hit, 1.0, 0.0)
    return table


def place_on(ring):
    chip = lax.axis_index("leaf") // CORES
    place = jnp.int32(0)
    for at, other in enumerate(ring):
        place = jnp.where(chip == other, at, place)
    return place


def device_of(ring, spot):
    chips = len(ring)
    core = lax.axis_index("leaf") % CORES
    place = place_on(ring)
    hop = (spot + 1) // 2
    step = hop if spot % 2 == 0 else -hop
    met = (place + step * (1 - 2 * core) + chips) % chips
    device = jnp.int32(0)
    for at, chip in enumerate(ring):
        device = jnp.where(met == at, chip * CORES + core, device)
    return device


def message_kernel(
    near_ref,
    far_ref,
    coords_ref,
    charges_ref,
    points_ref,
    leaf_ref,
    node_ref,
    upper_ref,
    message_ref,
    local_ref,
):
    dim, local = coords_ref.shape
    half = local // LEAVES
    charges = [charges_ref[:, 0:half], charges_ref[:, half:]]
    sent = [
        jnp.concatenate(charges, axis=0).astype(f32).T.astype(bf16),
        skeleton_rows(charges, leaf_ref, node_ref, upper_ref),
        points_ref[...],
    ]
    place = 0
    for part in sent:
        rows = slice(place, place + part.shape[0])
        message_ref[rows, :] = part
        local_ref[rows, :] = part
        place += part.shape[0]
    for block in range(local // LANES):
        local_ref[place : place + dim, :] = coords_ref[:, block * LANES : (block + 1) * LANES]
        place += dim
    table = count_rows(near_ref, far_ref)
    local_ref[place : place + 16, :] = jnp.concatenate([table, table], axis=0).astype(bf16)


def joined_kernel(mine_ref, other_ref, leaf_ref, node_ref, upper_ref, out_ref, *message_refs):
    half = mine_ref.shape[0]
    columns = LANES // LEAVES
    result = mine_ref[...] + other_ref[...]
    flat = result.T.astype(bf16)
    charges = [flat[0:columns], flat[columns:]]
    out_ref[...] = jnp.concatenate(charges, axis=1)
    rows = skeleton_rows(charges, leaf_ref, node_ref, upper_ref)
    for message_ref in message_refs:
        message_ref[0:half, :] = result.astype(bf16)
        message_ref[half : half + LANES, :] = rows


def added_kernel(mine_ref, other_ref, out_ref):
    columns = LANES // LEAVES
    flat = (mine_ref[...] + other_ref[...]).T.astype(bf16)
    out_ref[...] = jnp.concatenate([flat[0:columns], flat[columns:]], axis=1)


def stage_kernel(stage, *refs):
    ring, near_spots, blocks_at, far_spots, n_sub, dim, points, begins, first, last, near, far = stage
    refs = list(refs)
    spots = sorted(set(near_spots) | set(far_spots))
    makes_near, makes_far = near != "use", far != "use" and bool(far_spots)
    adds = near != "only"
    if begins:
        local_refs = refs.pop(0), refs.pop(0)
        charge_refs = skeleton_refs = {spots[0]: local_refs[0]}
    else:
        table_refs = refs.pop(0), refs.pop(0)
        place_refs = {}
        for spot, indices in zip(near_spots, blocks_at):
            place_refs[spot] = [refs.pop(0).at[index] for index in indices]
        skeleton_refs = {spot: refs.pop(0) for spot in far_spots} if makes_far else {}
        charge_refs = {spot: refs.pop(0) for spot in spots} if adds else {}
    kept_refs = {}
    far_kept_ref = None
    if near == "use":
        kept_refs = {spot: refs.pop(0) for spot in near_spots}
    if far == "use" and far_spots:
        far_kept_ref = refs.pop(0)
    if (makes_near or makes_far) and not begins:
        targets_ref = refs.pop(0)
    if not first and adds:
        refs.pop(0), refs.pop(0)
    upper_points_ref = refs.pop(0) if last and makes_far else None
    if begins:
        targets_ref = refs.pop(0)
        table_refs = refs.pop(0), refs.pop(0)
    if near in ("keep", "only"):
        kept_refs = {spot: refs.pop(0) for spot in near_spots}
    if far == "keep" and far_spots:
        far_kept_ref = refs.pop(0)
    if last and adds:
        half_refs = refs.pop(0), refs.pop(0)
    if adds:
        total_ref, sums_ref, far_charges_ref, charges_ref = (refs.pop(0) for _ in range(4))
    near_ref = refs.pop(0) if makes_near else None
    far_ref = refs.pop(0) if makes_far else None

    skeletons_at = points + LANES
    blocks = points // LANES
    low_half = in_low_half((LANES, LANES))
    lane = lax.broadcasted_iota(i32, (8, LANES), 1)

    def span_of(leaf):
        return slice(leaf * points, (leaf + 1) * points)

    def local_points(ref, leaf):
        begin = skeletons_at + dim + leaf * blocks * dim
        rows = [begin + block * dim for block in range(blocks)]
        return jnp.concatenate([ref[row : row + dim, :] for row in rows], axis=1)

    def points_of(spot, leaf):
        if begins:
            return local_points(local_refs[0], leaf)
        found = [ref[:, span_of(leaf)] for ref in place_refs[spot]]
        if len(found) == 1:
            return found[0]
        hop = (spot + 1) // 2
        first_to_even = (place_on(ring) + hop) % 2 == 1
        chosen = jnp.where(first_to_even == (spot % 2 == 0), 1.0, 0.0).astype(f32)
        chosen = jnp.full((1, 1), chosen, f32)
        return found[0] * chosen.astype(bf16) + found[1] * (1.0 - chosen).astype(bf16)

    if begins:
        begin = skeletons_at + dim + LEAVES * blocks * dim
        for core, ref in enumerate(local_refs):
            table_refs[core][...] = ref[begin : begin + 16, :].astype(f32)[0:8]
            for leaf in range(LEAVES):
                targets_ref[core, span_of(leaf), :] = target_rows(local_points(ref, leaf))
    if first:
        total_ref[...] = jnp.zeros_like(total_ref)
        sums_ref[...] = jnp.zeros_like(sums_ref)

    def table_of(core):
        mine, other = (ref[...] for ref in table_refs)
        return jnp.where(core == 0, mine, other)

    def picked(table, entry):
        return jnp.sum(jnp.where(lane == entry, table, 0.0), axis=1, keepdims=True)

    def values(makes, core, sources_ref, kept_ref):
        if not makes:
            return kept_ref[...]
        made = kernel_values(targets_ref[core], sources_ref[...])
        if kept_ref is not None:
            kept_ref[...] = made
        return made

    devices = {spot: device_of(ring, spot) for spot in spots}

    def near_part(turn, spot, core, leaf):
        at = near_spots.index(spot)
        table = table_of(core)
        named = [
            picked(table, devices[spot] * LEAVES + which)[0:LEAVES] for which in range(LEAVES)
        ]
        if leaf is None:
            second = jnp.where(jnp.sum(named[1], axis=0, keepdims=True) > 0.0, 1.0, 0.0)
        else:
            second = jnp.full((1, 1), float(leaf), f32)
        times = named[0] * (1.0 - second) + named[1] * second
        if makes_near:
            low, high = (points_of(spot, which) for which in range(LEAVES))
            chosen = low * (1.0 - second).astype(bf16) + high * second.astype(bf16)
            put_sources(near_ref.at[at], chosen)
        kept = kept_refs[spot].at[turn] if kept_refs else None
        kernel = values(makes_near, core, near_ref.at[at] if makes_near else None, kept)
        if not adds:
            return None
        half = jnp.where(lane[0:1] < LANES // LEAVES, 1.0 - second, second).astype(bf16)
        charges_ref[at] = charge_refs[spot][0:points, :] * half
        added = matmul(kernel, charges_ref[at])
        return [times[own : own + 1] * added[span_of(own)] for own in range(LEAVES)]

    weights = []
    skeletons = []
    for spot in far_spots:
        rows = charge_refs[spot][points : points + LANES, :].astype(f32)
        weights.append((jnp.where(low_half, rows, swapped(rows)), devices[spot]))
        sums_ref[devices[spot] // BRANCH] += rows
        if makes_far:
            skeletons.append(skeleton_refs[spot][skeletons_at : skeletons_at + dim, :])
    if last and adds:
        for sub in range(n_sub):
            rows = sums_ref[sub]
            weights.append((jnp.where(low_half, swapped(rows), rows), len(ring) * CORES + sub))
            if makes_far:
                skeletons.append(upper_points_ref[:, sub * LANES : (sub + 1) * LANES])
    if makes_far:
        put_sources(far_ref, jnp.concatenate(skeletons, axis=1))

    def far_part(core):
        table = table_of(core)
        kernel = values(
            makes_far,
            core,
            far_ref if makes_far else None,
            None if far_kept_ref is None else far_kept_ref.at[core],
        )
        added = []
        for own in range(LEAVES):
            for position, (block, node) in enumerate(weights):
                scaled = block * picked(table, node)[LEAVES + own : LEAVES + own + 1]
                high = scaled.astype(bf16).astype(f32)
                rows = slice(position * LANES, (position + 1) * LANES)
                far_charges_ref[own, rows, :] = jnp.where(low_half, high, scaled - high).astype(bf16)
            added.append(matmul(kernel[span_of(own)], far_charges_ref[own]))
        return added

    def add(core, parts):
        for own in range(LEAVES):
            total = total_ref[core, span_of(own), :]
            for part in parts:
                total = total + part[own]
            total_ref[core, span_of(own), :] = total

    if first:
        for leaf in range(LEAVES):
            add(0, [near_part(leaf, 0, 0, leaf)])
        add(1, [near_part(LEAVES, 0, 1, None), far_part(1)])
    else:

        def step(core, carry):
            parts = [near_part(core, spot, core, None) for spot in near_spots]
            if adds:
                add(core, parts + ([far_part(core)] if far_spots else []))
            return carry

        lax.fori_loop(0, CORES, step, 0)

    if last and adds:
        for core, ref in enumerate(half_refs):
            both = [total_ref[core, span_of(leaf), :] for leaf in range(LEAVES)]
            both = [total + swapped(total) for total in both]
            ref[...] = jnp.where(in_low_half(both[0].shape), both[0], both[1])


def gate_kernel(message_ref, after_ref, out_ref):
    pass


def gated(message, after):
    anywhere = pl.BlockSpec(memory_space=pl.ANY)
    return pl.pallas_call(
        gate_kernel,
        out_shape=jax.ShapeDtypeStruct(message.shape, message.dtype),
        in_specs=[anywhere] * 2,
        out_specs=anywhere,
        input_output_aliases={0: 0},
        compiler_params=pltpu.CompilerParams(vmem_limit_bytes=2**20),
    )(message, after)


def call(body, args, out_shapes, streamed=(), scratch=(), aliases={}, flops=0, vmem_mib=16):
    vmem = pl.BlockSpec(memory_space=pltpu.VMEM)
    specs = []
    for place, arg in enumerate(args):
        if arg.dtype == i32:
            specs.append(pl.BlockSpec(memory_space=pltpu.SMEM))
        elif place in streamed:
            specs.append(pl.BlockSpec(arg.shape, lambda i: (0,) * 2))
        else:
            specs.append(vmem)
    moved = sum(arg.size * arg.dtype.itemsize for arg in args)
    return pl.pallas_call(
        body,
        grid=(1,),
        out_shape=out_shapes,
        in_specs=specs,
        out_specs=[vmem for _ in out_shapes],
        scratch_shapes=list(scratch),
        input_output_aliases=aliases,
        compiler_params=pltpu.CompilerParams(vmem_limit_bytes=vmem_mib * 1024 * 1024),
        cost_estimate=pl.CostEstimate(flops=flops, bytes_accessed=moved, transcendentals=0),
    )(*args)


def ring_order(chips):
    if chips == 8:
        return [0, 2, 4, 6, 7, 5, 3, 1]
    return list(range(chips))


def on_device(
    coords,
    charges,
    near_lists,
    far_lists,
    leaf_interp,
    node_interp,
    upper_interp,
    node_points,
    upper_points,
):
    dim, local = coords.shape
    columns = charges.shape[0]
    points = local // LEAVES
    peers = lax.axis_size("leaf")
    n_sub = peers // BRANCH
    ring = ring_order(peers // CORES)
    chips = len(ring)

    def along(step):
        return [
            (ring[place] * CORES + core, ring[(place + step * (1 - 2 * core)) % chips] * CORES + core)
            for place in range(chips)
            for core in range(CORES)
        ]

    one_way = functools.partial(lax.ppermute, axis_name="leaf", perm=along(1))
    other_way = functools.partial(lax.ppermute, axis_name="leaf", perm=along(-1))
    to_sibling = functools.partial(
        lax.ppermute, axis_name="leaf", perm=[(device, device ^ 1) for device in range(peers)]
    )

    def shape(*extent, dtype=bf16):
        return jax.ShapeDtypeStruct(extent, dtype)

    maps = [leaf_interp, node_interp, upper_interp]
    def swap(turn):
        pairs = []
        for place, chip in enumerate(ring):
            for core in range(CORES):
                step = 1 if (place + core + turn) % 2 == 0 else -1
                pairs.append((chip * CORES + core, ring[(place + step) % chips] * CORES + core))
        return functools.partial(lax.ppermute, axis_name="leaf", perm=pairs)

    mine = coords[None]
    partner = swap(0)(mine)
    message, own = call(
        message_kernel,
        [near_lists, far_lists, coords, charges, node_points] + maps,
        [
            shape(points + LANES + dim, LANES),
            shape(points + LANES + dim + LEAVES * points // LANES * dim + 16, LANES),
        ],
        streamed=range(2, 8),
        vmem_mib=60,
    )
    sibling_own = to_sibling(own)
    sent = one_way(message), other_way(message)
    pair = swap(1)(jnp.concatenate([mine, partner], axis=0))

    total_shape = shape(CORES, local, LANES, dtype=f32)
    sums_shape = shape(n_sub, LANES, LANES, dtype=f32)
    half_shape = shape(points, LANES, dtype=f32)
    targets_shape = shape(CORES, local, LANES)

    steps = LEAVES + 1 + CORES * (chips - 1)
    kept_bytes = 2 * points * (steps * local + CORES * LEAVES * (chips + n_sub) * LANES)
    keeping = kept_bytes <= KEPT_MIB * 2**20

    def stage(near_spots, far_spots, given, carried, last, near, far, begins=False):
        adds = near != "only"
        blocks_at = ((),) * len(near_spots)
        first = not carried and adds
        makes_near, makes_far = near != "use", far != "use" and bool(far_spots)
        spots = sorted(set(near_spots) | set(far_spots))
        if begins:
            args = [own, sibling_own]
        else:
            args = list(given["tables"])
            if makes_near:
                blocks_at = tuple(tuple(at for _, at in given["places"][spot]) for spot in near_spots)
                args += [block for spot in near_spots for block, _ in given["places"][spot]]
            args += [given["skeletons"][spot] for spot in far_spots] if makes_far else []
            args += [given["charges"][spot] for spot in spots] if adds else []
        args += [given["near"][spot] for spot in near_spots] if near == "use" else []
        args += [given["far"][far_spots]] if far == "use" and far_spots else []
        args += [given["targets"]] if (makes_near or makes_far) and not begins else []
        carried_at = len(args)
        args += carried
        args += [upper_points] if last and makes_far else []
        far_width = max(LANES, LANES * (len(far_spots) + (n_sub if last else 0)))
        scratch = []
        if adds:
            scratch += [
                pltpu.VMEM((LEAVES, far_width, LANES), bf16),
                pltpu.VMEM((len(near_spots), points, LANES), bf16),
            ]
        scratch += [pltpu.VMEM((len(near_spots), LANES, points), bf16)] if makes_near else []
        scratch += [pltpu.VMEM((LANES, far_width), bf16)] if makes_far else []
        names, outs = [], []
        if begins:
            names += ["targets", "mine", "other"]
            outs += [targets_shape] + [shape(8, LANES, dtype=f32)] * CORES
        if near in ("keep", "only"):
            names += [("near", spot) for spot in near_spots]
            outs += [shape(LEAVES + 1 if first else CORES, local, points) for _ in near_spots]
        if far == "keep" and far_spots:
            names += [("far", far_spots)]
            outs += [shape(CORES, local, far_width)]
        if last and adds:
            names += ["mine", "other"]
            outs += [half_shape, half_shape]
        aliases = {carried_at + k: len(outs) + k for k in range(len(carried))}
        if adds:
            names += ["total", "sums"]
            outs += [total_shape, sums_shape]
        static = (ring, near_spots, blocks_at, far_spots, n_sub, dim, points)
        static += (begins, first, last, near, far)
        results = call(
            functools.partial(stage_kernel, static),
            args,
            outs,
            scratch=scratch,
            aliases=aliases,
            flops=len(near_spots) * (2 if makes_near else 1) * 10**9,
        )
        return dict(zip(names, results))

    def far_spots_of(spot):
        return (spot - 1, spot) if spot % 2 == 0 and spot > 0 else (spot,)

    mode = "keep" if keeping else "make"
    given = {"near": {}, "far": {}, "places": {0: [(mine, 0)]}, "skeletons": {0: message}}
    given["charges"] = given["skeletons"]

    def keep_results(results):
        for name, value in results.items():
            if isinstance(name, tuple):
                given[name[0]][name[1]] = value
        return [results["total"], results["sums"]]

    results = stage((0,), (0,), given, [], False, mode, mode, begins=True)
    given["targets"], given["tables"] = results["targets"], [results["mine"], results["other"]]
    carried = keep_results(results)
    arrivals = [(partner, 0), (pair, 0), (pair, 1)]
    for hop in range(1, chips // 2):
        final = hop == chips // 2 - 1
        spots = (2 * hop - 1, 2 * hop)
        sent = [gated(part, carried[1]) for part in sent]
        if not final:
            pair = gated(pair, carried[1])
            arrivals[-2:] = [(pair, 0), (pair, 1)]
        for at, spot in enumerate(spots):
            given["places"][spot] = arrivals[2 * hop - 2 : 2 * hop]
            given["skeletons"][spot] = sent[at]
        sent = one_way(sent[0]), None if final else other_way(sent[1])
        if not final:
            pair = swap(hop + 1)(pair)
            arrivals += [(pair, 0), (pair, 1)]
        carried = keep_results(stage(spots, spots, given, carried, False, mode, mode))
    across = (chips - 1,)
    given["places"][across[0]], given["skeletons"][across[0]] = arrivals[-1:], sent[0]
    near = mode
    if keeping:
        near = "use"
        results = stage(across, (), given, [], False, "only", "use")
        given["near"][across[0]] = results[("near", across[0])]
    results = stage(across, across, given, carried, True, near, mode)
    keep_results(results)
    first, message, again = call(
        joined_kernel,
        [results["mine"], to_sibling(results["other"])] + maps,
        [shape(columns, local)] + [shape(points + LANES, LANES)] * 2,
    )

    mode = "use" if keeping else "make"
    given["charges"] = {}
    carried = []

    def arrived(spot, message):
        nonlocal carried
        given["charges"][spot] = message
        last = spot == chips - 1
        far_spots = () if spot % 2 == 1 and not last else far_spots_of(spot)
        results = stage((spot,), far_spots, given, carried, last, mode, mode)
        carried = [results["total"], results["sums"]]
        return results

    one = one_way(message)
    arrived(0, message)
    other = other_way(gated(again, carried[1]))
    for hop in range(1, chips // 2):
        one_next = one_way(one)
        arrived(2 * hop - 1, one)
        other_next = None
        if hop < chips // 2 - 1:
            other = gated(other, carried[1])
            other_next = other_way(other)
        arrived(2 * hop, other)
        one, other = one_next, other_next
    results = arrived(chips - 1, one)
    (second,) = call(
        added_kernel, [results["mine"], to_sibling(results["other"])], [shape(columns, local)]
    )
    return (first, second)


def solution(mesh):
    placed = (
        P(None, ("groups", "leaf")),
        P(None, ("groups", "leaf")),
        P(("groups", "leaf"), None),
        P(("groups", "leaf"), None),
        P(("groups", "leaf"), None),
        P(("groups", "leaf"), None),
        P(("groups", "leaf"), None),
        P(None, ("groups", "leaf")),
        P(None, "groups"),
    )
    return jax.shard_map(
        on_device,
        mesh=mesh,
        in_specs=placed,
        out_specs=(P(None, ("groups", "leaf")), P(None, ("groups", "leaf"))),
        check_vma=False,
    )
```

```python
import functools

import jax
import jax.numpy as jnp
from jax import lax
from jax.experimental import pallas as pl
from jax.experimental.pallas import tpu as pltpu
from jax.sharding import PartitionSpec as P

BRANCH = 16
EXTRA = 16
LANES = 128
CORES = 2
LEAVES = 2
KEPT_MIB = 30

bf16 = jnp.bfloat16
f32 = jnp.float32
i32 = jnp.int32


def matmul(left, right):
    return jnp.dot(left, right, preferred_element_type=f32)


def square_parts(points):
    minus = -jnp.sum(points * points, axis=0, keepdims=True)
    high = minus.astype(bf16).astype(f32)
    rest = minus - high
    middle = rest.astype(bf16).astype(f32)
    low = rest - middle
    return high, middle, low


def extra_rows(parts, first, width):
    row = lax.broadcasted_iota(i32, (EXTRA, width), 0)
    rows = jnp.where(row < 6, 1.0, 0.0).astype(f32)
    for offset, part in enumerate(parts):
        rows = jnp.where(row == first + offset, jnp.broadcast_to(part, (EXTRA, width)), rows)
    return rows


def put_sources(sources_ref, points):
    dim, width = points.shape
    sources_ref[0:dim, :] = points
    parts = square_parts(points.astype(f32))
    sources_ref[dim : dim + EXTRA, :] = extra_rows(parts, 3, width).astype(bf16)
    sources_ref[dim + EXTRA :, :] = jnp.zeros((LANES - dim - EXTRA, width), bf16)


def target_rows(points):
    dim, width = points.shape
    points = points.astype(f32)
    extra = extra_rows(square_parts(points), 0, width)
    blank = jnp.zeros((LANES - dim - EXTRA, width), f32)
    return jnp.concatenate([2.0 * points, extra, blank], axis=0).T.astype(bf16)


def in_low_half(shape):
    return lax.broadcasted_iota(i32, shape, 1) < LANES // 2


def swapped(values):
    return pltpu.roll(values, LANES // 2, 1)


def kernel_values(targets, sources):
    return jnp.exp(matmul(targets, sources)).astype(bf16)


def skeleton_rows(charges, leaf_ref, node_ref, upper_ref):
    points = charges[0].shape[1]
    parts = []
    for leaf, block in enumerate(charges):
        span = slice(leaf * points, (leaf + 1) * points)
        parts.append(matmul(block, leaf_ref[span, :]).astype(bf16))
    weights = matmul(jnp.concatenate(parts, axis=1), node_ref[...]).astype(bf16)
    term = matmul(weights, upper_ref[...])
    return jnp.concatenate([weights.astype(f32), term], axis=0).T.astype(bf16)


def count_rows(near_ref, far_ref):
    shape = (8, LANES)
    row, lane = lax.broadcasted_iota(i32, shape, 0), lax.broadcasted_iota(i32, shape, 1)
    table = jnp.zeros(shape, f32)
    for leaf in range(LEAVES):
        for first, ref in ((0, near_ref), (LEAVES, far_ref)):
            for slot in range(ref.shape[1]):
                hit = (row == first + leaf) & (lane == ref[leaf, slot])
                table = table + jnp.where(hit, 1.0, 0.0)
    return table


def device_of(ring, spot):
    chips = len(ring)
    me = lax.axis_index("leaf")
    core = me % CORES
    place = jnp.int32(0)
    for at, chip in enumerate(ring):
        place = jnp.where(me // CORES == chip, at, place)
    hop = (spot + 1) // 2
    step = hop if spot % 2 == 0 else -hop
    met = (place + step * (1 - 2 * core) + chips) % chips
    device = jnp.int32(0)
    for at, chip in enumerate(ring):
        device = jnp.where(met == at, chip * CORES + core, device)
    return device


def message_kernel(
    near_ref,
    far_ref,
    coords_ref,
    charges_ref,
    points_ref,
    leaf_ref,
    node_ref,
    upper_ref,
    message_ref,
    local_ref,
    table_ref,
):
    dim, local = coords_ref.shape
    half = local // LEAVES
    charges = [charges_ref[:, 0:half], charges_ref[:, half:]]
    sent = [
        jnp.concatenate(charges, axis=0).astype(f32).T.astype(bf16),
        skeleton_rows(charges, leaf_ref, node_ref, upper_ref),
        points_ref[...],
    ]
    place = 0
    for part in sent:
        rows = slice(place, place + part.shape[0])
        message_ref[rows, :] = part
        local_ref[rows, :] = part
        place += part.shape[0]
    for block in range(local // LANES):
        local_ref[place : place + dim, :] = coords_ref[:, block * LANES : (block + 1) * LANES]
        place += dim
    table = count_rows(near_ref, far_ref)
    table_ref[...] = table
    local_ref[place : place + 16, :] = jnp.concatenate([table, table], axis=0).astype(bf16)


def joined_kernel(mine_ref, other_ref, leaf_ref, node_ref, upper_ref, out_ref, *message_refs):
    half = mine_ref.shape[0]
    columns = LANES // LEAVES
    result = mine_ref[...] + other_ref[...]
    flat = result.T.astype(bf16)
    charges = [flat[0:columns], flat[columns:]]
    out_ref[...] = jnp.concatenate(charges, axis=1)
    rows = skeleton_rows(charges, leaf_ref, node_ref, upper_ref)
    for message_ref in message_refs:
        message_ref[0:half, :] = result.astype(bf16)
        message_ref[half : half + LANES, :] = rows


def added_kernel(mine_ref, other_ref, out_ref):
    columns = LANES // LEAVES
    flat = (mine_ref[...] + other_ref[...]).T.astype(bf16)
    out_ref[...] = jnp.concatenate([flat[0:columns], flat[columns:]], axis=1)


def stage_kernel(stage, *refs):
    ring, near_spots, far_spots, n_sub, dim, points, begins, first, last, mode = stage
    refs = list(refs)
    use, keep = mode == "use", mode == "keep"
    spots = sorted(set(near_spots) | set(far_spots))
    makes = not use
    table_refs = [refs.pop(0) for _ in range(1 if begins else CORES)]
    if begins:
        local_ref = refs.pop(0)
        charge_refs = skeleton_refs = {spots[0]: local_ref}
    else:
        place_refs = {spot: refs.pop(0) for spot in near_spots} if makes else {}
        skeleton_refs = {spot: refs.pop(0) for spot in far_spots} if makes else {}
        charge_refs = {spot: refs.pop(0) for spot in spots}
    kept_refs = {}
    far_kept_ref = None
    if use:
        kept_refs = {spot: refs.pop(0) for spot in near_spots}
        far_kept_ref = refs.pop(0) if far_spots else None
    if begins:
        sibling_ref = refs.pop(0)
    elif makes:
        targets_ref = refs.pop(0)
    if not first:
        refs.pop(0), refs.pop(0)
    upper_points_ref = refs.pop(0) if last and makes else None
    if begins:
        targets_ref, table_ref = refs.pop(0), refs.pop(0)
    if keep:
        kept_refs = {spot: refs.pop(0) for spot in near_spots}
        far_kept_ref = refs.pop(0) if far_spots else None
    if last:
        half_refs = refs.pop(0), refs.pop(0)
    total_ref, sums_ref, far_charges_ref, charges_ref = refs[:4]
    if makes:
        near_ref, far_ref = refs[4:]

    skeletons_at = points + LANES
    blocks = points // LANES
    low_half = in_low_half((LANES, LANES))
    lane = lax.broadcasted_iota(i32, (8, LANES), 1)

    def span_of(leaf):
        return slice(leaf * points, (leaf + 1) * points)

    def points_of(spot, leaf):
        if not begins:
            return place_refs[spot][:, span_of(leaf)]
        begin = skeletons_at + dim + leaf * blocks * dim
        rows = [begin + block * dim for block in range(blocks)]
        return jnp.concatenate([local_ref[row : row + dim, :] for row in rows], axis=1)

    if begins:
        begin = skeletons_at + dim + LEAVES * blocks * dim
        table_ref[...] = local_ref[begin : begin + 16, :].astype(f32)[0:8]
        table_refs = [table_ref] + table_refs
        for leaf in range(LEAVES):
            targets_ref[0, span_of(leaf), :] = target_rows(points_of(0, leaf))
            targets_ref[1, span_of(leaf), :] = target_rows(sibling_ref[:, span_of(leaf)])
    if first:
        total_ref[...] = jnp.zeros_like(total_ref)
        sums_ref[...] = jnp.zeros_like(sums_ref)

    def table_of(core):
        return table_refs[core][...]

    def picked(table, entry):
        return jnp.sum(jnp.where(lane == entry, table, 0.0), axis=1, keepdims=True)

    def values(core, sources_ref, kept_ref):
        if use:
            return kept_ref[...]
        made = kernel_values(targets_ref[core], sources_ref[...])
        if kept_ref is not None:
            kept_ref[...] = made
        return made

    devices = {spot: device_of(ring, spot) for spot in spots}

    def near_part(turn, spot, core, leaf):
        at = core * len(near_spots) + near_spots.index(spot)
        table = table_of(core)
        named = [
            picked(table, devices[spot] * LEAVES + which)[0:LEAVES] for which in range(LEAVES)
        ]
        if leaf is None:
            second = jnp.where(jnp.sum(named[1], axis=0, keepdims=True) > 0.0, 1.0, 0.0)
        else:
            second = jnp.full((1, 1), float(leaf), f32)
        times = named[0] * (1.0 - second) + named[1] * second
        if makes:
            low, high = (points_of(spot, which) for which in range(LEAVES))
            chosen = low * (1.0 - second).astype(bf16) + high * second.astype(bf16)
            put_sources(near_ref.at[at], chosen)
        half = jnp.where(lane[0:1] < LANES // LEAVES, 1.0 - second, second).astype(bf16)
        charges_ref[at] = charge_refs[spot][0:points, :] * half
        kept = kept_refs[spot].at[turn] if kept_refs else None
        added = matmul(values(core, near_ref.at[at] if makes else None, kept), charges_ref[at])
        return [times[own : own + 1] * added[span_of(own)] for own in range(LEAVES)]

    weights = []
    skeletons = []
    for spot in far_spots:
        rows = charge_refs[spot][points : points + LANES, :].astype(f32)
        weights.append((jnp.where(low_half, rows, swapped(rows)), devices[spot]))
        sums_ref[devices[spot] // BRANCH] += rows
        if makes:
            skeletons.append(skeleton_refs[spot][skeletons_at : skeletons_at + dim, :])
    if last:
        for sub in range(n_sub):
            rows = sums_ref[sub]
            weights.append((jnp.where(low_half, swapped(rows), rows), len(ring) * CORES + sub))
            if makes:
                skeletons.append(upper_points_ref[:, sub * LANES : (sub + 1) * LANES])
    if far_spots and makes:
        put_sources(far_ref, jnp.concatenate(skeletons, axis=1))

    def far_part(core):
        table = table_of(core)
        kernel = values(
            core,
            far_ref if makes else None,
            None if far_kept_ref is None else far_kept_ref.at[core],
        )
        added = []
        for own in range(LEAVES):
            for position, (block, node) in enumerate(weights):
                scaled = block * picked(table, node)[LEAVES + own : LEAVES + own + 1]
                high = scaled.astype(bf16).astype(f32)
                rows = slice(position * LANES, (position + 1) * LANES)
                far_charges_ref[core * LEAVES + own, rows, :] = jnp.where(low_half, high, scaled - high).astype(bf16)
            added.append(matmul(kernel[span_of(own)], far_charges_ref[core * LEAVES + own]))
        return added

    def add(core, parts):
        for own in range(LEAVES):
            total = total_ref[core, span_of(own), :]
            for part in parts:
                total = total + part[own]
            total_ref[core, span_of(own), :] = total

    if first:
        for leaf in range(LEAVES):
            add(0, [near_part(leaf, 0, 0, leaf)])
        add(1, [near_part(LEAVES, 0, 1, None), far_part(1)])
    else:

        for core in range(CORES):
            parts = [near_part(core, spot, core, None) for spot in near_spots]
            add(core, parts + ([far_part(core)] if far_spots else []))

    if last:
        for core, ref in enumerate(half_refs):
            both = [total_ref[core, span_of(leaf), :] for leaf in range(LEAVES)]
            both = [total + swapped(total) for total in both]
            ref[...] = jnp.where(in_low_half(both[0].shape), both[0], both[1])


def gate_kernel(message_ref, after_ref, out_ref):
    pass


def gated(message, after):
    anywhere = pl.BlockSpec(memory_space=pl.ANY)
    return pl.pallas_call(
        gate_kernel,
        out_shape=jax.ShapeDtypeStruct(message.shape, message.dtype),
        in_specs=[anywhere] * 2,
        out_specs=anywhere,
        input_output_aliases={0: 0},
        compiler_params=pltpu.CompilerParams(vmem_limit_bytes=2**20),
    )(message, after)


def call(body, args, out_shapes, streamed=(), scratch=(), aliases={}, flops=0, vmem_mib=16):
    vmem = pl.BlockSpec(memory_space=pltpu.VMEM)
    specs = []
    for place, arg in enumerate(args):
        if arg.dtype == i32:
            specs.append(pl.BlockSpec(memory_space=pltpu.SMEM))
        elif place in streamed:
            specs.append(pl.BlockSpec(arg.shape, lambda i: (0,) * 2))
        else:
            specs.append(vmem)
    moved = sum(arg.size * arg.dtype.itemsize for arg in args)
    return pl.pallas_call(
        body,
        grid=(1,),
        out_shape=out_shapes,
        in_specs=specs,
        out_specs=[vmem for _ in out_shapes],
        scratch_shapes=list(scratch),
        input_output_aliases=aliases,
        compiler_params=pltpu.CompilerParams(vmem_limit_bytes=vmem_mib * 1024 * 1024),
        cost_estimate=pl.CostEstimate(flops=flops, bytes_accessed=moved, transcendentals=0),
    )(*args)


def ring_order(chips):
    if chips == 8:
        return [0, 2, 4, 6, 7, 5, 3, 1]
    return list(range(chips))


def on_device(
    coords,
    charges,
    near_lists,
    far_lists,
    leaf_interp,
    node_interp,
    upper_interp,
    node_points,
    upper_points,
):
    dim, local = coords.shape
    columns = charges.shape[0]
    points = local // LEAVES
    peers = lax.axis_size("leaf")
    n_sub = peers // BRANCH
    ring = ring_order(peers // CORES)
    chips = len(ring)

    def along(step):
        return [
            (ring[place] * CORES + core, ring[(place + step * (1 - 2 * core)) % chips] * CORES + core)
            for place in range(chips)
            for core in range(CORES)
        ]

    one_way = functools.partial(lax.ppermute, axis_name="leaf", perm=along(1))
    other_way = functools.partial(lax.ppermute, axis_name="leaf", perm=along(-1))
    to_sibling = functools.partial(
        lax.ppermute, axis_name="leaf", perm=[(device, device ^ 1) for device in range(peers)]
    )

    def shape(*extent, dtype=bf16):
        return jax.ShapeDtypeStruct(extent, dtype)

    maps = [leaf_interp, node_interp, upper_interp]
    sibling_coords = to_sibling(coords)
    coords_next = one_way(coords), other_way(coords)
    message, own, table = call(
        message_kernel,
        [near_lists, far_lists, coords, charges, node_points] + maps,
        [
            shape(points + LANES + dim, LANES),
            shape(points + LANES + dim + LEAVES * points // LANES * dim + 16, LANES),
            shape(8, LANES, dtype=f32),
        ],
        streamed=range(2, 8),
        vmem_mib=60,
    )
    sibling_table = to_sibling(table)

    total_shape = shape(CORES, local, LANES, dtype=f32)
    sums_shape = shape(n_sub, LANES, LANES, dtype=f32)
    half_shape = shape(points, LANES, dtype=f32)
    targets_shape = shape(CORES, local, LANES)

    steps = LEAVES + 1 + CORES * (chips - 1)
    kept_bytes = 2 * points * (steps * local + CORES * LEAVES * (chips + n_sub) * LANES)
    keeping = kept_bytes <= KEPT_MIB * 2**20

    def stage(near_spots, far_spots, given, carried, last, mode, begins=False):
        first = not carried
        makes = mode != "use"
        spots = sorted(set(near_spots) | set(far_spots))
        if begins:
            args = [sibling_table, own, sibling_coords]
        else:
            args = list(given["tables"])
            if makes:
                args += [given["places"][spot] for spot in near_spots]
                args += [given["skeletons"][spot] for spot in far_spots]
            args += [given["charges"][spot] for spot in spots]
            if makes:
                args += [given["targets"]]
            else:
                args += [given["near"][spot] for spot in near_spots]
                args += [given["far"][far_spots]] if far_spots else []
        carried_at = len(args)
        args += carried
        args += [upper_points] if last and makes else []
        far_width = max(LANES, LANES * (len(far_spots) + (n_sub if last else 0)))
        scratch = [
            pltpu.VMEM((CORES * LEAVES, far_width, LANES), bf16),
            pltpu.VMEM((CORES * len(near_spots), points, LANES), bf16),
        ]
        if makes:
            scratch += [
                pltpu.VMEM((CORES * len(near_spots), LANES, points), bf16),
                pltpu.VMEM((LANES, far_width), bf16),
            ]
        names, outs = [], []
        if begins:
            names += ["targets", "table"]
            outs += [targets_shape, shape(8, LANES, dtype=f32)]
        if mode == "keep":
            names += [("near", spot) for spot in near_spots]
            outs += [shape(LEAVES + 1 if first else CORES, local, points) for _ in near_spots]
            names += [("far", far_spots)] if far_spots else []
            outs += [shape(CORES, local, far_width)] if far_spots else []
        if last:
            names += ["mine", "other"]
            outs += [half_shape, half_shape]
        aliases = {carried_at + k: len(outs) + k for k in range(len(carried))}
        names += ["total", "sums"]
        outs += [total_shape, sums_shape]
        static = (
            ring, near_spots, far_spots, n_sub, dim, points, begins, first, last, mode
        )
        results = call(
            functools.partial(stage_kernel, static),
            args,
            outs,
            scratch=scratch,
            aliases=aliases,
            flops=len(near_spots) * (2 if makes else 1) * 10**9,
        )
        return dict(zip(names, results))

    def far_spots_of(spot):
        return (spot - 1, spot) if spot % 2 == 0 and spot > 0 else (spot,)

    mode = "keep" if keeping else "make"
    given = {"near": {}, "far": {}, "places": {0: coords}, "skeletons": {0: message}}
    given["charges"] = given["skeletons"]

    def keep_results(results):
        for name, value in results.items():
            if isinstance(name, tuple):
                given[name[0]][name[1]] = value
        return [results["total"], results["sums"]]

    sent = one_way(message), other_way(message)
    results = stage((0,), (0,), given, [], False, mode, begins=True)
    given["targets"], given["tables"] = results["targets"], [results["table"], sibling_table]
    carried = keep_results(results)
    for hop in range(1, chips // 2):
        final = hop == chips // 2 - 1
        spots = (2 * hop - 1, 2 * hop)
        for at, spot in enumerate(spots):
            given["places"][spot] = coords_next[at]
            given["skeletons"][spot] = sent[at]
        coords_next = one_way(coords_next[0]), None if final else other_way(coords_next[1])
        sent = one_way(sent[0]), None if final else other_way(sent[1])
        carried = keep_results(stage(spots, spots, given, carried, False, mode))
    across = (chips - 1,)
    given["places"][across[0]], given["skeletons"][across[0]] = coords_next[0], sent[0]
    results = stage(across, across, given, carried, True, mode)
    keep_results(results)
    first, message, again = call(
        joined_kernel,
        [results["mine"], to_sibling(results["other"])] + maps,
        [shape(columns, local)] + [shape(points + LANES, LANES)] * 2,
    )

    mode = "use" if keeping else "make"
    given["charges"] = {}
    carried = []

    def arrived(spot, message):
        nonlocal carried
        given["charges"][spot] = message
        last = spot == chips - 1
        far_spots = () if spot % 2 == 1 and not last else far_spots_of(spot)
        results = stage((spot,), far_spots, given, carried, last, mode)
        carried = [results["total"], results["sums"]]
        return results

    one = one_way(message)
    arrived(0, message)
    other = other_way(gated(again, carried[1]))
    for hop in range(1, chips // 2):
        one_next = one_way(one)
        arrived(2 * hop - 1, one)
        other_next = None
        if hop < chips // 2 - 1:
            other = gated(other, carried[1])
            other_next = other_way(other)
        arrived(2 * hop, other)
        one, other = one_next, other_next
    results = arrived(chips - 1, one)
    (second,) = call(
        added_kernel, [results["mine"], to_sibling(results["other"])], [shape(columns, local)]
    )
    return (first, second)


def solution(mesh):
    placed = (
        P(None, ("groups", "leaf")),
        P(None, ("groups", "leaf")),
        P(("groups", "leaf"), None),
        P(("groups", "leaf"), None),
        P(("groups", "leaf"), None),
        P(("groups", "leaf"), None),
        P(("groups", "leaf"), None),
        P(None, ("groups", "leaf")),
        P(None, "groups"),
    )
    return jax.shard_map(
        on_device,
        mesh=mesh,
        in_specs=placed,
        out_specs=(P(None, ("groups", "leaf")), P(None, ("groups", "leaf"))),
        check_vma=False,
    )
```

```python
import functools

import jax
import jax.numpy as jnp
from jax import lax
from jax.experimental import pallas as pl
from jax.experimental.pallas import tpu as pltpu
from jax.sharding import PartitionSpec as P

BRANCH = 16
EXTRA = 16
LANES = 128
CORES = 2
LEAVES = 2
KEPT_MIB = 30

bf16 = jnp.bfloat16
f32 = jnp.float32
i32 = jnp.int32


def matmul(left, right):
    return jnp.dot(left, right, preferred_element_type=f32)


def square_parts(points):
    minus = -jnp.sum(points * points, axis=0, keepdims=True)
    high = minus.astype(bf16).astype(f32)
    rest = minus - high
    middle = rest.astype(bf16).astype(f32)
    low = rest - middle
    return high, middle, low


def extra_rows(parts, first, width):
    row = lax.broadcasted_iota(i32, (EXTRA, width), 0)
    rows = jnp.where(row < 6, 1.0, 0.0).astype(f32)
    for offset, part in enumerate(parts):
        rows = jnp.where(row == first + offset, jnp.broadcast_to(part, (EXTRA, width)), rows)
    return rows


def put_sources(sources_ref, points):
    dim, width = points.shape
    sources_ref[0:dim, :] = points
    parts = square_parts(points.astype(f32))
    sources_ref[dim : dim + EXTRA, :] = extra_rows(parts, 3, width).astype(bf16)
    sources_ref[dim + EXTRA :, :] = jnp.zeros((LANES - dim - EXTRA, width), bf16)


def target_rows(points):
    dim, width = points.shape
    points = points.astype(f32)
    extra = extra_rows(square_parts(points), 0, width)
    blank = jnp.zeros((LANES - dim - EXTRA, width), f32)
    return jnp.concatenate([2.0 * points, extra, blank], axis=0).T.astype(bf16)


def in_low_half(shape):
    return lax.broadcasted_iota(i32, shape, 1) < LANES // 2


def swapped(values):
    return pltpu.roll(values, LANES // 2, 1)


def kernel_values(targets, sources):
    return jnp.exp(matmul(targets, sources)).astype(bf16)


def skeleton_rows(charges, leaf_ref, node_ref, upper_ref):
    points = charges[0].shape[1]
    parts = []
    for leaf, block in enumerate(charges):
        span = slice(leaf * points, (leaf + 1) * points)
        parts.append(matmul(block, leaf_ref[span, :]).astype(bf16))
    weights = matmul(jnp.concatenate(parts, axis=1), node_ref[...]).astype(bf16)
    term = matmul(weights, upper_ref[...])
    return jnp.concatenate([weights.astype(f32), term], axis=0).T.astype(bf16)


def count_rows(near_ref, far_ref):
    shape = (8, LANES)
    row, lane = lax.broadcasted_iota(i32, shape, 0), lax.broadcasted_iota(i32, shape, 1)
    table = jnp.zeros(shape, f32)
    for leaf in range(LEAVES):
        for first, ref in ((0, near_ref), (LEAVES, far_ref)):
            for slot in range(ref.shape[1]):
                hit = (row == first + leaf) & (lane == ref[leaf, slot])
                table = table + jnp.where(hit, 1.0, 0.0)
    return table


def device_of(ring, spot):
    chips = len(ring)
    me = lax.axis_index("leaf")
    core = me % CORES
    place = jnp.int32(0)
    for at, chip in enumerate(ring):
        place = jnp.where(me // CORES == chip, at, place)
    hop = (spot + 1) // 2
    step = hop if spot % 2 == 0 else -hop
    met = (place + step * (1 - 2 * core) + chips) % chips
    device = jnp.int32(0)
    for at, chip in enumerate(ring):
        device = jnp.where(met == at, chip * CORES + core, device)
    return device


def message_kernel(
    near_ref,
    far_ref,
    coords_ref,
    charges_ref,
    points_ref,
    leaf_ref,
    node_ref,
    upper_ref,
    message_ref,
    local_ref,
    table_ref,
):
    dim, local = coords_ref.shape
    half = local // LEAVES
    charges = [charges_ref[:, 0:half], charges_ref[:, half:]]
    sent = [
        jnp.concatenate(charges, axis=0).astype(f32).T.astype(bf16),
        skeleton_rows(charges, leaf_ref, node_ref, upper_ref),
        points_ref[...],
    ]
    place = 0
    for part in sent:
        rows = slice(place, place + part.shape[0])
        message_ref[rows, :] = part
        local_ref[rows, :] = part
        place += part.shape[0]
    for block in range(local // LANES):
        local_ref[place : place + dim, :] = coords_ref[:, block * LANES : (block + 1) * LANES]
        place += dim
    table = count_rows(near_ref, far_ref)
    table_ref[...] = table
    local_ref[place : place + 16, :] = jnp.concatenate([table, table], axis=0).astype(bf16)


def joined_kernel(mine_ref, other_ref, leaf_ref, node_ref, upper_ref, out_ref, message_ref):
    half = mine_ref.shape[0]
    columns = LANES // LEAVES
    result = mine_ref[...] + other_ref[...]
    message_ref[0:half, :] = result.astype(bf16)
    flat = result.T.astype(bf16)
    charges = [flat[0:columns], flat[columns:]]
    out_ref[...] = jnp.concatenate(charges, axis=1)
    message_ref[half : half + LANES, :] = skeleton_rows(charges, leaf_ref, node_ref, upper_ref)


def added_kernel(mine_ref, other_ref, out_ref):
    columns = LANES // LEAVES
    flat = (mine_ref[...] + other_ref[...]).T.astype(bf16)
    out_ref[...] = jnp.concatenate([flat[0:columns], flat[columns:]], axis=1)


def stage_kernel(stage, *refs):
    ring, near_spots, far_spots, n_sub, dim, points, begins, first, last, mode = stage
    refs = list(refs)
    use, keep = mode == "use", mode == "keep"
    spots = sorted(set(near_spots) | set(far_spots))
    makes = not use
    table_refs = [refs.pop(0) for _ in range(1 if begins else CORES)]
    if begins:
        local_ref = refs.pop(0)
        charge_refs = skeleton_refs = {spots[0]: local_ref}
    else:
        place_refs = {spot: refs.pop(0) for spot in near_spots} if makes else {}
        skeleton_refs = {spot: refs.pop(0) for spot in far_spots} if makes else {}
        charge_refs = {spot: refs.pop(0) for spot in spots}
    kept_refs = {}
    far_kept_ref = None
    if use:
        kept_refs = {spot: refs.pop(0) for spot in near_spots}
        far_kept_ref = refs.pop(0) if far_spots else None
    if begins:
        sibling_ref = refs.pop(0)
    elif makes:
        targets_ref = refs.pop(0)
    if not first:
        refs.pop(0), refs.pop(0)
    upper_points_ref = refs.pop(0) if last and makes else None
    if begins:
        targets_ref, table_ref = refs.pop(0), refs.pop(0)
    if keep:
        kept_refs = {spot: refs.pop(0) for spot in near_spots}
        far_kept_ref = refs.pop(0) if far_spots else None
    if last:
        half_refs = refs.pop(0), refs.pop(0)
    total_ref, sums_ref, far_charges_ref, charges_ref = refs[:4]
    if makes:
        near_ref, far_ref = refs[4:]

    skeletons_at = points + LANES
    blocks = points // LANES
    low_half = in_low_half((LANES, LANES))
    lane = lax.broadcasted_iota(i32, (8, LANES), 1)

    def span_of(leaf):
        return slice(leaf * points, (leaf + 1) * points)

    def points_of(spot, leaf):
        if not begins:
            return place_refs[spot][:, span_of(leaf)]
        begin = skeletons_at + dim + leaf * blocks * dim
        rows = [begin + block * dim for block in range(blocks)]
        return jnp.concatenate([local_ref[row : row + dim, :] for row in rows], axis=1)

    if begins:
        begin = skeletons_at + dim + LEAVES * blocks * dim
        table_ref[...] = local_ref[begin : begin + 16, :].astype(f32)[0:8]
        table_refs = [table_ref] + table_refs
        for leaf in range(LEAVES):
            targets_ref[0, span_of(leaf), :] = target_rows(points_of(0, leaf))
            targets_ref[1, span_of(leaf), :] = target_rows(sibling_ref[:, span_of(leaf)])
    if first:
        total_ref[...] = jnp.zeros_like(total_ref)
        sums_ref[...] = jnp.zeros_like(sums_ref)

    def table_of(core):
        return table_refs[core][...]

    def picked(table, entry):
        return jnp.sum(jnp.where(lane == entry, table, 0.0), axis=1, keepdims=True)

    def values(core, sources_ref, kept_ref):
        if use:
            return kept_ref[...]
        made = kernel_values(targets_ref[core], sources_ref[...])
        if kept_ref is not None:
            kept_ref[...] = made
        return made

    devices = {spot: device_of(ring, spot) for spot in spots}

    def near_part(turn, spot, core, leaf):
        at = turn if first else core * len(near_spots) + near_spots.index(spot)
        table = table_of(core)
        named = [
            picked(table, devices[spot] * LEAVES + which)[0:LEAVES] for which in range(LEAVES)
        ]
        if leaf is None:
            second = jnp.where(jnp.sum(named[1], axis=0, keepdims=True) > 0.0, 1.0, 0.0)
        else:
            second = jnp.full((1, 1), float(leaf), f32)
        times = named[0] * (1.0 - second) + named[1] * second
        if makes:
            low, high = (points_of(spot, which) for which in range(LEAVES))
            chosen = low * (1.0 - second).astype(bf16) + high * second.astype(bf16)
            put_sources(near_ref.at[at], chosen)
        half = jnp.where(lane[0:1] < LANES // LEAVES, 1.0 - second, second).astype(bf16)
        charges_ref[at] = charge_refs[spot][0:points, :] * half
        kept = kept_refs[spot].at[turn] if kept_refs else None
        added = matmul(values(core, near_ref.at[at] if makes else None, kept), charges_ref[at])
        return [times[own : own + 1] * added[span_of(own)] for own in range(LEAVES)]

    weights = []
    skeletons = []
    for spot in far_spots:
        rows = charge_refs[spot][points : points + LANES, :].astype(f32)
        weights.append((jnp.where(low_half, rows, swapped(rows)), devices[spot]))
        sums_ref[devices[spot] // BRANCH] += rows
        if makes:
            skeletons.append(skeleton_refs[spot][skeletons_at : skeletons_at + dim, :])
    if last:
        for sub in range(n_sub):
            rows = sums_ref[sub]
            weights.append((jnp.where(low_half, swapped(rows), rows), len(ring) * CORES + sub))
            if makes:
                skeletons.append(upper_points_ref[:, sub * LANES : (sub + 1) * LANES])
    if far_spots and makes:
        put_sources(far_ref, jnp.concatenate(skeletons, axis=1))

    def far_part(core):
        table = table_of(core)
        kernel = values(
            core,
            far_ref if makes else None,
            None if far_kept_ref is None else far_kept_ref.at[core],
        )
        added = []
        for own in range(LEAVES):
            for position, (block, node) in enumerate(weights):
                scaled = block * picked(table, node)[LEAVES + own : LEAVES + own + 1]
                high = scaled.astype(bf16).astype(f32)
                rows = slice(position * LANES, (position + 1) * LANES)
                far_charges_ref[core * LEAVES + own, rows, :] = jnp.where(low_half, high, scaled - high).astype(bf16)
            added.append(matmul(kernel[span_of(own)], far_charges_ref[core * LEAVES + own]))
        return added

    def add(core, parts):
        for own in range(LEAVES):
            total = total_ref[core, span_of(own), :]
            for part in parts:
                total = total + part[own]
            total_ref[core, span_of(own), :] = total

    if first:
        for leaf in range(LEAVES):
            add(0, [near_part(leaf, 0, 0, leaf)])
        add(1, [near_part(LEAVES, 0, 1, None), far_part(1)])
    else:

        for core in range(CORES):
            parts = [near_part(core, spot, core, None) for spot in near_spots]
            add(core, parts + ([far_part(core)] if far_spots else []))

    if last:
        for core, ref in enumerate(half_refs):
            both = [total_ref[core, span_of(leaf), :] for leaf in range(LEAVES)]
            both = [total + swapped(total) for total in both]
            ref[...] = jnp.where(in_low_half(both[0].shape), both[0], both[1])


def call(body, args, out_shapes, streamed=(), scratch=(), aliases={}, flops=0, vmem_mib=16):
    vmem = pl.BlockSpec(memory_space=pltpu.VMEM)
    specs = []
    for place, arg in enumerate(args):
        if arg.dtype == i32:
            specs.append(pl.BlockSpec(memory_space=pltpu.SMEM))
        elif place in streamed:
            specs.append(pl.BlockSpec(arg.shape, lambda i: (0,) * 2))
        else:
            specs.append(vmem)
    moved = sum(arg.size * arg.dtype.itemsize for arg in args)
    return pl.pallas_call(
        body,
        grid=(1,),
        out_shape=out_shapes,
        in_specs=specs,
        out_specs=[vmem for _ in out_shapes],
        scratch_shapes=list(scratch),
        input_output_aliases=aliases,
        compiler_params=pltpu.CompilerParams(vmem_limit_bytes=vmem_mib * 1024 * 1024),
        cost_estimate=pl.CostEstimate(flops=flops, bytes_accessed=moved, transcendentals=0),
    )(*args)


def ring_order(chips):
    if chips == 8:
        return [0, 2, 4, 6, 7, 5, 3, 1]
    return list(range(chips))


def on_device(
    coords,
    charges,
    near_lists,
    far_lists,
    leaf_interp,
    node_interp,
    upper_interp,
    node_points,
    upper_points,
):
    dim, local = coords.shape
    columns = charges.shape[0]
    points = local // LEAVES
    peers = lax.axis_size("leaf")
    n_sub = peers // BRANCH
    ring = ring_order(peers // CORES)
    chips = len(ring)

    def along(step):
        return [
            (ring[place] * CORES + core, ring[(place + step * (1 - 2 * core)) % chips] * CORES + core)
            for place in range(chips)
            for core in range(CORES)
        ]

    one_way = functools.partial(lax.ppermute, axis_name="leaf", perm=along(1))
    other_way = functools.partial(lax.ppermute, axis_name="leaf", perm=along(-1))
    to_sibling = functools.partial(
        lax.ppermute, axis_name="leaf", perm=[(device, device ^ 1) for device in range(peers)]
    )

    def shape(*extent, dtype=bf16):
        return jax.ShapeDtypeStruct(extent, dtype)

    maps = [leaf_interp, node_interp, upper_interp]
    sibling_coords = to_sibling(coords)
    coords_next = one_way(coords), other_way(coords)
    message, own, table = call(
        message_kernel,
        [near_lists, far_lists, coords, charges, node_points] + maps,
        [
            shape(points + LANES + dim, LANES),
            shape(points + LANES + dim + LEAVES * points // LANES * dim + 16, LANES),
            shape(8, LANES, dtype=f32),
        ],
        streamed=range(2, 8),
        vmem_mib=60,
    )
    sibling_table = to_sibling(table)

    total_shape = shape(CORES, local, LANES, dtype=f32)
    sums_shape = shape(n_sub, LANES, LANES, dtype=f32)
    half_shape = shape(points, LANES, dtype=f32)
    targets_shape = shape(CORES, local, LANES)

    steps = LEAVES + 1 + CORES * (chips - 1)
    kept_bytes = 2 * points * (steps * local + CORES * LEAVES * (chips + n_sub) * LANES)
    keeping = kept_bytes <= KEPT_MIB * 2**20

    def stage(near_spots, far_spots, given, carried, last, mode, begins=False):
        first = not carried
        makes = mode != "use"
        spots = sorted(set(near_spots) | set(far_spots))
        if begins:
            args = [sibling_table, own, sibling_coords]
        else:
            args = list(given["tables"])
            if makes:
                args += [given["places"][spot] for spot in near_spots]
                args += [given["skeletons"][spot] for spot in far_spots]
            args += [given["charges"][spot] for spot in spots]
            if makes:
                args += [given["targets"]]
            else:
                args += [given["near"][spot] for spot in near_spots]
                args += [given["far"][far_spots]] if far_spots else []
        carried_at = len(args)
        args += carried
        args += [upper_points] if last and makes else []
        far_width = max(LANES, LANES * (len(far_spots) + (n_sub if last else 0)))
        scratch = [
            pltpu.VMEM((CORES * LEAVES, far_width, LANES), bf16),
            pltpu.VMEM((LEAVES + 1 if first else CORES * len(near_spots), points, LANES), bf16),
        ]
        if makes:
            scratch += [
                pltpu.VMEM((LEAVES + 1 if first else CORES * len(near_spots), LANES, points), bf16),
                pltpu.VMEM((LANES, far_width), bf16),
            ]
        names, outs = [], []
        if begins:
            names += ["targets", "table"]
            outs += [targets_shape, shape(8, LANES, dtype=f32)]
        if mode == "keep":
            names += [("near", spot) for spot in near_spots]
            outs += [shape(LEAVES + 1 if first else CORES, local, points) for _ in near_spots]
            names += [("far", far_spots)] if far_spots else []
            outs += [shape(CORES, local, far_width)] if far_spots else []
        if last:
            names += ["mine", "other"]
            outs += [half_shape, half_shape]
        aliases = {carried_at + k: len(outs) + k for k in range(len(carried))}
        names += ["total", "sums"]
        outs += [total_shape, sums_shape]
        static = (
            ring, near_spots, far_spots, n_sub, dim, points, begins, first, last, mode
        )
        results = call(
            functools.partial(stage_kernel, static),
            args,
            outs,
            scratch=scratch,
            aliases=aliases,
            flops=len(near_spots) * (2 if makes else 1) * 10**9,
        )
        return dict(zip(names, results))

    mode = "keep" if keeping else "make"
    given = {"near": {}, "far": {}, "places": {0: coords}, "skeletons": {0: message}}
    given["charges"] = given["skeletons"]

    def keep_results(results):
        for name, value in results.items():
            if isinstance(name, tuple):
                given[name[0]][name[1]] = value
        return [results["total"], results["sums"]]

    sent = one_way(message), other_way(message)
    results = stage((0,), (0,), given, [], False, mode, begins=True)
    given["targets"], given["tables"] = results["targets"], [results["table"], sibling_table]
    carried = keep_results(results)
    for hop in range(1, chips // 2):
        final = hop == chips // 2 - 1
        spots = (2 * hop - 1, 2 * hop)
        for at, spot in enumerate(spots):
            given["places"][spot] = coords_next[at]
            given["skeletons"][spot] = sent[at]
        coords_next = one_way(coords_next[0]), None if final else other_way(coords_next[1])
        sent = one_way(sent[0]), None if final else other_way(sent[1])
        carried = keep_results(stage(spots, spots, given, carried, False, mode))
    across = (chips - 1,)
    given["places"][across[0]], given["skeletons"][across[0]] = coords_next[0], sent[0]
    results = stage(across, across, given, carried, True, mode)
    keep_results(results)
    first, message = call(
        joined_kernel,
        [results["mine"], to_sibling(results["other"])] + maps,
        [shape(columns, local), shape(points + LANES, LANES)],
    )

    mode = "use" if keeping else "make"
    given["charges"] = {0: message}
    sent = one_way(message), other_way(message)
    results = stage((0,), (0,), given, [], False, mode)
    carried = [results["total"], results["sums"]]
    for hop in range(1, chips // 2):
        spots = (2 * hop - 1, 2 * hop)
        for at, spot in enumerate(spots):
            given["charges"][spot] = sent[at]
        sent = one_way(sent[0]), None if hop == chips // 2 - 1 else other_way(sent[1])
        results = stage(spots, spots, given, carried, False, mode)
        carried = [results["total"], results["sums"]]
    given["charges"][across[0]] = sent[0]
    results = stage(across, across, given, carried, True, mode)
    (second,) = call(
        added_kernel, [results["mine"], to_sibling(results["other"])], [shape(columns, local)]
    )
    return (first, second)


def solution(mesh):
    placed = (
        P(None, ("groups", "leaf")),
        P(None, ("groups", "leaf")),
        P(("groups", "leaf"), None),
        P(("groups", "leaf"), None),
        P(("groups", "leaf"), None),
        P(("groups", "leaf"), None),
        P(("groups", "leaf"), None),
        P(None, ("groups", "leaf")),
        P(None, "groups"),
    )
    return jax.shard_map(
        on_device,
        mesh=mesh,
        in_specs=placed,
        out_specs=(P(None, ("groups", "leaf")), P(None, ("groups", "leaf"))),
        check_vma=False,
    )
```

```python
import functools

import jax
import jax.numpy as jnp
from jax import lax
from jax.experimental import pallas as pl
from jax.experimental.pallas import tpu as pltpu
from jax.sharding import PartitionSpec as P

BRANCH = 16
EXTRA = 16
LANES = 128
CORES = 2
LEAVES = 2
KEPT_MIB = 30

bf16 = jnp.bfloat16
f32 = jnp.float32
i32 = jnp.int32


def matmul(left, right):
    return jnp.dot(left, right, preferred_element_type=f32)


def square_parts(points):
    minus = -jnp.sum(points * points, axis=0, keepdims=True)
    high = minus.astype(bf16).astype(f32)
    rest = minus - high
    middle = rest.astype(bf16).astype(f32)
    low = rest - middle
    return high, middle, low


def extra_rows(parts, first, width):
    row = lax.broadcasted_iota(i32, (EXTRA, width), 0)
    rows = jnp.where(row < 6, 1.0, 0.0).astype(f32)
    for offset, part in enumerate(parts):
        rows = jnp.where(row == first + offset, jnp.broadcast_to(part, (EXTRA, width)), rows)
    return rows


def put_sources(sources_ref, points):
    dim, width = points.shape
    sources_ref[0:dim, :] = points
    parts = square_parts(points.astype(f32))
    sources_ref[dim : dim + EXTRA, :] = extra_rows(parts, 3, width).astype(bf16)
    sources_ref[dim + EXTRA :, :] = jnp.zeros((LANES - dim - EXTRA, width), bf16)


def target_rows(points):
    dim, width = points.shape
    points = points.astype(f32)
    extra = extra_rows(square_parts(points), 0, width)
    blank = jnp.zeros((LANES - dim - EXTRA, width), f32)
    return jnp.concatenate([2.0 * points, extra, blank], axis=0).T.astype(bf16)


def in_low_half(shape):
    return lax.broadcasted_iota(i32, shape, 1) < LANES // 2


def swapped(values):
    return pltpu.roll(values, LANES // 2, 1)


def kernel_values(targets, sources):
    return jnp.exp(matmul(targets, sources)).astype(bf16)


def skeleton_rows(charges, leaf_ref, node_ref, upper_ref):
    points = charges[0].shape[1]
    parts = []
    for leaf, block in enumerate(charges):
        span = slice(leaf * points, (leaf + 1) * points)
        parts.append(matmul(block, leaf_ref[span, :]).astype(bf16))
    weights = matmul(jnp.concatenate(parts, axis=1), node_ref[...]).astype(bf16)
    term = matmul(weights, upper_ref[...])
    return jnp.concatenate([weights.astype(f32), term], axis=0).T.astype(bf16)


def count_rows(near_ref, far_ref):
    shape = (8, LANES)
    row, lane = lax.broadcasted_iota(i32, shape, 0), lax.broadcasted_iota(i32, shape, 1)
    table = jnp.zeros(shape, f32)
    for leaf in range(LEAVES):
        for first, ref in ((0, near_ref), (LEAVES, far_ref)):
            for slot in range(ref.shape[1]):
                hit = (row == first + leaf) & (lane == ref[leaf, slot])
                table = table + jnp.where(hit, 1.0, 0.0)
    return table


def device_of(ring, spot):
    chips = len(ring)
    me = lax.axis_index("leaf")
    core = me % CORES
    place = jnp.int32(0)
    for at, chip in enumerate(ring):
        place = jnp.where(me // CORES == chip, at, place)
    hop = (spot + 1) // 2
    step = hop if spot % 2 == 0 else -hop
    met = (place + step * (1 - 2 * core) + chips) % chips
    device = jnp.int32(0)
    for at, chip in enumerate(ring):
        device = jnp.where(met == at, chip * CORES + core, device)
    return device


def message_kernel(
    near_ref,
    far_ref,
    coords_ref,
    charges_ref,
    points_ref,
    leaf_ref,
    node_ref,
    upper_ref,
    message_ref,
    local_ref,
    table_ref,
):
    dim, local = coords_ref.shape
    half = local // LEAVES
    charges = [charges_ref[:, 0:half], charges_ref[:, half:]]
    sent = [
        jnp.concatenate(charges, axis=0).astype(f32).T.astype(bf16),
        skeleton_rows(charges, leaf_ref, node_ref, upper_ref),
        points_ref[...],
    ]
    place = 0
    for part in sent:
        rows = slice(place, place + part.shape[0])
        message_ref[rows, :] = part
        local_ref[rows, :] = part
        place += part.shape[0]
    for block in range(local // LANES):
        local_ref[place : place + dim, :] = coords_ref[:, block * LANES : (block + 1) * LANES]
        place += dim
    table = count_rows(near_ref, far_ref)
    table_ref[...] = table
    local_ref[place : place + 16, :] = jnp.concatenate([table, table], axis=0).astype(bf16)


def joined_kernel(mine_ref, other_ref, leaf_ref, node_ref, upper_ref, out_ref, *message_refs):
    half = mine_ref.shape[0]
    columns = LANES // LEAVES
    result = mine_ref[...] + other_ref[...]
    flat = result.T.astype(bf16)
    charges = [flat[0:columns], flat[columns:]]
    out_ref[...] = jnp.concatenate(charges, axis=1)
    rows = skeleton_rows(charges, leaf_ref, node_ref, upper_ref)
    for message_ref in message_refs:
        message_ref[0:half, :] = result.astype(bf16)
        message_ref[half : half + LANES, :] = rows


def added_kernel(mine_ref, other_ref, out_ref):
    columns = LANES // LEAVES
    flat = (mine_ref[...] + other_ref[...]).T.astype(bf16)
    out_ref[...] = jnp.concatenate([flat[0:columns], flat[columns:]], axis=1)


def stage_kernel(stage, *refs):
    ring, near_spots, far_spots, n_sub, dim, points, begins, first, last, mode = stage
    refs = list(refs)
    use, keep = mode == "use", mode == "keep"
    spots = sorted(set(near_spots) | set(far_spots))
    makes = not use
    table_refs = [refs.pop(0) for _ in range(1 if begins else CORES)]
    if begins:
        local_ref = refs.pop(0)
        charge_refs = skeleton_refs = {spots[0]: local_ref}
    else:
        place_refs = {spot: refs.pop(0) for spot in near_spots} if makes else {}
        skeleton_refs = {spot: refs.pop(0) for spot in far_spots} if makes else {}
        charge_refs = {spot: refs.pop(0) for spot in spots}
    kept_refs = {}
    far_kept_ref = None
    if use:
        kept_refs = {spot: refs.pop(0) for spot in near_spots}
        far_kept_ref = refs.pop(0) if far_spots else None
    if begins:
        sibling_ref = refs.pop(0)
    elif makes:
        targets_ref = refs.pop(0)
    if not first:
        refs.pop(0), refs.pop(0)
    upper_points_ref = refs.pop(0) if last and makes else None
    if begins:
        targets_ref, table_ref = refs.pop(0), refs.pop(0)
    if keep:
        kept_refs = {spot: refs.pop(0) for spot in near_spots}
        far_kept_ref = refs.pop(0) if far_spots else None
    if last:
        half_refs = refs.pop(0), refs.pop(0)
    total_ref, sums_ref, far_charges_ref, charges_ref = refs[:4]
    if makes:
        near_ref, far_ref = refs[4:]

    skeletons_at = points + LANES
    blocks = points // LANES
    low_half = in_low_half((LANES, LANES))
    lane = lax.broadcasted_iota(i32, (8, LANES), 1)

    def span_of(leaf):
        return slice(leaf * points, (leaf + 1) * points)

    def points_of(spot, leaf):
        if not begins:
            return place_refs[spot][:, span_of(leaf)]
        begin = skeletons_at + dim + leaf * blocks * dim
        rows = [begin + block * dim for block in range(blocks)]
        return jnp.concatenate([local_ref[row : row + dim, :] for row in rows], axis=1)

    if begins:
        begin = skeletons_at + dim + LEAVES * blocks * dim
        table_ref[...] = local_ref[begin : begin + 16, :].astype(f32)[0:8]
        table_refs = [table_ref] + table_refs
        for leaf in range(LEAVES):
            targets_ref[0, span_of(leaf), :] = target_rows(points_of(0, leaf))
            targets_ref[1, span_of(leaf), :] = target_rows(sibling_ref[:, span_of(leaf)])
    if first:
        total_ref[...] = jnp.zeros_like(total_ref)
        sums_ref[...] = jnp.zeros_like(sums_ref)

    def table_of(core):
        return table_refs[core][...]

    def picked(table, entry):
        return jnp.sum(jnp.where(lane == entry, table, 0.0), axis=1, keepdims=True)

    def values(core, sources_ref, kept_ref):
        if use:
            return kept_ref[...]
        made = kernel_values(targets_ref[core], sources_ref[...])
        if kept_ref is not None:
            kept_ref[...] = made
        return made

    devices = {spot: device_of(ring, spot) for spot in spots}

    def near_values(turn, spot, core, leaf):
        at = turn if first else core * len(near_spots) + near_spots.index(spot)
        table = table_of(core)
        named = [
            picked(table, devices[spot] * LEAVES + which)[0:LEAVES] for which in range(LEAVES)
        ]
        if leaf is None:
            second = jnp.where(jnp.sum(named[1], axis=0, keepdims=True) > 0.0, 1.0, 0.0)
        else:
            second = jnp.full((1, 1), float(leaf), f32)
        times = named[0] * (1.0 - second) + named[1] * second
        if makes:
            low, high = (points_of(spot, which) for which in range(LEAVES))
            chosen = low * (1.0 - second).astype(bf16) + high * second.astype(bf16)
            put_sources(near_ref.at[at], chosen)
        half = jnp.where(lane[0:1] < LANES // LEAVES, 1.0 - second, second).astype(bf16)
        charges_ref[at] = charge_refs[spot][0:points, :] * half
        kept = kept_refs[spot].at[turn] if kept_refs else None
        return values(core, near_ref.at[at] if makes else None, kept), at, times

    def near_product(core, kernel, at, times):
        added = matmul(kernel, charges_ref[at])
        return [times[own : own + 1] * added[span_of(own)] for own in range(LEAVES)]

    weights = []
    skeletons = []
    for spot in far_spots:
        rows = charge_refs[spot][points : points + LANES, :].astype(f32)
        weights.append((jnp.where(low_half, rows, swapped(rows)), devices[spot]))
        sums_ref[devices[spot] // BRANCH] += rows
        if makes:
            skeletons.append(skeleton_refs[spot][skeletons_at : skeletons_at + dim, :])
    if last:
        for sub in range(n_sub):
            rows = sums_ref[sub]
            weights.append((jnp.where(low_half, swapped(rows), rows), len(ring) * CORES + sub))
            if makes:
                skeletons.append(upper_points_ref[:, sub * LANES : (sub + 1) * LANES])
    if far_spots and makes:
        put_sources(far_ref, jnp.concatenate(skeletons, axis=1))

    def far_values(core):
        table = table_of(core)
        for own in range(LEAVES):
            for position, (block, node) in enumerate(weights):
                scaled = block * picked(table, node)[LEAVES + own : LEAVES + own + 1]
                high = scaled.astype(bf16).astype(f32)
                rows = slice(position * LANES, (position + 1) * LANES)
                far_charges_ref[core * LEAVES + own, rows, :] = jnp.where(
                    low_half, high, scaled - high
                ).astype(bf16)
        kept = None if far_kept_ref is None else far_kept_ref.at[core]
        return (values(core, far_ref if makes else None, kept),)

    def far_product(core, kernel):
        return [
            matmul(kernel[span_of(own)], far_charges_ref[core * LEAVES + own])
            for own in range(LEAVES)
        ]

    def add(core, parts):
        for own in range(LEAVES):
            total = total_ref[core, span_of(own), :]
            for part in parts:
                total = total + part[own]
            total_ref[core, span_of(own), :] = total

    work = []
    for core in range(CORES):
        if first and core == 0:
            wanted = [(leaf, 0, leaf) for leaf in range(LEAVES)]
        elif first:
            wanted = [(LEAVES, 0, None)]
        else:
            wanted = [(core, spot, None) for spot in near_spots]
        for turn, spot, leaf in wanted:
            work.append((core, functools.partial(near_values, turn, spot, core, leaf), near_product))
        if far_spots and not (first and core == 0):
            work.append((core, functools.partial(far_values, core), far_product))
    parts = [[] for _ in range(CORES)]
    waiting = None
    for step in work + [None]:
        found = step[1]() if step else None
        if waiting:
            core, product, ready = waiting
            parts[core].append(product(core, *ready))
            if not step or step[0] != core:
                add(core, parts[core])
        waiting = (step[0], step[2], found) if step else None

    if last:
        for core, ref in enumerate(half_refs):
            both = [total_ref[core, span_of(leaf), :] for leaf in range(LEAVES)]
            both = [total + swapped(total) for total in both]
            ref[...] = jnp.where(in_low_half(both[0].shape), both[0], both[1])


def gate_kernel(message_ref, after_ref, out_ref):
    pass


def gated(message, after):
    anywhere = pl.BlockSpec(memory_space=pl.ANY)
    return pl.pallas_call(
        gate_kernel,
        out_shape=jax.ShapeDtypeStruct(message.shape, message.dtype),
        in_specs=[anywhere] * 2,
        out_specs=anywhere,
        input_output_aliases={0: 0},
        compiler_params=pltpu.CompilerParams(vmem_limit_bytes=2**20),
    )(message, after)


def call(body, args, out_shapes, streamed=(), scratch=(), aliases={}, flops=0, vmem_mib=16):
    vmem = pl.BlockSpec(memory_space=pltpu.VMEM)
    specs = []
    for place, arg in enumerate(args):
        if arg.dtype == i32:
            specs.append(pl.BlockSpec(memory_space=pltpu.SMEM))
        elif place in streamed:
            specs.append(pl.BlockSpec(arg.shape, lambda i: (0,) * 2))
        else:
            specs.append(vmem)
    moved = sum(arg.size * arg.dtype.itemsize for arg in args)
    return pl.pallas_call(
        body,
        grid=(1,),
        out_shape=out_shapes,
        in_specs=specs,
        out_specs=[vmem for _ in out_shapes],
        scratch_shapes=list(scratch),
        input_output_aliases=aliases,
        compiler_params=pltpu.CompilerParams(vmem_limit_bytes=vmem_mib * 1024 * 1024),
        cost_estimate=pl.CostEstimate(flops=flops, bytes_accessed=moved, transcendentals=0),
    )(*args)


def ring_order(chips):
    if chips == 8:
        return [0, 2, 4, 6, 7, 5, 3, 1]
    return list(range(chips))


def on_device(
    coords,
    charges,
    near_lists,
    far_lists,
    leaf_interp,
    node_interp,
    upper_interp,
    node_points,
    upper_points,
):
    dim, local = coords.shape
    columns = charges.shape[0]
    points = local // LEAVES
    peers = lax.axis_size("leaf")
    n_sub = peers // BRANCH
    ring = ring_order(peers // CORES)
    chips = len(ring)

    def along(step):
        return [
            (ring[place] * CORES + core, ring[(place + step * (1 - 2 * core)) % chips] * CORES + core)
            for place in range(chips)
            for core in range(CORES)
        ]

    one_way = functools.partial(lax.ppermute, axis_name="leaf", perm=along(1))
    other_way = functools.partial(lax.ppermute, axis_name="leaf", perm=along(-1))
    to_sibling = functools.partial(
        lax.ppermute, axis_name="leaf", perm=[(device, device ^ 1) for device in range(peers)]
    )

    def shape(*extent, dtype=bf16):
        return jax.ShapeDtypeStruct(extent, dtype)

    maps = [leaf_interp, node_interp, upper_interp]
    sibling_coords = to_sibling(coords)
    coords_next = one_way(coords), other_way(coords)
    message, own, table = call(
        message_kernel,
        [near_lists, far_lists, coords, charges, node_points] + maps,
        [
            shape(points + LANES + dim, LANES),
            shape(points + LANES + dim + LEAVES * points // LANES * dim + 16, LANES),
            shape(8, LANES, dtype=f32),
        ],
        streamed=range(2, 8),
        vmem_mib=60,
    )
    sibling_table = to_sibling(table)

    total_shape = shape(CORES, local, LANES, dtype=f32)
    sums_shape = shape(n_sub, LANES, LANES, dtype=f32)
    half_shape = shape(points, LANES, dtype=f32)
    targets_shape = shape(CORES, local, LANES)

    steps = LEAVES + 1 + CORES * (chips - 1)
    kept_bytes = 2 * points * (steps * local + CORES * LEAVES * (chips + n_sub) * LANES)
    keeping = kept_bytes <= KEPT_MIB * 2**20

    def stage(near_spots, far_spots, given, carried, last, mode, begins=False):
        first = not carried
        makes = mode != "use"
        spots = sorted(set(near_spots) | set(far_spots))
        if begins:
            args = [sibling_table, own, sibling_coords]
        else:
            args = list(given["tables"])
            if makes:
                args += [given["places"][spot] for spot in near_spots]
                args += [given["skeletons"][spot] for spot in far_spots]
            args += [given["charges"][spot] for spot in spots]
            if makes:
                args += [given["targets"]]
            else:
                args += [given["near"][spot] for spot in near_spots]
                args += [given["far"][far_spots]] if far_spots else []
        carried_at = len(args)
        args += carried
        args += [upper_points] if last and makes else []
        far_width = max(LANES, LANES * (len(far_spots) + (n_sub if last else 0)))
        scratch = [
            pltpu.VMEM((CORES * LEAVES, far_width, LANES), bf16),
            pltpu.VMEM((LEAVES + 1 if first else CORES * len(near_spots), points, LANES), bf16),
        ]
        if makes:
            scratch += [
                pltpu.VMEM((LEAVES + 1 if first else CORES * len(near_spots), LANES, points), bf16),
                pltpu.VMEM((LANES, far_width), bf16),
            ]
        names, outs = [], []
        if begins:
            names += ["targets", "table"]
            outs += [targets_shape, shape(8, LANES, dtype=f32)]
        if mode == "keep":
            names += [("near", spot) for spot in near_spots]
            outs += [shape(LEAVES + 1 if first else CORES, local, points) for _ in near_spots]
            names += [("far", far_spots)] if far_spots else []
            outs += [shape(CORES, local, far_width)] if far_spots else []
        if last:
            names += ["mine", "other"]
            outs += [half_shape, half_shape]
        aliases = {carried_at + k: len(outs) + k for k in range(len(carried))}
        names += ["total", "sums"]
        outs += [total_shape, sums_shape]
        static = (
            ring, near_spots, far_spots, n_sub, dim, points, begins, first, last, mode
        )
        results = call(
            functools.partial(stage_kernel, static),
            args,
            outs,
            scratch=scratch,
            aliases=aliases,
            flops=len(near_spots) * (2 if makes else 1) * 10**9,
        )
        return dict(zip(names, results))

    def far_spots_of(spot):
        return (spot - 1, spot) if spot % 2 == 0 and spot > 0 else (spot,)

    mode = "keep" if keeping else "make"
    given = {"near": {}, "far": {}, "places": {0: coords}, "skeletons": {0: message}}
    given["charges"] = given["skeletons"]

    def keep_results(results):
        for name, value in results.items():
            if isinstance(name, tuple):
                given[name[0]][name[1]] = value
        return [results["total"], results["sums"]]

    sent = one_way(message), other_way(message)
    results = stage((0,), (0,), given, [], False, mode, begins=True)
    given["targets"], given["tables"] = results["targets"], [results["table"], sibling_table]
    carried = keep_results(results)
    for hop in range(1, chips // 2):
        final = hop == chips // 2 - 1
        spots = (2 * hop - 1, 2 * hop)
        for at, spot in enumerate(spots):
            given["places"][spot] = coords_next[at]
            given["skeletons"][spot] = sent[at]
        coords_next = one_way(coords_next[0]), None if final else other_way(coords_next[1])
        sent = one_way(sent[0]), None if final else other_way(sent[1])
        carried = keep_results(stage(spots, spots, given, carried, False, mode))
    across = (chips - 1,)
    given["places"][across[0]], given["skeletons"][across[0]] = coords_next[0], sent[0]
    results = stage(across, across, given, carried, True, mode)
    keep_results(results)
    first, message, again = call(
        joined_kernel,
        [results["mine"], to_sibling(results["other"])] + maps,
        [shape(columns, local)] + [shape(points + LANES, LANES)] * 2,
    )

    mode = "use" if keeping else "make"
    given["charges"] = {}
    carried = []

    def arrived(spot, message):
        nonlocal carried
        given["charges"][spot] = message
        last = spot == chips - 1
        far_spots = () if spot % 2 == 1 and not last else far_spots_of(spot)
        results = stage((spot,), far_spots, given, carried, last, mode)
        carried = [results["total"], results["sums"]]
        return results

    one = one_way(message)
    arrived(0, message)
    other = other_way(gated(again, carried[1]))
    for hop in range(1, chips // 2):
        one_next = one_way(one)
        arrived(2 * hop - 1, one)
        other_next = None
        if hop < chips // 2 - 1:
            other = gated(other, carried[1])
            other_next = other_way(other)
        arrived(2 * hop, other)
        one, other = one_next, other_next
    results = arrived(chips - 1, one)
    (second,) = call(
        added_kernel, [results["mine"], to_sibling(results["other"])], [shape(columns, local)]
    )
    return (first, second)


def solution(mesh):
    placed = (
        P(None, ("groups", "leaf")),
        P(None, ("groups", "leaf")),
        P(("groups", "leaf"), None),
        P(("groups", "leaf"), None),
        P(("groups", "leaf"), None),
        P(("groups", "leaf"), None),
        P(("groups", "leaf"), None),
        P(None, ("groups", "leaf")),
        P(None, "groups"),
    )
    return jax.shard_map(
        on_device,
        mesh=mesh,
        in_specs=placed,
        out_specs=(P(None, ("groups", "leaf")), P(None, ("groups", "leaf"))),
        check_vma=False,
    )
```

```python
import functools

import jax
import jax.numpy as jnp
from jax import lax
from jax.experimental import pallas as pl
from jax.experimental.pallas import tpu as pltpu
from jax.sharding import PartitionSpec as P

BRANCH = 16
EXTRA = 16
LANES = 128
CORES = 2
LEAVES = 2
KEPT_MIB = 30

bf16 = jnp.bfloat16
f32 = jnp.float32
i32 = jnp.int32


def matmul(left, right):
    return jnp.dot(left, right, preferred_element_type=f32)


def square_parts(points):
    minus = -jnp.sum(points * points, axis=0, keepdims=True)
    high = minus.astype(bf16).astype(f32)
    rest = minus - high
    middle = rest.astype(bf16).astype(f32)
    low = rest - middle
    return high, middle, low


def extra_rows(parts, first, width):
    row = lax.broadcasted_iota(i32, (EXTRA, width), 0)
    rows = jnp.where(row < 6, 1.0, 0.0).astype(f32)
    for offset, part in enumerate(parts):
        rows = jnp.where(row == first + offset, jnp.broadcast_to(part, (EXTRA, width)), rows)
    return rows


def put_sources(sources_ref, points):
    dim, width = points.shape
    sources_ref[0:dim, :] = points
    parts = square_parts(points.astype(f32))
    sources_ref[dim : dim + EXTRA, :] = extra_rows(parts, 3, width).astype(bf16)
    sources_ref[dim + EXTRA :, :] = jnp.zeros((LANES - dim - EXTRA, width), bf16)


def target_rows(points):
    dim, width = points.shape
    points = points.astype(f32)
    extra = extra_rows(square_parts(points), 0, width)
    blank = jnp.zeros((LANES - dim - EXTRA, width), f32)
    return jnp.concatenate([2.0 * points, extra, blank], axis=0).T.astype(bf16)


def in_low_half(shape):
    return lax.broadcasted_iota(i32, shape, 1) < LANES // 2


def swapped(values):
    return pltpu.roll(values, LANES // 2, 1)


def kernel_values(targets, sources):
    return jnp.exp(matmul(targets, sources)).astype(bf16)


def skeleton_rows(charges, leaf_ref, node_ref, upper_ref):
    points = charges[0].shape[1]
    parts = []
    for leaf, block in enumerate(charges):
        span = slice(leaf * points, (leaf + 1) * points)
        parts.append(matmul(block, leaf_ref[span, :]).astype(bf16))
    weights = matmul(jnp.concatenate(parts, axis=1), node_ref[...]).astype(bf16)
    term = matmul(weights, upper_ref[...])
    return jnp.concatenate([weights.astype(f32), term], axis=0).T.astype(bf16)


def count_rows(near_ref, far_ref):
    shape = (8, LANES)
    row, lane = lax.broadcasted_iota(i32, shape, 0), lax.broadcasted_iota(i32, shape, 1)
    table = jnp.zeros(shape, f32)
    for leaf in range(LEAVES):
        for first, ref in ((0, near_ref), (LEAVES, far_ref)):
            for slot in range(ref.shape[1]):
                hit = (row == first + leaf) & (lane == ref[leaf, slot])
                table = table + jnp.where(hit, 1.0, 0.0)
    return table


def device_of(ring, spot):
    chips = len(ring)
    me = lax.axis_index("leaf")
    core = me % CORES
    place = jnp.int32(0)
    for at, chip in enumerate(ring):
        place = jnp.where(me // CORES == chip, at, place)
    hop = (spot + 1) // 2
    step = hop if spot % 2 == 0 else -hop
    met = (place + step * (1 - 2 * core) + chips) % chips
    device = jnp.int32(0)
    for at, chip in enumerate(ring):
        device = jnp.where(met == at, chip * CORES + core, device)
    return device


def message_kernel(
    near_ref,
    far_ref,
    coords_ref,
    charges_ref,
    points_ref,
    leaf_ref,
    node_ref,
    upper_ref,
    message_ref,
    local_ref,
    table_ref,
):
    dim, local = coords_ref.shape
    half = local // LEAVES
    charges = [charges_ref[:, 0:half], charges_ref[:, half:]]
    sent = [
        jnp.concatenate(charges, axis=0).astype(f32).T.astype(bf16),
        skeleton_rows(charges, leaf_ref, node_ref, upper_ref),
        points_ref[...],
    ]
    place = 0
    for part in sent:
        rows = slice(place, place + part.shape[0])
        message_ref[rows, :] = part
        local_ref[rows, :] = part
        place += part.shape[0]
    for block in range(local // LANES):
        local_ref[place : place + dim, :] = coords_ref[:, block * LANES : (block + 1) * LANES]
        place += dim
    table = count_rows(near_ref, far_ref)
    table_ref[...] = table
    local_ref[place : place + 16, :] = jnp.concatenate([table, table], axis=0).astype(bf16)


def joined_kernel(mine_ref, other_ref, leaf_ref, node_ref, upper_ref, out_ref, *message_refs):
    half = mine_ref.shape[0]
    columns = LANES // LEAVES
    result = mine_ref[...] + other_ref[...]
    flat = result.T.astype(bf16)
    charges = [flat[0:columns], flat[columns:]]
    out_ref[...] = jnp.concatenate(charges, axis=1)
    rows = skeleton_rows(charges, leaf_ref, node_ref, upper_ref)
    for message_ref in message_refs:
        message_ref[0:half, :] = result.astype(bf16)
        message_ref[half : half + LANES, :] = rows


def added_kernel(mine_ref, other_ref, out_ref):
    columns = LANES // LEAVES
    flat = (mine_ref[...] + other_ref[...]).T.astype(bf16)
    out_ref[...] = jnp.concatenate([flat[0:columns], flat[columns:]], axis=1)


def stage_kernel(stage, *refs):
    ring, near_spots, far_spots, n_sub, dim, points, begins, first, last, mode, near_given = stage
    refs = list(refs)
    use, keep = mode == "use", mode == "keep"
    spots = sorted(set(near_spots) | set(far_spots))
    makes = not use
    makes_near = makes and not near_given
    table_refs = [refs.pop(0) for _ in range(1 if begins else CORES)]
    if begins:
        local_ref = refs.pop(0)
        charge_refs = skeleton_refs = {spots[0]: local_ref}
    else:
        place_refs = {spot: refs.pop(0) for spot in near_spots} if makes_near else {}
        skeleton_refs = {spot: refs.pop(0) for spot in far_spots} if makes else {}
        charge_refs = {spot: refs.pop(0) for spot in spots}
    kept_refs = {}
    far_kept_ref = None
    if not makes_near:
        kept_refs = {spot: refs.pop(0) for spot in near_spots}
    if use:
        far_kept_ref = refs.pop(0) if far_spots else None
    if begins:
        sibling_ref = refs.pop(0)
    elif makes:
        targets_ref = refs.pop(0)
    if not first:
        refs.pop(0), refs.pop(0)
    upper_points_ref = refs.pop(0) if last and makes else None
    if begins:
        targets_ref, table_ref = refs.pop(0), refs.pop(0)
    if keep:
        if makes_near:
            kept_refs = {spot: refs.pop(0) for spot in near_spots}
        far_kept_ref = refs.pop(0) if far_spots else None
    if last:
        half_refs = refs.pop(0), refs.pop(0)
    total_ref, sums_ref, far_charges_ref, charges_ref = refs[:4]
    near_ref = refs[4] if makes_near else None
    far_ref = refs[-1] if makes else None

    skeletons_at = points + LANES
    blocks = points // LANES
    low_half = in_low_half((LANES, LANES))
    lane = lax.broadcasted_iota(i32, (8, LANES), 1)

    def span_of(leaf):
        return slice(leaf * points, (leaf + 1) * points)

    def points_of(spot, leaf):
        if not begins:
            return place_refs[spot][:, span_of(leaf)]
        begin = skeletons_at + dim + leaf * blocks * dim
        rows = [begin + block * dim for block in range(blocks)]
        return jnp.concatenate([local_ref[row : row + dim, :] for row in rows], axis=1)

    if begins:
        begin = skeletons_at + dim + LEAVES * blocks * dim
        table_ref[...] = local_ref[begin : begin + 16, :].astype(f32)[0:8]
        table_refs = [table_ref] + table_refs
        for leaf in range(LEAVES):
            targets_ref[0, span_of(leaf), :] = target_rows(points_of(0, leaf))
            targets_ref[1, span_of(leaf), :] = target_rows(sibling_ref[:, span_of(leaf)])
    if first:
        total_ref[...] = jnp.zeros_like(total_ref)
        sums_ref[...] = jnp.zeros_like(sums_ref)

    def table_of(core):
        return table_refs[core][...]

    def picked(table, entry):
        return jnp.sum(jnp.where(lane == entry, table, 0.0), axis=1, keepdims=True)

    def values(core, sources_ref, kept_ref):
        if sources_ref is None:
            return kept_ref[...]
        made = kernel_values(targets_ref[core], sources_ref[...])
        if kept_ref is not None:
            kept_ref[...] = made
        return made

    devices = {spot: device_of(ring, spot) for spot in spots}

    def near_part(turn, spot, core, leaf):
        at = core * len(near_spots) + near_spots.index(spot)
        table = table_of(core)
        named = [
            picked(table, devices[spot] * LEAVES + which)[0:LEAVES] for which in range(LEAVES)
        ]
        if leaf is None:
            second = jnp.where(jnp.sum(named[1], axis=0, keepdims=True) > 0.0, 1.0, 0.0)
        else:
            second = jnp.full((1, 1), float(leaf), f32)
        times = named[0] * (1.0 - second) + named[1] * second
        if makes_near:
            low, high = (points_of(spot, which) for which in range(LEAVES))
            chosen = low * (1.0 - second).astype(bf16) + high * second.astype(bf16)
            put_sources(near_ref.at[at], chosen)
        half = jnp.where(lane[0:1] < LANES // LEAVES, 1.0 - second, second).astype(bf16)
        charges_ref[at] = charge_refs[spot][0:points, :] * half
        kept = kept_refs[spot].at[turn] if kept_refs else None
        added = matmul(values(core, near_ref.at[at] if makes_near else None, kept), charges_ref[at])
        return [times[own : own + 1] * added[span_of(own)] for own in range(LEAVES)]

    weights = []
    skeletons = []
    for spot in far_spots:
        rows = charge_refs[spot][points : points + LANES, :].astype(f32)
        weights.append((jnp.where(low_half, rows, swapped(rows)), devices[spot]))
        sums_ref[devices[spot] // BRANCH] += rows
        if makes:
            skeletons.append(skeleton_refs[spot][skeletons_at : skeletons_at + dim, :])
    if last:
        for sub in range(n_sub):
            rows = sums_ref[sub]
            weights.append((jnp.where(low_half, swapped(rows), rows), len(ring) * CORES + sub))
            if makes:
                skeletons.append(upper_points_ref[:, sub * LANES : (sub + 1) * LANES])
    if far_spots and makes:
        put_sources(far_ref, jnp.concatenate(skeletons, axis=1))

    def far_part(core):
        table = table_of(core)
        kernel = values(
            core,
            far_ref if makes else None,
            None if far_kept_ref is None else far_kept_ref.at[core],
        )
        added = []
        for own in range(LEAVES):
            for position, (block, node) in enumerate(weights):
                scaled = block * picked(table, node)[LEAVES + own : LEAVES + own + 1]
                high = scaled.astype(bf16).astype(f32)
                rows = slice(position * LANES, (position + 1) * LANES)
                far_charges_ref[core * LEAVES + own, rows, :] = jnp.where(low_half, high, scaled - high).astype(bf16)
            added.append(matmul(kernel[span_of(own)], far_charges_ref[core * LEAVES + own]))
        return added

    def add(core, parts):
        for own in range(LEAVES):
            total = total_ref[core, span_of(own), :]
            for part in parts:
                total = total + part[own]
            total_ref[core, span_of(own), :] = total

    if first:
        for leaf in range(LEAVES):
            add(0, [near_part(leaf, 0, 0, leaf)])
        add(1, [near_part(LEAVES, 0, 1, None), far_part(1)])
    else:

        for core in range(CORES):
            parts = [near_part(core, spot, core, None) for spot in near_spots]
            add(core, parts + ([far_part(core)] if far_spots else []))

    if last:
        for core, ref in enumerate(half_refs):
            both = [total_ref[core, span_of(leaf), :] for leaf in range(LEAVES)]
            both = [total + swapped(total) for total in both]
            ref[...] = jnp.where(in_low_half(both[0].shape), both[0], both[1])


def near_values_kernel(ring, spot, points, mine_ref, other_ref, place_ref, targets_ref, kept_ref, near_ref):
    lane = lax.broadcasted_iota(i32, (LEAVES, LANES), 1)
    entry = device_of(ring, spot) * LEAVES + 1
    for core, table_ref in enumerate((mine_ref, other_ref)):
        named = jnp.where(lane == entry, table_ref[0:LEAVES, :], 0.0)
        named = jnp.sum(jnp.sum(named, axis=1, keepdims=True), axis=0, keepdims=True)
        second = jnp.where(named > 0.0, 1.0, 0.0)
        low, high = place_ref[:, 0:points], place_ref[:, points:]
        chosen = low * (1.0 - second).astype(bf16) + high * second.astype(bf16)
        put_sources(near_ref.at[core], chosen)
        kept_ref[core] = kernel_values(targets_ref[core], near_ref[core])


def gate_kernel(message_ref, after_ref, out_ref):
    pass


def gated(message, after):
    anywhere = pl.BlockSpec(memory_space=pl.ANY)
    return pl.pallas_call(
        gate_kernel,
        out_shape=jax.ShapeDtypeStruct(message.shape, message.dtype),
        in_specs=[anywhere] * 2,
        out_specs=anywhere,
        input_output_aliases={0: 0},
        compiler_params=pltpu.CompilerParams(vmem_limit_bytes=2**20),
    )(message, after)


def call(body, args, out_shapes, streamed=(), scratch=(), aliases={}, flops=0, vmem_mib=16):
    vmem = pl.BlockSpec(memory_space=pltpu.VMEM)
    specs = []
    for place, arg in enumerate(args):
        if arg.dtype == i32:
            specs.append(pl.BlockSpec(memory_space=pltpu.SMEM))
        elif place in streamed:
            specs.append(pl.BlockSpec(arg.shape, lambda i: (0,) * 2))
        else:
            specs.append(vmem)
    moved = sum(arg.size * arg.dtype.itemsize for arg in args)
    return pl.pallas_call(
        body,
        grid=(1,),
        out_shape=out_shapes,
        in_specs=specs,
        out_specs=[vmem for _ in out_shapes],
        scratch_shapes=list(scratch),
        input_output_aliases=aliases,
        compiler_params=pltpu.CompilerParams(vmem_limit_bytes=vmem_mib * 1024 * 1024),
        cost_estimate=pl.CostEstimate(flops=flops, bytes_accessed=moved, transcendentals=0),
    )(*args)


def ring_order(chips):
    if chips == 8:
        return [0, 2, 4, 6, 7, 5, 3, 1]
    return list(range(chips))


def on_device(
    coords,
    charges,
    near_lists,
    far_lists,
    leaf_interp,
    node_interp,
    upper_interp,
    node_points,
    upper_points,
):
    dim, local = coords.shape
    columns = charges.shape[0]
    points = local // LEAVES
    peers = lax.axis_size("leaf")
    n_sub = peers // BRANCH
    ring = ring_order(peers // CORES)
    chips = len(ring)

    def along(step):
        return [
            (ring[place] * CORES + core, ring[(place + step * (1 - 2 * core)) % chips] * CORES + core)
            for place in range(chips)
            for core in range(CORES)
        ]

    one_way = functools.partial(lax.ppermute, axis_name="leaf", perm=along(1))
    other_way = functools.partial(lax.ppermute, axis_name="leaf", perm=along(-1))
    to_sibling = functools.partial(
        lax.ppermute, axis_name="leaf", perm=[(device, device ^ 1) for device in range(peers)]
    )

    def shape(*extent, dtype=bf16):
        return jax.ShapeDtypeStruct(extent, dtype)

    maps = [leaf_interp, node_interp, upper_interp]
    sibling_coords = to_sibling(coords)
    coords_next = one_way(coords), other_way(coords)
    message, own, table = call(
        message_kernel,
        [near_lists, far_lists, coords, charges, node_points] + maps,
        [
            shape(points + LANES + dim, LANES),
            shape(points + LANES + dim + LEAVES * points // LANES * dim + 16, LANES),
            shape(8, LANES, dtype=f32),
        ],
        streamed=range(2, 8),
        vmem_mib=60,
    )
    sibling_table = to_sibling(table)

    total_shape = shape(CORES, local, LANES, dtype=f32)
    sums_shape = shape(n_sub, LANES, LANES, dtype=f32)
    half_shape = shape(points, LANES, dtype=f32)
    targets_shape = shape(CORES, local, LANES)

    steps = LEAVES + 1 + CORES * (chips - 1)
    kept_bytes = 2 * points * (steps * local + CORES * LEAVES * (chips + n_sub) * LANES)
    keeping = kept_bytes <= KEPT_MIB * 2**20

    def stage(near_spots, far_spots, given, carried, last, mode, begins=False, near_given=False):
        first = not carried
        makes = mode != "use"
        spots = sorted(set(near_spots) | set(far_spots))
        if begins:
            args = [sibling_table, own, sibling_coords]
        else:
            args = list(given["tables"])
            if makes:
                if not near_given:
                    args += [given["places"][spot] for spot in near_spots]
                args += [given["skeletons"][spot] for spot in far_spots]
            args += [given["charges"][spot] for spot in spots]
            if near_given or not makes:
                args += [given["near"][spot] for spot in near_spots]
            if makes:
                args += [given["targets"]]
            else:
                args += [given["far"][far_spots]] if far_spots else []
        carried_at = len(args)
        args += carried
        args += [upper_points] if last and makes else []
        far_width = max(LANES, LANES * (len(far_spots) + (n_sub if last else 0)))
        scratch = [
            pltpu.VMEM((CORES * LEAVES, far_width, LANES), bf16),
            pltpu.VMEM((CORES * len(near_spots), points, LANES), bf16),
        ]
        if makes and not near_given:
            scratch += [pltpu.VMEM((CORES * len(near_spots), LANES, points), bf16)]
        if makes:
            scratch += [pltpu.VMEM((LANES, far_width), bf16)]
        names, outs = [], []
        if begins:
            names += ["targets", "table"]
            outs += [targets_shape, shape(8, LANES, dtype=f32)]
        if mode == "keep":
            if not near_given:
                names += [("near", spot) for spot in near_spots]
                outs += [shape(LEAVES + 1 if first else CORES, local, points) for _ in near_spots]
            names += [("far", far_spots)] if far_spots else []
            outs += [shape(CORES, local, far_width)] if far_spots else []
        if last:
            names += ["mine", "other"]
            outs += [half_shape, half_shape]
        aliases = {carried_at + k: len(outs) + k for k in range(len(carried))}
        names += ["total", "sums"]
        outs += [total_shape, sums_shape]
        static = (
            ring, near_spots, far_spots, n_sub, dim, points, begins, first, last, mode, near_given
        )
        results = call(
            functools.partial(stage_kernel, static),
            args,
            outs,
            scratch=scratch,
            aliases=aliases,
            flops=len(near_spots) * (2 if makes else 1) * 10**9,
        )
        return dict(zip(names, results))

    def far_spots_of(spot):
        return (spot - 1, spot) if spot % 2 == 0 and spot > 0 else (spot,)

    mode = "keep" if keeping else "make"
    given = {"near": {}, "far": {}, "places": {0: coords}, "skeletons": {0: message}}
    given["charges"] = given["skeletons"]

    def keep_results(results):
        for name, value in results.items():
            if isinstance(name, tuple):
                given[name[0]][name[1]] = value
        return [results["total"], results["sums"]]

    sent = one_way(message), other_way(message)
    results = stage((0,), (0,), given, [], False, mode, begins=True)
    given["targets"], given["tables"] = results["targets"], [results["table"], sibling_table]
    carried = keep_results(results)
    for hop in range(1, chips // 2):
        final = hop == chips // 2 - 1
        spots = (2 * hop - 1, 2 * hop)
        for at, spot in enumerate(spots):
            given["places"][spot] = coords_next[at]
            given["skeletons"][spot] = sent[at]
        coords_next = one_way(coords_next[0]), None if final else other_way(coords_next[1])
        sent = one_way(sent[0]), None if final else other_way(sent[1])
        carried = keep_results(stage(spots, spots, given, carried, False, mode))
    across = (chips - 1,)
    given["places"][across[0]], given["skeletons"][across[0]] = coords_next[0], sent[0]
    if keeping:
        (given["near"][across[0]],) = call(
            functools.partial(near_values_kernel, ring, across[0], points),
            given["tables"] + [gated(coords_next[0], carried[1]), given["targets"]],
            [shape(CORES, local, points)],
            scratch=[pltpu.VMEM((CORES, LANES, points), bf16)],
            flops=10**9,
        )
    results = stage(across, across, given, carried, True, mode, near_given=keeping)
    keep_results(results)
    first, message, again = call(
        joined_kernel,
        [results["mine"], to_sibling(results["other"])] + maps,
        [shape(columns, local)] + [shape(points + LANES, LANES)] * 2,
    )

    mode = "use" if keeping else "make"
    given["charges"] = {}
    carried = []

    def arrived(spot, message):
        nonlocal carried
        given["charges"][spot] = message
        last = spot == chips - 1
        far_spots = () if spot % 2 == 1 and not last else far_spots_of(spot)
        results = stage((spot,), far_spots, given, carried, last, mode)
        carried = [results["total"], results["sums"]]
        return results

    one = one_way(message)
    arrived(0, message)
    other = other_way(gated(again, carried[1]))
    for hop in range(1, chips // 2):
        one_next = one_way(one)
        arrived(2 * hop - 1, one)
        other_next = None
        if hop < chips // 2 - 1:
            other = gated(other, carried[1])
            other_next = other_way(other)
        arrived(2 * hop, other)
        one, other = one_next, other_next
    results = arrived(chips - 1, one)
    (second,) = call(
        added_kernel, [results["mine"], to_sibling(results["other"])], [shape(columns, local)]
    )
    return (first, second)


def solution(mesh):
    placed = (
        P(None, ("groups", "leaf")),
        P(None, ("groups", "leaf")),
        P(("groups", "leaf"), None),
        P(("groups", "leaf"), None),
        P(("groups", "leaf"), None),
        P(("groups", "leaf"), None),
        P(("groups", "leaf"), None),
        P(None, ("groups", "leaf")),
        P(None, "groups"),
    )
    return jax.shard_map(
        on_device,
        mesh=mesh,
        in_specs=placed,
        out_specs=(P(None, ("groups", "leaf")), P(None, ("groups", "leaf"))),
        check_vma=False,
    )
```

```python
import functools

import jax
import jax.numpy as jnp
from jax import lax
from jax.experimental import pallas as pl
from jax.experimental.pallas import tpu as pltpu
from jax.sharding import PartitionSpec as P

BRANCH = 16
EXTRA = 16
LANES = 128
CORES = 2
LEAVES = 2
KEPT_MIB = 30

bf16 = jnp.bfloat16
f32 = jnp.float32
i32 = jnp.int32


def matmul(left, right):
    return jnp.dot(left, right, preferred_element_type=f32)


def square_parts(points):
    minus = -jnp.sum(points * points, axis=0, keepdims=True)
    high = minus.astype(bf16).astype(f32)
    rest = minus - high
    middle = rest.astype(bf16).astype(f32)
    low = rest - middle
    return high, middle, low


def extra_rows(parts, first, width):
    row = lax.broadcasted_iota(i32, (EXTRA, width), 0)
    rows = jnp.where(row < 6, 1.0, 0.0).astype(f32)
    for offset, part in enumerate(parts):
        rows = jnp.where(row == first + offset, jnp.broadcast_to(part, (EXTRA, width)), rows)
    return rows


def put_sources(sources_ref, points):
    dim, width = points.shape
    sources_ref[0:dim, :] = points
    parts = square_parts(points.astype(f32))
    sources_ref[dim : dim + EXTRA, :] = extra_rows(parts, 3, width).astype(bf16)
    sources_ref[dim + EXTRA :, :] = jnp.zeros((LANES - dim - EXTRA, width), bf16)


def target_rows(points):
    dim, width = points.shape
    points = points.astype(f32)
    extra = extra_rows(square_parts(points), 0, width)
    blank = jnp.zeros((LANES - dim - EXTRA, width), f32)
    return jnp.concatenate([2.0 * points, extra, blank], axis=0).T.astype(bf16)


def in_low_half(shape):
    return lax.broadcasted_iota(i32, shape, 1) < LANES // 2


def swapped(values):
    return pltpu.roll(values, LANES // 2, 1)


def kernel_values(targets, sources):
    return jnp.exp(matmul(targets, sources)).astype(bf16)


def skeleton_rows(charges, leaf_ref, node_ref, upper_ref):
    points = charges[0].shape[1]
    parts = []
    for leaf, block in enumerate(charges):
        span = slice(leaf * points, (leaf + 1) * points)
        parts.append(matmul(block, leaf_ref[span, :]).astype(bf16))
    weights = matmul(jnp.concatenate(parts, axis=1), node_ref[...]).astype(bf16)
    term = matmul(weights, upper_ref[...])
    return jnp.concatenate([weights.astype(f32), term], axis=0).T.astype(bf16)


def count_rows(near_ref, far_ref):
    shape = (8, LANES)
    row, lane = lax.broadcasted_iota(i32, shape, 0), lax.broadcasted_iota(i32, shape, 1)
    table = jnp.zeros(shape, f32)
    for leaf in range(LEAVES):
        for first, ref in ((0, near_ref), (LEAVES, far_ref)):
            for slot in range(ref.shape[1]):
                hit = (row == first + leaf) & (lane == ref[leaf, slot])
                table = table + jnp.where(hit, 1.0, 0.0)
    return table


def device_of(ring, spot):
    chips = len(ring)
    me = lax.axis_index("leaf")
    core = me % CORES
    place = jnp.int32(0)
    for at, chip in enumerate(ring):
        place = jnp.where(me // CORES == chip, at, place)
    hop = (spot + 1) // 2
    step = hop if spot % 2 == 0 else -hop
    met = (place + step * (1 - 2 * core) + chips) % chips
    device = jnp.int32(0)
    for at, chip in enumerate(ring):
        device = jnp.where(met == at, chip * CORES + core, device)
    return device


def message_kernel(
    near_ref,
    far_ref,
    coords_ref,
    charges_ref,
    points_ref,
    leaf_ref,
    node_ref,
    upper_ref,
    message_ref,
    local_ref,
    table_ref,
):
    dim, local = coords_ref.shape
    half = local // LEAVES
    charges = [charges_ref[:, 0:half], charges_ref[:, half:]]
    sent = [
        jnp.concatenate(charges, axis=0).astype(f32).T.astype(bf16),
        skeleton_rows(charges, leaf_ref, node_ref, upper_ref),
        points_ref[...],
    ]
    place = 0
    for part in sent:
        rows = slice(place, place + part.shape[0])
        message_ref[rows, :] = part
        local_ref[rows, :] = part
        place += part.shape[0]
    for block in range(local // LANES):
        local_ref[place : place + dim, :] = coords_ref[:, block * LANES : (block + 1) * LANES]
        place += dim
    table = count_rows(near_ref, far_ref)
    table_ref[...] = table
    local_ref[place : place + 16, :] = jnp.concatenate([table, table], axis=0).astype(bf16)


def joined_kernel(mine_ref, other_ref, leaf_ref, node_ref, upper_ref, out_ref, *message_refs):
    half = mine_ref.shape[0]
    columns = LANES // LEAVES
    result = mine_ref[...] + other_ref[...]
    flat = result.T.astype(bf16)
    charges = [flat[0:columns], flat[columns:]]
    out_ref[...] = jnp.concatenate(charges, axis=1)
    rows = skeleton_rows(charges, leaf_ref, node_ref, upper_ref)
    for message_ref in message_refs:
        message_ref[0:half, :] = result.astype(bf16)
        message_ref[half : half + LANES, :] = rows


def added_kernel(mine_ref, other_ref, out_ref):
    columns = LANES // LEAVES
    flat = (mine_ref[...] + other_ref[...]).T.astype(bf16)
    out_ref[...] = jnp.concatenate([flat[0:columns], flat[columns:]], axis=1)


def stage_kernel(stage, *refs):
    ring, near_spots, far_spots, n_sub, dim, points, begins, first, last, mode, near_given = stage
    refs = list(refs)
    use, keep = mode == "use", mode == "keep"
    spots = sorted(set(near_spots) | set(far_spots))
    makes = not use
    makes_near = makes and not near_given
    table_refs = [refs.pop(0) for _ in range(1 if begins else CORES)]
    if begins:
        local_ref = refs.pop(0)
        charge_refs = skeleton_refs = {spots[0]: local_ref}
    else:
        place_refs = {spot: refs.pop(0) for spot in near_spots} if makes_near else {}
        skeleton_refs = {spot: refs.pop(0) for spot in far_spots} if makes else {}
        charge_refs = {spot: refs.pop(0) for spot in spots}
    kept_refs = {}
    far_kept_ref = None
    if not makes_near:
        kept_refs = {spot: refs.pop(0) for spot in near_spots}
    if use:
        far_kept_ref = refs.pop(0) if far_spots else None
    if begins:
        sibling_ref = refs.pop(0)
    elif makes:
        targets_ref = refs.pop(0)
    if not first:
        refs.pop(0), refs.pop(0)
    upper_points_ref = refs.pop(0) if last and makes else None
    if begins:
        targets_ref, table_ref = refs.pop(0), refs.pop(0)
    if keep:
        if makes_near:
            kept_refs = {spot: refs.pop(0) for spot in near_spots}
        far_kept_ref = refs.pop(0) if far_spots else None
    if last:
        half_refs = refs.pop(0), refs.pop(0)
    total_ref, sums_ref, far_charges_ref, charges_ref = refs[:4]
    near_ref = refs[4] if makes_near else None
    far_ref = refs[-1] if makes else None

    skeletons_at = points + LANES
    blocks = points // LANES
    low_half = in_low_half((LANES, LANES))
    lane = lax.broadcasted_iota(i32, (8, LANES), 1)

    def span_of(leaf):
        return slice(leaf * points, (leaf + 1) * points)

    def points_of(spot, leaf):
        if not begins:
            return place_refs[spot][:, span_of(leaf)]
        begin = skeletons_at + dim + leaf * blocks * dim
        rows = [begin + block * dim for block in range(blocks)]
        return jnp.concatenate([local_ref[row : row + dim, :] for row in rows], axis=1)

    if begins:
        begin = skeletons_at + dim + LEAVES * blocks * dim
        table_ref[...] = local_ref[begin : begin + 16, :].astype(f32)[0:8]
        table_refs = [table_ref] + table_refs
        for leaf in range(LEAVES):
            targets_ref[0, span_of(leaf), :] = target_rows(points_of(0, leaf))
            targets_ref[1, span_of(leaf), :] = target_rows(sibling_ref[:, span_of(leaf)])
    if first:
        total_ref[...] = jnp.zeros_like(total_ref)
        sums_ref[...] = jnp.zeros_like(sums_ref)

    def table_of(core):
        return table_refs[core][...]

    def picked(table, entry):
        return jnp.sum(jnp.where(lane == entry, table, 0.0), axis=1, keepdims=True)

    def values(core, sources_ref, kept_ref):
        if sources_ref is None:
            return kept_ref[...]
        made = kernel_values(targets_ref[core], sources_ref[...])
        if kept_ref is not None:
            kept_ref[...] = made
        return made

    devices = {spot: device_of(ring, spot) for spot in spots}

    def near_part(turn, spot, core, leaf):
        at = core * len(near_spots) + near_spots.index(spot)
        table = table_of(core)
        named = [
            picked(table, devices[spot] * LEAVES + which)[0:LEAVES] for which in range(LEAVES)
        ]
        if leaf is None:
            second = jnp.where(jnp.sum(named[1], axis=0, keepdims=True) > 0.0, 1.0, 0.0)
        else:
            second = jnp.full((1, 1), float(leaf), f32)
        times = named[0] * (1.0 - second) + named[1] * second
        if makes_near:
            low, high = (points_of(spot, which) for which in range(LEAVES))
            chosen = low * (1.0 - second).astype(bf16) + high * second.astype(bf16)
            put_sources(near_ref.at[at], chosen)
        half = jnp.where(lane[0:1] < LANES // LEAVES, 1.0 - second, second).astype(bf16)
        charges_ref[at] = charge_refs[spot][0:points, :] * half
        kept = kept_refs[spot].at[turn] if kept_refs else None
        added = matmul(values(core, near_ref.at[at] if makes_near else None, kept), charges_ref[at])
        return [times[own : own + 1] * added[span_of(own)] for own in range(LEAVES)]

    weights = []
    skeletons = []
    for spot in far_spots:
        rows = charge_refs[spot][points : points + LANES, :].astype(f32)
        weights.append((jnp.where(low_half, rows, swapped(rows)), devices[spot]))
        sums_ref[devices[spot] // BRANCH] += rows
        if makes:
            skeletons.append(skeleton_refs[spot][skeletons_at : skeletons_at + dim, :])
    if last:
        for sub in range(n_sub):
            rows = sums_ref[sub]
            weights.append((jnp.where(low_half, swapped(rows), rows), len(ring) * CORES + sub))
            if makes:
                skeletons.append(upper_points_ref[:, sub * LANES : (sub + 1) * LANES])
    if far_spots and makes:
        put_sources(far_ref, jnp.concatenate(skeletons, axis=1))

    def far_part(core):
        table = table_of(core)
        kernel = values(
            core,
            far_ref if makes else None,
            None if far_kept_ref is None else far_kept_ref.at[core],
        )
        added = []
        for own in range(LEAVES):
            for position, (block, node) in enumerate(weights):
                scaled = block * picked(table, node)[LEAVES + own : LEAVES + own + 1]
                high = scaled.astype(bf16).astype(f32)
                rows = slice(position * LANES, (position + 1) * LANES)
                far_charges_ref[core * LEAVES + own, rows, :] = jnp.where(low_half, high, scaled - high).astype(bf16)
            added.append(matmul(kernel[span_of(own)], far_charges_ref[core * LEAVES + own]))
        return added

    def add(core, parts):
        for own in range(LEAVES):
            total = total_ref[core, span_of(own), :]
            for part in parts:
                total = total + part[own]
            total_ref[core, span_of(own), :] = total

    if first:
        for leaf in range(LEAVES):
            add(0, [near_part(leaf, 0, 0, leaf)])
        add(1, [near_part(LEAVES, 0, 1, None), far_part(1)])
    else:

        for core in range(CORES):
            parts = [near_part(core, spot, core, None) for spot in near_spots]
            add(core, parts + ([far_part(core)] if far_spots else []))

    if last:
        for core, ref in enumerate(half_refs):
            both = [total_ref[core, span_of(leaf), :] for leaf in range(LEAVES)]
            both = [total + swapped(total) for total in both]
            ref[...] = jnp.where(in_low_half(both[0].shape), both[0], both[1])


def near_values_kernel(ring, spot, points, mine_ref, other_ref, place_ref, targets_ref, kept_ref, near_ref):
    lane = lax.broadcasted_iota(i32, (LEAVES, LANES), 1)
    entry = device_of(ring, spot) * LEAVES + 1
    for core, table_ref in enumerate((mine_ref, other_ref)):
        named = jnp.where(lane == entry, table_ref[0:LEAVES, :], 0.0)
        named = jnp.sum(jnp.sum(named, axis=1, keepdims=True), axis=0, keepdims=True)
        second = jnp.where(named > 0.0, 1.0, 0.0)
        low, high = place_ref[:, 0:points], place_ref[:, points:]
        chosen = low * (1.0 - second).astype(bf16) + high * second.astype(bf16)
        put_sources(near_ref.at[core], chosen)
        kept_ref[core] = kernel_values(targets_ref[core], near_ref[core])


def gate_kernel(message_ref, after_ref, out_ref):
    pass


def gated(message, after):
    anywhere = pl.BlockSpec(memory_space=pl.ANY)
    return pl.pallas_call(
        gate_kernel,
        out_shape=jax.ShapeDtypeStruct(message.shape, message.dtype),
        in_specs=[anywhere] * 2,
        out_specs=anywhere,
        input_output_aliases={0: 0},
        compiler_params=pltpu.CompilerParams(vmem_limit_bytes=2**20),
    )(message, after)


def call(body, args, out_shapes, streamed=(), scratch=(), aliases={}, flops=0, vmem_mib=16):
    vmem = pl.BlockSpec(memory_space=pltpu.VMEM)
    specs = []
    for place, arg in enumerate(args):
        if arg.dtype == i32:
            specs.append(pl.BlockSpec(memory_space=pltpu.SMEM))
        elif place in streamed:
            specs.append(pl.BlockSpec(arg.shape, lambda i: (0,) * 2))
        else:
            specs.append(vmem)
    moved = sum(arg.size * arg.dtype.itemsize for arg in args)
    return pl.pallas_call(
        body,
        grid=(1,),
        out_shape=out_shapes,
        in_specs=specs,
        out_specs=[vmem for _ in out_shapes],
        scratch_shapes=list(scratch),
        input_output_aliases=aliases,
        compiler_params=pltpu.CompilerParams(vmem_limit_bytes=vmem_mib * 1024 * 1024),
        cost_estimate=pl.CostEstimate(flops=flops, bytes_accessed=moved, transcendentals=0),
    )(*args)


def ring_order(chips):
    if chips == 8:
        return [0, 2, 4, 6, 7, 5, 3, 1]
    return list(range(chips))


def on_device(
    coords,
    charges,
    near_lists,
    far_lists,
    leaf_interp,
    node_interp,
    upper_interp,
    node_points,
    upper_points,
):
    dim, local = coords.shape
    columns = charges.shape[0]
    points = local // LEAVES
    peers = lax.axis_size("leaf")
    n_sub = peers // BRANCH
    ring = ring_order(peers // CORES)
    chips = len(ring)

    def along(step):
        return [
            (ring[place] * CORES + core, ring[(place + step * (1 - 2 * core)) % chips] * CORES + core)
            for place in range(chips)
            for core in range(CORES)
        ]

    one_way = functools.partial(lax.ppermute, axis_name="leaf", perm=along(1))
    other_way = functools.partial(lax.ppermute, axis_name="leaf", perm=along(-1))
    to_sibling = functools.partial(
        lax.ppermute, axis_name="leaf", perm=[(device, device ^ 1) for device in range(peers)]
    )

    def shape(*extent, dtype=bf16):
        return jax.ShapeDtypeStruct(extent, dtype)

    maps = [leaf_interp, node_interp, upper_interp]
    sibling_coords = to_sibling(coords)
    coords_next = one_way(coords), other_way(coords)
    message, own, table = call(
        message_kernel,
        [near_lists, far_lists, coords, charges, node_points] + maps,
        [
            shape(points + LANES + dim, LANES),
            shape(points + LANES + dim + LEAVES * points // LANES * dim + 16, LANES),
            shape(8, LANES, dtype=f32),
        ],
        streamed=range(2, 8),
        vmem_mib=60,
        flops=25 * 10**8,
    )
    sibling_table = to_sibling(table)

    total_shape = shape(CORES, local, LANES, dtype=f32)
    sums_shape = shape(n_sub, LANES, LANES, dtype=f32)
    half_shape = shape(points, LANES, dtype=f32)
    targets_shape = shape(CORES, local, LANES)

    steps = LEAVES + 1 + CORES * (chips - 1)
    kept_bytes = 2 * points * (steps * local + CORES * LEAVES * (chips + n_sub) * LANES)
    keeping = kept_bytes <= KEPT_MIB * 2**20

    def stage(near_spots, far_spots, given, carried, last, mode, begins=False, near_given=False):
        first = not carried
        makes = mode != "use"
        spots = sorted(set(near_spots) | set(far_spots))
        if begins:
            args = [sibling_table, own, sibling_coords]
        else:
            args = list(given["tables"])
            if makes:
                if not near_given:
                    args += [given["places"][spot] for spot in near_spots]
                args += [given["skeletons"][spot] for spot in far_spots]
            args += [given["charges"][spot] for spot in spots]
            if near_given or not makes:
                args += [given["near"][spot] for spot in near_spots]
            if makes:
                args += [given["targets"]]
            else:
                args += [given["far"][far_spots]] if far_spots else []
        carried_at = len(args)
        args += carried
        args += [upper_points] if last and makes else []
        far_width = max(LANES, LANES * (len(far_spots) + (n_sub if last else 0)))
        scratch = [
            pltpu.VMEM((CORES * LEAVES, far_width, LANES), bf16),
            pltpu.VMEM((CORES * len(near_spots), points, LANES), bf16),
        ]
        if makes and not near_given:
            scratch += [pltpu.VMEM((CORES * len(near_spots), LANES, points), bf16)]
        if makes:
            scratch += [pltpu.VMEM((LANES, far_width), bf16)]
        names, outs = [], []
        if begins:
            names += ["targets", "table"]
            outs += [targets_shape, shape(8, LANES, dtype=f32)]
        if mode == "keep":
            if not near_given:
                names += [("near", spot) for spot in near_spots]
                outs += [shape(LEAVES + 1 if first else CORES, local, points) for _ in near_spots]
            names += [("far", far_spots)] if far_spots else []
            outs += [shape(CORES, local, far_width)] if far_spots else []
        if last:
            names += ["mine", "other"]
            outs += [half_shape, half_shape]
        aliases = {carried_at + k: len(outs) + k for k in range(len(carried))}
        names += ["total", "sums"]
        outs += [total_shape, sums_shape]
        static = (
            ring, near_spots, far_spots, n_sub, dim, points, begins, first, last, mode, near_given
        )
        results = call(
            functools.partial(stage_kernel, static),
            args,
            outs,
            scratch=scratch,
            aliases=aliases,
            flops=len(near_spots) * (2 if makes else 1) * 10**9,
        )
        return dict(zip(names, results))

    def far_spots_of(spot):
        return (spot - 1, spot) if spot % 2 == 0 and spot > 0 else (spot,)

    mode = "keep" if keeping else "make"
    given = {"near": {}, "far": {}, "places": {0: coords}, "skeletons": {0: message}}
    given["charges"] = given["skeletons"]

    def keep_results(results):
        for name, value in results.items():
            if isinstance(name, tuple):
                given[name[0]][name[1]] = value
        return [results["total"], results["sums"]]

    sent = one_way(message), other_way(message)
    results = stage((0,), (0,), given, [], False, mode, begins=True)
    given["targets"], given["tables"] = results["targets"], [results["table"], sibling_table]
    carried = keep_results(results)
    for hop in range(1, chips // 2):
        final = hop == chips // 2 - 1
        spots = (2 * hop - 1, 2 * hop)
        for at, spot in enumerate(spots):
            given["places"][spot] = coords_next[at]
            given["skeletons"][spot] = sent[at]
        coords_next = one_way(coords_next[0]), None if final else other_way(coords_next[1])
        sent = one_way(sent[0]), None if final else other_way(sent[1])
        carried = keep_results(stage(spots, spots, given, carried, False, mode))
    across = (chips - 1,)
    given["places"][across[0]], given["skeletons"][across[0]] = coords_next[0], sent[0]
    if keeping:
        (given["near"][across[0]],) = call(
            functools.partial(near_values_kernel, ring, across[0], points),
            given["tables"] + [gated(coords_next[0], carried[1]), given["targets"]],
            [shape(CORES, local, points)],
            scratch=[pltpu.VMEM((CORES, LANES, points), bf16)],
            flops=10**9,
        )
    results = stage(across, across, given, carried, True, mode, near_given=keeping)
    keep_results(results)
    first, message, again = call(
        joined_kernel,
        [results["mine"], to_sibling(results["other"])] + maps,
        [shape(columns, local)] + [shape(points + LANES, LANES)] * 2,
    )

    mode = "use" if keeping else "make"
    given["charges"] = {}
    carried = []

    def arrived(spot, message):
        nonlocal carried
        given["charges"][spot] = message
        last = spot == chips - 1
        far_spots = () if spot % 2 == 1 and not last else far_spots_of(spot)
        results = stage((spot,), far_spots, given, carried, last, mode)
        carried = [results["total"], results["sums"]]
        return results

    one = one_way(message)
    arrived(0, message)
    other = other_way(gated(again, carried[1]))
    for hop in range(1, chips // 2):
        one_next = one_way(one)
        arrived(2 * hop - 1, one)
        other_next = None
        if hop < chips // 2 - 1:
            other = gated(other, carried[1])
            other_next = other_way(other)
        arrived(2 * hop, other)
        one, other = one_next, other_next
    results = arrived(chips - 1, one)
    (second,) = call(
        added_kernel, [results["mine"], to_sibling(results["other"])], [shape(columns, local)]
    )
    return (first, second)


def solution(mesh):
    placed = (
        P(None, ("groups", "leaf")),
        P(None, ("groups", "leaf")),
        P(("groups", "leaf"), None),
        P(("groups", "leaf"), None),
        P(("groups", "leaf"), None),
        P(("groups", "leaf"), None),
        P(("groups", "leaf"), None),
        P(None, ("groups", "leaf")),
        P(None, "groups"),
    )
    return jax.shard_map(
        on_device,
        mesh=mesh,
        in_specs=placed,
        out_specs=(P(None, ("groups", "leaf")), P(None, ("groups", "leaf"))),
        check_vma=False,
    )
```

```python
import functools

import jax
import jax.numpy as jnp
from jax import lax
from jax.experimental import pallas as pl
from jax.experimental.pallas import tpu as pltpu
from jax.sharding import PartitionSpec as P

BRANCH = 16
EXTRA = 16
LANES = 128
CORES = 2
LEAVES = 2
KEPT_MIB = 30

bf16 = jnp.bfloat16
f32 = jnp.float32
i32 = jnp.int32


def matmul(left, right):
    return jnp.dot(left, right, preferred_element_type=f32)


def square_parts(points):
    minus = -jnp.sum(points * points, axis=0, keepdims=True)
    high = minus.astype(bf16).astype(f32)
    rest = minus - high
    middle = rest.astype(bf16).astype(f32)
    low = rest - middle
    return high, middle, low


def extra_rows(parts, first, width):
    row = lax.broadcasted_iota(i32, (EXTRA, width), 0)
    rows = jnp.where(row < 6, 1.0, 0.0).astype(f32)
    for offset, part in enumerate(parts):
        rows = jnp.where(row == first + offset, jnp.broadcast_to(part, (EXTRA, width)), rows)
    return rows


def put_sources(sources_ref, points):
    dim, width = points.shape
    sources_ref[0:dim, :] = points
    parts = square_parts(points.astype(f32))
    sources_ref[dim : dim + EXTRA, :] = extra_rows(parts, 3, width).astype(bf16)
    sources_ref[dim + EXTRA :, :] = jnp.zeros((LANES - dim - EXTRA, width), bf16)


def target_rows(points):
    dim, width = points.shape
    points = points.astype(f32)
    extra = extra_rows(square_parts(points), 0, width)
    blank = jnp.zeros((LANES - dim - EXTRA, width), f32)
    return jnp.concatenate([2.0 * points, extra, blank], axis=0).T.astype(bf16)


def in_low_half(shape):
    return lax.broadcasted_iota(i32, shape, 1) < LANES // 2


def swapped(values):
    return pltpu.roll(values, LANES // 2, 1)


def kernel_values(targets, sources):
    return jnp.exp(matmul(targets, sources)).astype(bf16)


def skeleton_rows(charges, leaf_ref, node_ref, upper_ref):
    points = charges[0].shape[1]
    parts = []
    for leaf, block in enumerate(charges):
        span = slice(leaf * points, (leaf + 1) * points)
        parts.append(matmul(block, leaf_ref[span, :]).astype(bf16))
    weights = matmul(jnp.concatenate(parts, axis=1), node_ref[...]).astype(bf16)
    term = matmul(weights, upper_ref[...])
    return jnp.concatenate([weights.astype(f32), term], axis=0).T.astype(bf16)


def count_rows(near_ref, far_ref):
    shape = (8, LANES)
    row, lane = lax.broadcasted_iota(i32, shape, 0), lax.broadcasted_iota(i32, shape, 1)
    table = jnp.zeros(shape, f32)
    for leaf in range(LEAVES):
        for first, ref in ((0, near_ref), (LEAVES, far_ref)):
            for slot in range(ref.shape[1]):
                hit = (row == first + leaf) & (lane == ref[leaf, slot])
                table = table + jnp.where(hit, 1.0, 0.0)
    return table


def device_of(ring, spot):
    chips = len(ring)
    me = lax.axis_index("leaf")
    core = me % CORES
    place = jnp.int32(0)
    for at, chip in enumerate(ring):
        place = jnp.where(me // CORES == chip, at, place)
    hop = (spot + 1) // 2
    step = hop if spot % 2 == 0 else -hop
    met = (place + step * (1 - 2 * core) + chips) % chips
    device = jnp.int32(0)
    for at, chip in enumerate(ring):
        device = jnp.where(met == at, chip * CORES + core, device)
    return device


def message_kernel(
    near_ref,
    far_ref,
    coords_ref,
    charges_ref,
    points_ref,
    leaf_ref,
    node_ref,
    upper_ref,
    message_ref,
    local_ref,
    table_ref,
):
    dim, local = coords_ref.shape
    half = local // LEAVES
    charges = [charges_ref[:, 0:half], charges_ref[:, half:]]
    sent = [
        jnp.concatenate(charges, axis=0).T,
        skeleton_rows(charges, leaf_ref, node_ref, upper_ref),
        points_ref[...],
    ]
    place = 0
    for part in sent:
        rows = slice(place, place + part.shape[0])
        message_ref[rows, :] = part
        local_ref[rows, :] = part
        place += part.shape[0]
    for block in range(local // LANES):
        local_ref[place : place + dim, :] = coords_ref[:, block * LANES : (block + 1) * LANES]
        place += dim
    table = count_rows(near_ref, far_ref)
    table_ref[...] = table
    local_ref[place : place + 16, :] = jnp.concatenate([table, table], axis=0).astype(bf16)


def joined_kernel(mine_ref, other_ref, leaf_ref, node_ref, upper_ref, out_ref, *message_refs):
    half = mine_ref.shape[0]
    columns = LANES // LEAVES
    result = mine_ref[...] + other_ref[...]
    flat = result.T.astype(bf16)
    charges = [flat[0:columns], flat[columns:]]
    out_ref[...] = jnp.concatenate(charges, axis=1)
    rows = skeleton_rows(charges, leaf_ref, node_ref, upper_ref)
    for message_ref in message_refs:
        message_ref[0:half, :] = result.astype(bf16)
        message_ref[half : half + LANES, :] = rows


def added_kernel(mine_ref, other_ref, out_ref):
    columns = LANES // LEAVES
    flat = (mine_ref[...] + other_ref[...]).T.astype(bf16)
    out_ref[...] = jnp.concatenate([flat[0:columns], flat[columns:]], axis=1)


def stage_kernel(stage, *refs):
    ring, near_spots, far_spots, n_sub, dim, points, begins, first, last, mode, near_given = stage
    refs = list(refs)
    use, keep = mode == "use", mode == "keep"
    spots = sorted(set(near_spots) | set(far_spots))
    makes = not use
    makes_near = makes and not near_given
    table_refs = [refs.pop(0) for _ in range(1 if begins else CORES)]
    if begins:
        local_ref = refs.pop(0)
        charge_refs = skeleton_refs = {spots[0]: local_ref}
    else:
        place_refs = {spot: refs.pop(0) for spot in near_spots} if makes_near else {}
        skeleton_refs = {spot: refs.pop(0) for spot in far_spots} if makes else {}
        charge_refs = {spot: refs.pop(0) for spot in spots}
    kept_refs = {}
    far_kept_ref = None
    if not makes_near:
        kept_refs = {spot: refs.pop(0) for spot in near_spots}
    if use:
        far_kept_ref = refs.pop(0) if far_spots else None
    if begins:
        sibling_ref = refs.pop(0)
    elif makes:
        targets_ref = refs.pop(0)
    if not first:
        refs.pop(0), refs.pop(0)
    upper_points_ref = refs.pop(0) if last and makes else None
    if begins:
        targets_ref, table_ref = refs.pop(0), refs.pop(0)
    if keep:
        if makes_near:
            kept_refs = {spot: refs.pop(0) for spot in near_spots}
        far_kept_ref = refs.pop(0) if far_spots else None
    if last:
        half_refs = refs.pop(0), refs.pop(0)
    total_ref, sums_ref, far_charges_ref, charges_ref = refs[:4]
    near_ref = refs[4] if makes_near else None
    far_ref = refs[-1] if makes else None

    skeletons_at = points + LANES
    blocks = points // LANES
    low_half = in_low_half((LANES, LANES))
    lane = lax.broadcasted_iota(i32, (8, LANES), 1)

    def span_of(leaf):
        return slice(leaf * points, (leaf + 1) * points)

    def points_of(spot, leaf):
        if not begins:
            return place_refs[spot][:, span_of(leaf)]
        begin = skeletons_at + dim + leaf * blocks * dim
        rows = [begin + block * dim for block in range(blocks)]
        return jnp.concatenate([local_ref[row : row + dim, :] for row in rows], axis=1)

    if begins:
        begin = skeletons_at + dim + LEAVES * blocks * dim
        table_ref[...] = local_ref[begin : begin + 16, :].astype(f32)[0:8]
        table_refs = [table_ref] + table_refs
        for leaf in range(LEAVES):
            targets_ref[0, span_of(leaf), :] = target_rows(points_of(0, leaf))
            targets_ref[1, span_of(leaf), :] = target_rows(sibling_ref[:, span_of(leaf)])
    if first:
        total_ref[...] = jnp.zeros_like(total_ref)
        sums_ref[...] = jnp.zeros_like(sums_ref)

    def table_of(core):
        return table_refs[core][...]

    def picked(table, entry):
        return jnp.sum(jnp.where(lane == entry, table, 0.0), axis=1, keepdims=True)

    def values(core, sources_ref, kept_ref):
        if sources_ref is None:
            return kept_ref[...]
        made = kernel_values(targets_ref[core], sources_ref[...])
        if kept_ref is not None:
            kept_ref[...] = made
        return made

    devices = {spot: device_of(ring, spot) for spot in spots}

    def near_part(turn, spot, core, leaf):
        at = core * len(near_spots) + near_spots.index(spot)
        table = table_of(core)
        named = [
            picked(table, devices[spot] * LEAVES + which)[0:LEAVES] for which in range(LEAVES)
        ]
        if leaf is None:
            second = jnp.where(jnp.sum(named[1], axis=0, keepdims=True) > 0.0, 1.0, 0.0)
        else:
            second = jnp.full((1, 1), float(leaf), f32)
        times = named[0] * (1.0 - second) + named[1] * second
        if makes_near:
            low, high = (points_of(spot, which) for which in range(LEAVES))
            chosen = low * (1.0 - second).astype(bf16) + high * second.astype(bf16)
            put_sources(near_ref.at[at], chosen)
        half = jnp.where(lane[0:1] < LANES // LEAVES, 1.0 - second, second).astype(bf16)
        charges_ref[at] = charge_refs[spot][0:points, :] * half
        kept = kept_refs[spot].at[turn] if kept_refs else None
        added = matmul(values(core, near_ref.at[at] if makes_near else None, kept), charges_ref[at])
        return [times[own : own + 1] * added[span_of(own)] for own in range(LEAVES)]

    weights = []
    skeletons = []
    for spot in far_spots:
        rows = charge_refs[spot][points : points + LANES, :].astype(f32)
        weights.append((jnp.where(low_half, rows, swapped(rows)), devices[spot]))
        sums_ref[devices[spot] // BRANCH] += rows
        if makes:
            skeletons.append(skeleton_refs[spot][skeletons_at : skeletons_at + dim, :])
    if last:
        for sub in range(n_sub):
            rows = sums_ref[sub]
            weights.append((jnp.where(low_half, swapped(rows), rows), len(ring) * CORES + sub))
            if makes:
                skeletons.append(upper_points_ref[:, sub * LANES : (sub + 1) * LANES])
    if far_spots and makes:
        put_sources(far_ref, jnp.concatenate(skeletons, axis=1))

    def far_part(core):
        table = table_of(core)
        kernel = values(
            core,
            far_ref if makes else None,
            None if far_kept_ref is None else far_kept_ref.at[core],
        )
        added = []
        for own in range(LEAVES):
            for position, (block, node) in enumerate(weights):
                scaled = block * picked(table, node)[LEAVES + own : LEAVES + own + 1]
                high = scaled.astype(bf16).astype(f32)
                rows = slice(position * LANES, (position + 1) * LANES)
                far_charges_ref[core * LEAVES + own, rows, :] = jnp.where(low_half, high, scaled - high).astype(bf16)
            added.append(matmul(kernel[span_of(own)], far_charges_ref[core * LEAVES + own]))
        return added

    def add(core, parts):
        for own in range(LEAVES):
            total = total_ref[core, span_of(own), :]
            for part in parts:
                total = total + part[own]
            total_ref[core, span_of(own), :] = total

    if first:
        for leaf in range(LEAVES):
            add(0, [near_part(leaf, 0, 0, leaf)])
        add(1, [near_part(LEAVES, 0, 1, None), far_part(1)])
    else:

        for core in range(CORES):
            parts = [near_part(core, spot, core, None) for spot in near_spots]
            add(core, parts + ([far_part(core)] if far_spots else []))

    if last:
        for core, ref in enumerate(half_refs):
            both = [total_ref[core, span_of(leaf), :] for leaf in range(LEAVES)]
            both = [total + swapped(total) for total in both]
            ref[...] = jnp.where(in_low_half(both[0].shape), both[0], both[1])


def near_values_kernel(ring, spot, points, mine_ref, other_ref, place_ref, targets_ref, kept_ref, near_ref):
    lane = lax.broadcasted_iota(i32, (LEAVES, LANES), 1)
    entry = device_of(ring, spot) * LEAVES + 1
    for core, table_ref in enumerate((mine_ref, other_ref)):
        named = jnp.where(lane == entry, table_ref[0:LEAVES, :], 0.0)
        named = jnp.sum(jnp.sum(named, axis=1, keepdims=True), axis=0, keepdims=True)
        second = jnp.where(named > 0.0, 1.0, 0.0)
        low, high = place_ref[:, 0:points], place_ref[:, points:]
        chosen = low * (1.0 - second).astype(bf16) + high * second.astype(bf16)
        put_sources(near_ref.at[core], chosen)
        kept_ref[core] = kernel_values(targets_ref[core], near_ref[core])


def gate_kernel(message_ref, after_ref, out_ref):
    pass


def gated(message, after):
    anywhere = pl.BlockSpec(memory_space=pl.ANY)
    return pl.pallas_call(
        gate_kernel,
        out_shape=jax.ShapeDtypeStruct(message.shape, message.dtype),
        in_specs=[anywhere] * 2,
        out_specs=anywhere,
        input_output_aliases={0: 0},
        compiler_params=pltpu.CompilerParams(vmem_limit_bytes=2**20),
    )(message, after)


def call(body, args, out_shapes, streamed=(), scratch=(), aliases={}, flops=0, vmem_mib=16):
    vmem = pl.BlockSpec(memory_space=pltpu.VMEM)
    specs = []
    for place, arg in enumerate(args):
        if arg.dtype == i32:
            specs.append(pl.BlockSpec(memory_space=pltpu.SMEM))
        elif place in streamed:
            specs.append(pl.BlockSpec(arg.shape, lambda i: (0,) * 2))
        else:
            specs.append(vmem)
    moved = sum(arg.size * arg.dtype.itemsize for arg in args)
    return pl.pallas_call(
        body,
        grid=(1,),
        out_shape=out_shapes,
        in_specs=specs,
        out_specs=[vmem for _ in out_shapes],
        scratch_shapes=list(scratch),
        input_output_aliases=aliases,
        compiler_params=pltpu.CompilerParams(vmem_limit_bytes=vmem_mib * 1024 * 1024),
        cost_estimate=pl.CostEstimate(flops=flops, bytes_accessed=moved, transcendentals=0),
    )(*args)


def ring_order(chips):
    if chips == 8:
        return [0, 2, 4, 6, 7, 5, 3, 1]
    return list(range(chips))


def on_device(
    coords,
    charges,
    near_lists,
    far_lists,
    leaf_interp,
    node_interp,
    upper_interp,
    node_points,
    upper_points,
):
    dim, local = coords.shape
    columns = charges.shape[0]
    points = local // LEAVES
    peers = lax.axis_size("leaf")
    n_sub = peers // BRANCH
    ring = ring_order(peers // CORES)
    chips = len(ring)

    def along(step):
        return [
            (ring[place] * CORES + core, ring[(place + step * (1 - 2 * core)) % chips] * CORES + core)
            for place in range(chips)
            for core in range(CORES)
        ]

    one_way = functools.partial(lax.ppermute, axis_name="leaf", perm=along(1))
    other_way = functools.partial(lax.ppermute, axis_name="leaf", perm=along(-1))
    to_sibling = functools.partial(
        lax.ppermute, axis_name="leaf", perm=[(device, device ^ 1) for device in range(peers)]
    )

    def shape(*extent, dtype=bf16):
        return jax.ShapeDtypeStruct(extent, dtype)

    maps = [leaf_interp, node_interp, upper_interp]
    sibling_coords = to_sibling(coords)
    coords_next = one_way(coords), other_way(coords)
    message, own, table = call(
        message_kernel,
        [near_lists, far_lists, coords, charges, node_points] + maps,
        [
            shape(points + LANES + dim, LANES),
            shape(points + LANES + dim + LEAVES * points // LANES * dim + 16, LANES),
            shape(8, LANES, dtype=f32),
        ],
        streamed=range(2, 8),
        vmem_mib=60,
        flops=25 * 10**8,
    )
    sibling_table = to_sibling(table)

    total_shape = shape(CORES, local, LANES, dtype=f32)
    sums_shape = shape(n_sub, LANES, LANES, dtype=f32)
    half_shape = shape(points, LANES, dtype=f32)
    targets_shape = shape(CORES, local, LANES)

    steps = LEAVES + 1 + CORES * (chips - 1)
    kept_bytes = 2 * points * (steps * local + CORES * LEAVES * (chips + n_sub) * LANES)
    keeping = kept_bytes <= KEPT_MIB * 2**20

    def stage(near_spots, far_spots, given, carried, last, mode, begins=False, near_given=False):
        first = not carried
        makes = mode != "use"
        spots = sorted(set(near_spots) | set(far_spots))
        if begins:
            args = [sibling_table, own, sibling_coords]
        else:
            args = list(given["tables"])
            if makes:
                if not near_given:
                    args += [given["places"][spot] for spot in near_spots]
                args += [given["skeletons"][spot] for spot in far_spots]
            args += [given["charges"][spot] for spot in spots]
            if near_given or not makes:
                args += [given["near"][spot] for spot in near_spots]
            if makes:
                args += [given["targets"]]
            else:
                args += [given["far"][far_spots]] if far_spots else []
        carried_at = len(args)
        args += carried
        args += [upper_points] if last and makes else []
        far_width = max(LANES, LANES * (len(far_spots) + (n_sub if last else 0)))
        scratch = [
            pltpu.VMEM((CORES * LEAVES, far_width, LANES), bf16),
            pltpu.VMEM((CORES * len(near_spots), points, LANES), bf16),
        ]
        if makes and not near_given:
            scratch += [pltpu.VMEM((CORES * len(near_spots), LANES, points), bf16)]
        if makes:
            scratch += [pltpu.VMEM((LANES, far_width), bf16)]
        names, outs = [], []
        if begins:
            names += ["targets", "table"]
            outs += [targets_shape, shape(8, LANES, dtype=f32)]
        if mode == "keep":
            if not near_given:
                names += [("near", spot) for spot in near_spots]
                outs += [shape(LEAVES + 1 if first else CORES, local, points) for _ in near_spots]
            names += [("far", far_spots)] if far_spots else []
            outs += [shape(CORES, local, far_width)] if far_spots else []
        if last:
            names += ["mine", "other"]
            outs += [half_shape, half_shape]
        aliases = {carried_at + k: len(outs) + k for k in range(len(carried))}
        names += ["total", "sums"]
        outs += [total_shape, sums_shape]
        static = (
            ring, near_spots, far_spots, n_sub, dim, points, begins, first, last, mode, near_given
        )
        results = call(
            functools.partial(stage_kernel, static),
            args,
            outs,
            scratch=scratch,
            aliases=aliases,
            flops=len(near_spots) * (2 if makes else 1) * 10**9,
        )
        return dict(zip(names, results))

    def far_spots_of(spot):
        return (spot - 1, spot) if spot % 2 == 0 and spot > 0 else (spot,)

    mode = "keep" if keeping else "make"
    given = {"near": {}, "far": {}, "places": {0: coords}, "skeletons": {0: message}}
    given["charges"] = given["skeletons"]

    def keep_results(results):
        for name, value in results.items():
            if isinstance(name, tuple):
                given[name[0]][name[1]] = value
        return [results["total"], results["sums"]]

    sent = one_way(message), other_way(message)
    results = stage((0,), (0,), given, [], False, mode, begins=True)
    given["targets"], given["tables"] = results["targets"], [results["table"], sibling_table]
    carried = keep_results(results)
    for hop in range(1, chips // 2):
        final = hop == chips // 2 - 1
        spots = (2 * hop - 1, 2 * hop)
        for at, spot in enumerate(spots):
            given["places"][spot] = coords_next[at]
            given["skeletons"][spot] = sent[at]
        coords_next = one_way(coords_next[0]), None if final else other_way(coords_next[1])
        sent = one_way(sent[0]), None if final else other_way(sent[1])
        carried = keep_results(stage(spots, spots, given, carried, False, mode))
    across = (chips - 1,)
    given["places"][across[0]], given["skeletons"][across[0]] = coords_next[0], sent[0]
    if keeping:
        (given["near"][across[0]],) = call(
            functools.partial(near_values_kernel, ring, across[0], points),
            given["tables"] + [gated(coords_next[0], carried[1]), given["targets"]],
            [shape(CORES, local, points)],
            scratch=[pltpu.VMEM((CORES, LANES, points), bf16)],
            flops=10**9,
        )
    results = stage(across, across, given, carried, True, mode, near_given=keeping)
    keep_results(results)
    first, message, again = call(
        joined_kernel,
        [results["mine"], to_sibling(results["other"])] + maps,
        [shape(columns, local)] + [shape(points + LANES, LANES)] * 2,
    )

    mode = "use" if keeping else "make"
    given["charges"] = {}
    carried = []

    def arrived(spot, message):
        nonlocal carried
        given["charges"][spot] = message
        last = spot == chips - 1
        far_spots = () if spot % 2 == 1 and not last else far_spots_of(spot)
        results = stage((spot,), far_spots, given, carried, last, mode)
        carried = [results["total"], results["sums"]]
        return results

    one = one_way(message)
    arrived(0, message)
    other = other_way(gated(again, carried[1]))
    for hop in range(1, chips // 2):
        one_next = one_way(one)
        arrived(2 * hop - 1, one)
        other_next = None
        if hop < chips // 2 - 1:
            other = gated(other, carried[1])
            other_next = other_way(other)
        arrived(2 * hop, other)
        one, other = one_next, other_next
    results = arrived(chips - 1, one)
    (second,) = call(
        added_kernel, [results["mine"], to_sibling(results["other"])], [shape(columns, local)]
    )
    return (first, second)


def solution(mesh):
    placed = (
        P(None, ("groups", "leaf")),
        P(None, ("groups", "leaf")),
        P(("groups", "leaf"), None),
        P(("groups", "leaf"), None),
        P(("groups", "leaf"), None),
        P(("groups", "leaf"), None),
        P(("groups", "leaf"), None),
        P(None, ("groups", "leaf")),
        P(None, "groups"),
    )
    return jax.shard_map(
        on_device,
        mesh=mesh,
        in_specs=placed,
        out_specs=(P(None, ("groups", "leaf")), P(None, ("groups", "leaf"))),
        check_vma=False,
    )
```
